128 devices in a mesh: fsdp: 4 (over z), ctx: 32 (over x, y, core).
Axes of the slice: x: 4, y: 4, z: 4, core: 2. Of those that a mesh axis runs over, the one named last changes fastest.
Arguments:
- query_vectors: bfloat16 [4, 4096, 1024], P('fsdp', 'ctx'), may hold values from -6 to 6
- key_vectors: bfloat16 [4, 4096, 1024], P('fsdp', 'ctx'), may hold values from -6 to 6
- value_vectors: bfloat16 [4, 4096, 2048], P('fsdp', 'ctx'), may hold values from -24 to 24
- output_gate: bfloat16 [4, 4096, 2048], P('fsdp', 'ctx'), may hold values from -6 to 6
- log_decay: float32 [4, 4096, 16], P('fsdp', 'ctx'), may hold values from -1 to 0
- write_rate: float32 [4, 4096, 16], P('fsdp', 'ctx'), may hold values from 0 to 1
- out_weight: bfloat16 [2048, 2048], P('fsdp'), may hold values from -0.125 to 0.125
- cotangent: bfloat16 [4, 4096, 2048], P('fsdp', 'ctx'), may hold values from -6 to 6
- lengths: int32 [4], replicated, may hold values from 2048 to 4096, as said below
- pairing: int32 [4], replicated, may hold values from 0 to 3, each once
- log_ratio: float32 [4], replicated, may hold values from -1 to 1
Outputs:
- mixed_out: bfloat16 [4, 4096, 2048], P('fsdp', 'ctx')
- query_grad: bfloat16 [4, 4096, 1024], P('fsdp', 'ctx')
- key_grad: bfloat16 [4, 4096, 1024], P('fsdp', 'ctx')
- value_grad: bfloat16 [4, 4096, 2048], P('fsdp', 'ctx')
- gate_grad: bfloat16 [4, 4096, 2048], P('fsdp', 'ctx')
- weight_grad: float32 [2048, 2048], P(('fsdp', 'ctx'))
The draws below stay inside these ranges and needn't reach their ends.
Inputs may be any that keep to these rules, and one draw needn't show every extreme that they name: `lengths`: some sequence has exactly 4096 live tokens.
All inputs are finite; a program needn't handle non-finite values.
Results may differ from the reference program's by a relative error of at most 0.019.
Values may be sent and summed in bfloat16 or wider, within the bound.
No kernel may reach another device: no remote copies, remote signals or barrier semaphores. Data moves between devices by JAX's collectives and lax.ppermute only.
A program may use at most 448 MiB of HBM per device.

```python
import math
from functools import partial
import jax
import jax.numpy as jnp
from jax import lax

D = 2048
VALUE_HEADS = 16
HK = 8
DK = 128
DV = 128
BLOCK = 64
TOK_DEV = 128
SEQUENCE_LENGTH = 4096
SEQUENCE_TOTAL = 4
QKDIM = 1024
VDIM = 2048


def slow_heads(base_key, slow_share):
    return jax.random.uniform(base_key, (SEQUENCE_TOTAL, 1, VALUE_HEADS)) < slow_share


def draw_log_decay(key, part):
    slow_share = 0.5
    slow = slow_heads(key, slow_share)
    key = jax.random.fold_in(key, 11)
    random_subkeys = jax.random.split(key, 6)
    fast_rate = jnp.exp(jax.random.uniform(random_subkeys[0], (SEQUENCE_TOTAL, 1, VALUE_HEADS), minval=math.log(1.0 / 50.0), maxval=math.log(1.0 / 30.0)))
    slow_rate = jnp.exp(jax.random.uniform(random_subkeys[1], (SEQUENCE_TOTAL, 1, VALUE_HEADS), minval=math.log(0.1), maxval=math.log(0.5))) / SEQUENCE_LENGTH
    base_rate = jnp.where(slow, slow_rate, fast_rate)
    block_count = SEQUENCE_LENGTH // TOK_DEV
    modulation = jnp.exp(jax.random.uniform(random_subkeys[2], (SEQUENCE_TOTAL, block_count, 1, VALUE_HEADS), minval=math.log(0.5), maxval=math.log(2.0)))
    roughness = jax.random.uniform(random_subkeys[3], (SEQUENCE_TOTAL, block_count, TOK_DEV, VALUE_HEADS), minval=0.5, maxval=1.5)
    constant_level = -(base_rate[:, None] * modulation * roughness).reshape(SEQUENCE_TOTAL, SEQUENCE_LENGTH, VALUE_HEADS)
    spike_position = jax.random.randint(random_subkeys[4], (SEQUENCE_TOTAL, 2, 1, VALUE_HEADS), 0, SEQUENCE_LENGTH)
    spike_length = jnp.log(jax.random.uniform(random_subkeys[5], (SEQUENCE_TOTAL, 2, 1, VALUE_HEADS), minval=0.6, maxval=0.8))
    token_positions = jnp.arange(SEQUENCE_LENGTH).reshape(1, 1, SEQUENCE_LENGTH, 1)
    spike_groups = jnp.sum(jnp.where(token_positions == spike_position, spike_length, 0.0), axis=1)
    return (constant_level + spike_groups).astype(jnp.float32)


def draw_write_rate(key, part):
    slow_share = 0.5
    slow = slow_heads(key, slow_share)
    key = jax.random.fold_in(key, 12)
    random_subkeys = jax.random.split(key, 3)
    level = jnp.exp(jax.random.uniform(random_subkeys[0], (SEQUENCE_TOTAL, 1, VALUE_HEADS), minval=math.log(0.1), maxval=math.log(0.5))) * DK / SEQUENCE_LENGTH
    slow_rate = level * jax.random.uniform(random_subkeys[1], (SEQUENCE_TOTAL, SEQUENCE_LENGTH, VALUE_HEADS), minval=0.5, maxval=1.5)
    fast_rate = jax.random.uniform(random_subkeys[2], (SEQUENCE_TOTAL, SEQUENCE_LENGTH, VALUE_HEADS), minval=0.05, maxval=0.95)
    return jnp.where(slow, slow_rate, fast_rate).astype(jnp.float32)


def draw_lengths(key, part):
    key = jax.random.fold_in(key, 13)
    first_key, second_key = jax.random.split(key)
    drawn = jax.random.randint(first_key, (SEQUENCE_TOTAL,), SEQUENCE_LENGTH // 2, SEQUENCE_LENGTH + 1)
    longest = jax.random.randint(second_key, (1,), 0, SEQUENCE_TOTAL)
    return jnp.where(jnp.arange(SEQUENCE_TOTAL) == longest, SEQUENCE_LENGTH, drawn).astype(jnp.int32)


def block_levels(key, dims, cuts, smallest, high):
    loudness, own = 1.0, jax.random.fold_in(key, 6)
    for position, shards_of in cuts:
        heights = jnp.exp(jax.random.uniform(jax.random.fold_in(own, position), (shards_of,), jnp.float32, smallest / len(cuts), high / len(cuts)))
        loudness = loudness * jnp.repeat(heights, dims[position] // shards_of).reshape([-1 if axis == position else 1 for axis in range(len(dims))])
    return loudness


def bell_draw(key, extent, width, most, cuts=(), kind=jnp.bfloat16):
    values = jax.random.normal(key, extent, jnp.float32) * width
    if len(cuts) > 0:
        values = block_levels(key, extent, cuts, -0.22, 0.18) * values
    return jnp.clip(values, min=-most, max=most).astype(kind)


def setup_inputs(seed: int = 0) -> dict:
    key_list = jax.random.split(jax.random.key(seed), 12)
    return {
        "query_vectors": bell_draw(key_list[0], (SEQUENCE_TOTAL, SEQUENCE_LENGTH, QKDIM), 1.0, 6.0, ((0, 4), (1, 32))),
        "key_vectors": bell_draw(key_list[1], (SEQUENCE_TOTAL, SEQUENCE_LENGTH, QKDIM), 1.0, 6.0, ((0, 4), (1, 32))),
        "value_vectors": bell_draw(key_list[2], (SEQUENCE_TOTAL, SEQUENCE_LENGTH, VDIM), 4.0, 24.0, ((0, 4), (1, 32))),
        "output_gate": bell_draw(key_list[3], (SEQUENCE_TOTAL, SEQUENCE_LENGTH, VDIM), 1.0, 6.0, ((0, 4), (1, 32))),
        "log_decay": draw_log_decay(jax.random.fold_in(key_list[11], 71), 0),
        "write_rate": draw_write_rate(jax.random.fold_in(key_list[11], 71), 0),
        "out_weight": bell_draw(key_list[6], (VDIM, D), VDIM ** -0.5, 0.125, ((0, 4),)),
        "cotangent": bell_draw(key_list[7], (SEQUENCE_TOTAL, SEQUENCE_LENGTH, D), 1.0, 6.0, ((0, 4), (1, 32))),
        "lengths": draw_lengths(jax.random.fold_in(key_list[11], 71), 0),
        "pairing": jax.random.permutation(key_list[9], SEQUENCE_TOTAL).astype(jnp.int32),
        "log_ratio": jnp.clip(jax.random.uniform(key_list[10], (SEQUENCE_TOTAL,), jnp.float32, -1.0, 1.0), -1.0, 1.0),
    }


PRECISE = lax.Precision.HIGHEST
BLOCKWISE = lax.Precision.HIGH
CHI_BETA = 0.5
NORM_EPS = 1e-06

def unit_rows(matrix):
    return matrix * lax.rsqrt(lax.optimization_barrier(jnp.sum(matrix * matrix, axis=-1, keepdims=True)) + NORM_EPS)

def head_major(matrix, head_count):
    return jnp.swapaxes(matrix.reshape(matrix.shape[0], head_count, -1), 0, 1)

def prepare(query_vectors, key_vectors, value_vectors):
    group_size = VALUE_HEADS // HK
    queries = unit_rows(head_major(query_vectors, HK)) * DK ** (-0.5)
    unit_keys = unit_rows(head_major(key_vectors, HK))
    return (jnp.repeat(queries, group_size, axis=0), jnp.repeat(unit_keys, group_size, axis=0), head_major(value_vectors, VALUE_HEADS))

def block_parts(queries, unit_keys, values, decays, write_rates):
    block_len = queries.shape[-2]
    cumulative = jnp.cumsum(decays, axis=-1)
    row_index = lax.broadcasted_iota(jnp.int32, (block_len, block_len), 0)
    col_index = lax.broadcasted_iota(jnp.int32, (block_len, block_len), 1)
    causal = row_index >= col_index
    strict = row_index > col_index
    spread = cumulative[..., :, None] - cumulative[..., None, :]
    within = jnp.where(causal, jnp.exp(jnp.where(causal, spread, 0.0)), 0.0)
    intersection = jnp.einsum('bhtd,bhjd->bhtj', unit_keys, unit_keys, precision=BLOCKWISE)
    coupling = jnp.where(strict, intersection * within, 0.0) * write_rates[..., :, None]
    identity_c = jnp.eye(block_len, dtype=decays.dtype)
    negated = -coupling
    inverse = identity_c + negated
    powered = negated
    for repeat in range(block_len.bit_length() - 2):
        powered = jnp.einsum('bhij,bhjk->bhik', powered, powered, precision=PRECISE)
        inverse = jnp.einsum('bhij,bhjk->bhik', inverse, identity_c + powered, precision=PRECISE)
    growth = jnp.exp(cumulative)
    new_values = jnp.einsum('bhtj,bhjv->bhtv', inverse, write_rates[..., None] * values, precision=BLOCKWISE)
    new_keys = jnp.einsum('bhtj,bhjk->bhtk', inverse, (write_rates * growth)[..., None] * unit_keys, precision=BLOCKWISE)
    scores = jnp.einsum('bhtd,bhjd->bhtj', queries, unit_keys, precision=BLOCKWISE) * within
    inner_out = jnp.einsum('bhtj,bhjv->bhtv', scores, new_values, precision=BLOCKWISE)
    reach_rows = growth[..., None] * queries - jnp.einsum('bhtj,bhjk->bhtk', scores, new_keys, precision=BLOCKWISE)
    block_total = cumulative[..., -1:]
    carried = jnp.exp(block_total - cumulative)[..., None] * unit_keys
    identity_k = jnp.eye(unit_keys.shape[-1], dtype=decays.dtype)
    transit = jnp.exp(block_total)[..., None] * identity_k - jnp.einsum('bhcx,bhcy->bhxy', new_keys, carried, precision=BLOCKWISE)
    written = jnp.einsum('bhcv,bhck->bhvk', new_values, carried, precision=BLOCKWISE)
    return (inner_out, reach_rows, transit, written)

def norm_gate(outputs, gates):
    shaped = outputs.reshape(outputs.shape[:-1] + (VALUE_HEADS, DV))
    scaled = shaped * lax.rsqrt(lax.optimization_barrier(jnp.mean(shaped * shaped, axis=-1, keepdims=True)) + NORM_EPS)
    return scaled.reshape(outputs.shape) * jax.nn.silu(gates)

def pair_weights(log_ratio, pairing):
    seq_count = log_ratio.shape[0]
    couples = pairing.reshape(seq_count // 2, 2)
    seq_index = lax.broadcasted_iota(jnp.int32, (seq_count // 2, seq_count), 1)
    chosen = (couples[:, :1] == seq_index).astype(log_ratio.dtype)
    rejected = (couples[:, 1:] == seq_index).astype(log_ratio.dtype)
    ratio_c = lax.optimization_barrier(jnp.sum(chosen * log_ratio[None, :], axis=1))
    ratio_r = lax.optimization_barrier(jnp.sum(rejected * log_ratio[None, :], axis=1))
    margin = CHI_BETA * (jnp.exp(ratio_c) + ratio_c - jnp.exp(ratio_r) - ratio_r)
    pull_scale = CHI_BETA * jax.nn.sigmoid(-margin)
    weight_c = -pull_scale * (jnp.exp(ratio_c) + 1.0)
    weight_r = pull_scale * (jnp.exp(ratio_r) + 1.0)
    return lax.optimization_barrier(jnp.sum(chosen * weight_c[:, None] + rejected * weight_r[:, None], axis=0))

def layer_core(log_decay, write_rate, query_vectors, key_vectors, value_vectors, output_gate):
    queries, unit_keys, values = jax.vmap(prepare)(query_vectors, key_vectors, value_vectors)
    block_count = SEQUENCE_LENGTH // BLOCK

    def to_blocks(tensor):
        shaped = tensor.reshape(tensor.shape[:2] + (block_count, BLOCK) + tensor.shape[3:])
        return jnp.moveaxis(shaped, 2, 0)
    pieces = (to_blocks(queries), to_blocks(unit_keys), to_blocks(values), to_blocks(jnp.swapaxes(log_decay, 1, 2)), to_blocks(jnp.swapaxes(write_rate, 1, 2)))

    def advance(state_now, block_in):
        inner_out, reach_rows, transit, written = block_parts(*block_in)
        produced = inner_out + jnp.einsum('bhck,bhvk->bhcv', reach_rows, state_now, precision=BLOCKWISE)
        state_next = jnp.einsum('bhvx,bhxy->bhvy', state_now, transit, precision=PRECISE) + written
        return (state_next, produced)
    initial = jnp.zeros((SEQUENCE_TOTAL, VALUE_HEADS, DV, DK), jnp.float32)
    final_state, produced = lax.scan(jax.checkpoint(advance), initial, pieces)
    core = jnp.moveaxis(produced, 0, 2).reshape(SEQUENCE_TOTAL, VALUE_HEADS, SEQUENCE_LENGTH, DV)
    core = jnp.swapaxes(core, 1, 2).reshape(SEQUENCE_TOTAL, SEQUENCE_LENGTH, VALUE_HEADS * DV)
    return norm_gate(core, output_gate)

def reference(query_vectors, key_vectors, value_vectors, output_gate, log_decay, write_rate, out_weight, cotangent, lengths, pairing, log_ratio):
    floats = tuple((tensor.astype(jnp.float32) for tensor in (query_vectors, key_vectors, value_vectors, output_gate)))
    gated_out, pullback = jax.vjp(partial(layer_core, log_decay, write_rate), *floats)
    normed = gated_out.astype(jnp.bfloat16)
    flat_normed = normed.reshape(SEQUENCE_TOTAL * SEQUENCE_LENGTH, VALUE_HEADS * DV)
    mixed_out = jnp.dot(flat_normed, out_weight, preferred_element_type=jnp.float32).astype(jnp.bfloat16)
    weights = pair_weights(log_ratio, pairing)
    token_positions = lax.broadcasted_iota(jnp.int32, (SEQUENCE_TOTAL, SEQUENCE_LENGTH), 1)
    live_mask = (token_positions < lengths[:, None]).astype(jnp.float32)
    scaled = (cotangent.astype(jnp.float32) * (weights[:, None] * live_mask)[..., None]).astype(jnp.bfloat16)
    flat_scaled = scaled.reshape(SEQUENCE_TOTAL * SEQUENCE_LENGTH, D)
    back_grad = jnp.dot(flat_scaled, out_weight.T, preferred_element_type=jnp.float32).astype(jnp.bfloat16)
    back_grad = lax.optimization_barrier(back_grad).astype(jnp.float32)
    input_grads = pullback(back_grad.reshape(SEQUENCE_TOTAL, SEQUENCE_LENGTH, VALUE_HEADS * DV))
    weight_grad = jnp.dot(flat_normed.T, flat_scaled, preferred_element_type=jnp.float32)
    return (mixed_out.reshape(SEQUENCE_TOTAL, SEQUENCE_LENGTH, D), input_grads[0].astype(jnp.bfloat16), input_grads[1].astype(jnp.bfloat16), input_grads[2].astype(jnp.bfloat16), input_grads[3].astype(jnp.bfloat16), weight_grad)
```

```python
import functools

import jax
import jax.numpy as jnp
from jax import lax
from jax.experimental import pallas as pl
from jax.experimental.pallas import tpu as pltpu
from jax.sharding import PartitionSpec as P

VALUE_HEADS = 16
HK = 8
DK = 128
DV = 128
T = 128
HALF = 64
TAIL = 16
CHI_BETA = 0.5
NORM_EPS = 1e-06
F32 = jnp.float32
BF16 = jnp.bfloat16

NN = (((1,), (0,)), ((), ()))
NT = (((1,), (1,)), ((), ()))
TN = (((0,), (0,)), ((), ()))


def dot1(a, b, dims=NN):
    return lax.dot_general(a.astype(BF16), b.astype(BF16), dims, preferred_element_type=F32)


def split(a):
    high = a.astype(BF16)
    return high, (a - high.astype(F32)).astype(BF16)


def dot3(a, b, dims=NN):
    a_high, a_low = split(a)
    b_high, b_low = split(b)
    return dot1(a_high, b_high, dims) + (dot1(a_low, b_high, dims) + dot1(a_high, b_low, dims))


def grid_index():
    row = lax.broadcasted_iota(jnp.int32, (T, T), 0)
    col = lax.broadcasted_iota(jnp.int32, (T, T), 1)
    return row, col


def unit(x):
    return lax.rsqrt(jnp.sum(x * x, axis=-1, keepdims=True) + NORM_EPS)


def cumulative_decay(decay, row, col):
    lower = (row >= col).astype(BF16)
    first, rest = decay.astype(BF16), decay
    rest = rest - first.astype(F32)
    second = rest.astype(BF16)
    third = (rest - second.astype(F32)).astype(BF16)
    return dot1(lower, first) + (dot1(lower, second) + dot1(lower, third))


def column(table, head):
    lane = lax.broadcasted_iota(jnp.int32, table.shape, 1)
    return jnp.sum(jnp.where(lane == head, table, 0.0), axis=1, keepdims=True)


def as_row(table_t, head):
    sub = lax.broadcasted_iota(jnp.int32, table_t.shape, 0)
    return jnp.sum(jnp.where(sub == head, table_t, 0.0), axis=0, keepdims=True)


def decay_within(cum_col, cum_row, causal):
    return jnp.where(causal, jnp.exp(jnp.where(causal, cum_col - cum_row, 0.0)), 0.0)


def invert(coupling, row, col):
    eye = (row == col).astype(F32)
    inverse = eye - jnp.where((row >> 1) == (col >> 1), coupling, 0.0)
    for level in range(1, 7):
        mask = ((row >> (level + 1)) == (col >> (level + 1))) & ((row >> level) != (col >> level))
        off = jnp.where(mask, coupling, 0.0)
        inverse = inverse - dot1(inverse, dot1(off, inverse))
    residual = eye - inverse - dot3(coupling, inverse)
    return inverse + dot1(inverse, residual)


def forward_kernel(heads, q_ref, k_ref, v_ref, ld_ref, be_ref,
                   ab_ref, t_ref, p_ref, u0_ref, kg_ref, r_ref, io_ref):
    group = pl.program_id(0)
    row, col = grid_index()
    causal, strict = row >= col, row > col
    cum = cumulative_decay(ld_ref[...], row, col)
    cum_t = cum.T
    beta = be_ref[...]
    for key_head in range(heads):
        lanes = slice(key_head * DK, (key_head + 1) * DK)
        q = q_ref[:, lanes].astype(F32)
        k = k_ref[:, lanes].astype(F32)
        qn = q * unit(q) * DK ** (-0.5)
        kn = k * unit(k)
        kk = dot3(kn, kn, NT)
        qk = dot3(qn, kn, NT)
        for sub in range(2):
            local = 2 * key_head + sub
            head = 2 * heads * group + local
            cum_col = column(cum, head)
            cum_row = as_row(cum_t, head)
            rate = column(beta, head)
            within = decay_within(cum_col, cum_row, causal)
            coupling = jnp.where(strict, kk * within, 0.0) * rate
            inverse = invert(coupling, row, col)
            growth = jnp.exp(cum_col)
            total = cum_col[T - 1:, :]
            v = v_ref[:, local * DV:(local + 1) * DV].astype(F32)
            u0 = dot1(inverse, rate * v)
            kg = dot1(inverse, (rate * growth) * kn)
            scores = qk * within
            io_ref[local] = dot1(scores, u0)
            r_ref[local] = (growth * qn - dot1(scores, kg)).astype(BF16)
            carried = jnp.exp(total - cum_col) * kn
            transit = dot1(kg, carried, TN).astype(BF16)
            written = dot1(u0, carried, TN).astype(BF16)
            t_ref[local] = inverse.astype(BF16)
            p_ref[local] = scores.astype(BF16)
            u0_ref[local] = u0
            kg_ref[local] = kg.astype(BF16)
            wide = jnp.broadcast_to(total, (TAIL, DK))
            high, low = split(wide)
            low2 = (wide - high.astype(F32) - low.astype(F32)).astype(BF16)
            sub_row = lax.broadcasted_iota(jnp.int32, (TAIL, DK), 0)
            tail = jnp.where(sub_row == 0, high.astype(F32),
                             jnp.where(sub_row == 1, low.astype(F32),
                                       jnp.where(sub_row == 2, low2.astype(F32), 0.0)))
            for half in range(2):
                slot = 2 * local + half
                ab_ref[slot, 0:DK, :] = transit
                ab_ref[slot, DK:DK + HALF, :] = written[half * HALF:(half + 1) * HALF]
                ab_ref[slot, DK + HALF:, :] = tail.astype(BF16)


def forward_local(q, k, v, ld, be, heads=2):
    steps = HK // heads
    nv = 2 * heads
    per_head = lambda dtype: jax.ShapeDtypeStruct((VALUE_HEADS, T, DK), dtype)
    head_block = pl.BlockSpec((nv, T, DK), lambda i: (i, 0, 0))
    whole = pl.BlockSpec((T, VALUE_HEADS), lambda i: (0, 0))
    rows = DK + HALF + TAIL
    return pl.pallas_call(
        functools.partial(forward_kernel, heads),
        grid=(steps,),
        in_specs=[
            pl.BlockSpec((T, heads * DK), lambda i: (0, i)),
            pl.BlockSpec((T, heads * DK), lambda i: (0, i)),
            pl.BlockSpec((T, nv * DV), lambda i: (0, i)),
            whole,
            whole,
        ],
        out_specs=[pl.BlockSpec((2 * nv, rows, DK), lambda i: (i, 0, 0))] + [head_block] * 6,
        out_shape=[
            jax.ShapeDtypeStruct((2 * VALUE_HEADS, rows, DK), BF16),
            per_head(BF16), per_head(BF16), per_head(F32), per_head(BF16), per_head(BF16),
            per_head(F32),
        ],
        compiler_params=pltpu.CompilerParams(vmem_limit_bytes=48 << 20),
        name="forward_local",
    )(q, k, v, ld, be)


def chain_up_kernel(count, ab_ref, s_ref):
    def step(i, state):
        s_ref[i] = state.astype(BF16)
        tail = ab_ref[i, DK + HALF:, :].astype(F32)
        decay = jnp.exp(jnp.sum(tail, axis=0, keepdims=True))
        high, low = split(state)
        moved = dot1(jnp.concatenate([high, low], axis=0), ab_ref[i, 0:DK, :])
        written = ab_ref[i, DK:DK + HALF, :].astype(F32)
        return decay * state - (moved[:HALF] + moved[HALF:]) + written

    lax.fori_loop(0, count, step, jnp.zeros((HALF, DK), F32), unroll=True)


def chain_down_kernel(count, ab_ref, g_ref, l_ref):
    def step(j, state):
        i = count - 1 - j
        l_ref[i] = state.astype(BF16)
        tail = ab_ref[i, DK + HALF:, :].astype(F32)
        decay = jnp.exp(jnp.sum(tail, axis=0, keepdims=True))
        high, low = split(state)
        moved = dot1(jnp.concatenate([high, low], axis=0), ab_ref[i, 0:DK, :], NT)
        return decay * state - (moved[:HALF] + moved[HALF:]) + g_ref[i].astype(F32)

    lax.fori_loop(0, count, step, jnp.zeros((HALF, DK), F32), unroll=True)


def chain(kernel, count, *args):
    return pl.pallas_call(
        functools.partial(kernel, count),
        out_shape=jax.ShapeDtypeStruct((count, HALF, DK), BF16),
        compiler_params=pltpu.CompilerParams(vmem_limit_bytes=48 << 20),
        name="chain",
    )(*args)


def gate_kernel(heads, s_ref, gate_ref, bg_ref, io_ref, u0_ref, kg_ref, r_ref,
                normed_ref, gg_ref, do_ref, u_ref, g_ref):
    for local in range(heads):
        lanes = slice(local * DV, (local + 1) * DV)
        state = s_ref[local]
        reach = r_ref[local]
        out = io_ref[local] + dot1(reach, state, NT)
        u_ref[local] = (u0_ref[local] - dot1(kg_ref[local], state, NT)).astype(BF16)
        scale = lax.rsqrt(jnp.mean(out * out, axis=-1, keepdims=True) + NORM_EPS)
        z = out * scale
        gate = gate_ref[:, lanes].astype(F32)
        sig = 1.0 / (1.0 + jnp.exp(-gate))
        sil = gate * sig
        normed_ref[:, lanes] = (z * sil).astype(BF16)
        bg = bg_ref[:, lanes].astype(F32)
        gg_ref[:, lanes] = (bg * z * (sig + sil * (1.0 - sig))).astype(BF16)
        dz = bg * sil
        d_out = scale * (dz - z * jnp.mean(dz * z, axis=-1, keepdims=True))
        d_out = d_out.astype(BF16)
        do_ref[local] = d_out
        g_ref[local] = dot1(d_out, reach, TN).astype(BF16)


def gate_local(s, gate, bg, io, u0, kg, r, heads=4):
    steps = VALUE_HEADS // heads
    head_block = pl.BlockSpec((heads, T, DK), lambda i: (i, 0, 0))
    flat = pl.BlockSpec((T, heads * DV), lambda i: (0, i))
    per_head = jax.ShapeDtypeStruct((VALUE_HEADS, T, DK), BF16)
    tokens = jax.ShapeDtypeStruct((T, VALUE_HEADS * DV), BF16)
    return pl.pallas_call(
        functools.partial(gate_kernel, heads),
        grid=(steps,),
        in_specs=[head_block, flat, flat] + [head_block] * 4,
        out_specs=[flat, flat] + [head_block] * 3,
        out_shape=[tokens, tokens, per_head, per_head, per_head],
        compiler_params=pltpu.CompilerParams(vmem_limit_bytes=48 << 20),
        name="gate_local",
    )(s, gate, bg, io, u0, kg, r)


def backward_kernel(heads, q_ref, k_ref, ld_ref, be_ref, t_ref, p_ref, u_ref, do_ref, s_ref, l_ref,
                    dq_ref, dk_ref, dv_ref):
    group = pl.program_id(0)
    row, col = grid_index()
    causal, strict = row >= col, row > col
    cum = cumulative_decay(ld_ref[...], row, col)
    cum_t = cum.T
    beta = be_ref[...]
    for key_head in range(heads):
        lanes = slice(key_head * DK, (key_head + 1) * DK)
        q = q_ref[:, lanes].astype(F32)
        k = k_ref[:, lanes].astype(F32)
        q_scale, k_scale = unit(q), unit(k)
        qn = q * q_scale * DK ** (-0.5)
        kn = k * k_scale
        qn_b, kn_b = qn.astype(BF16), kn.astype(BF16)
        dqn = jnp.zeros((T, DK), F32)
        dkn = jnp.zeros((T, DK), F32)
        for sub in range(2):
            local = 2 * key_head + sub
            head = 2 * heads * group + local
            cum_col = column(cum, head)
            cum_row = as_row(cum_t, head)
            rate = column(beta, head)
            within = decay_within(cum_col, cum_row, causal)
            growth = jnp.exp(cum_col)
            fade = jnp.exp(cum_col[T - 1:, :] - cum_col)
            state, leaving = s_ref[local], l_ref[local]
            u, d_out = u_ref[local], do_ref[local]
            du = dot1(p_ref[local], d_out, TN) + fade * dot1(kn_b, leaving, NT)
            dx = dot1(t_ref[local], du, TN)
            dv_ref[:, local * DV:(local + 1) * DV] = (rate * dx).astype(BF16)
            dx_b = dx.astype(BF16)
            d_scores = dot1(d_out, u, NT) * within
            d_inter = jnp.where(strict, dot1(dx_b, u, NT) * within, 0.0) * (-rate)
            both = d_inter + d_inter.T
            d_scores_b = d_scores.astype(BF16)
            dqn += growth * dot1(d_out, state) + dot1(d_scores_b, kn_b)
            dkn += (dot1(d_scores_b, qn_b, TN) + dot1(both, kn_b)
                    - (rate * growth) * dot1(dx_b, state) + fade * dot1(u, leaving))
        dq = q_scale * DK ** (-0.5) * (
            dqn - q * (q_scale * q_scale) * jnp.sum(q * dqn, axis=-1, keepdims=True))
        dk = k_scale * (dkn - k * (k_scale * k_scale) * jnp.sum(k * dkn, axis=-1, keepdims=True))
        dq_ref[:, lanes] = dq.astype(BF16)
        dk_ref[:, lanes] = dk.astype(BF16)


def backward_local(q, k, ld, be, t, p, u, d_out, s, l, heads=2):
    steps = HK // heads
    nv = 2 * heads
    head_block = pl.BlockSpec((nv, T, DK), lambda i: (i, 0, 0))
    keys = pl.BlockSpec((T, heads * DK), lambda i: (0, i))
    values = pl.BlockSpec((T, nv * DV), lambda i: (0, i))
    whole = pl.BlockSpec((T, VALUE_HEADS), lambda i: (0, 0))
    return pl.pallas_call(
        functools.partial(backward_kernel, heads),
        grid=(steps,),
        in_specs=[keys, keys, whole, whole] + [head_block] * 6,
        out_specs=[keys, keys, values],
        out_shape=[
            jax.ShapeDtypeStruct((T, HK * DK), BF16),
            jax.ShapeDtypeStruct((T, HK * DK), BF16),
            jax.ShapeDtypeStruct((T, VALUE_HEADS * DV), BF16),
        ],
        compiler_params=pltpu.CompilerParams(vmem_limit_bytes=48 << 20),
        name="backward_local",
    )(q, k, ld, be, t, p, u, d_out, s, l)


def pair_weights(log_ratio, pairing):
    seq_count = log_ratio.shape[0]
    couples = pairing.reshape(seq_count // 2, 2)
    seq_index = lax.broadcasted_iota(jnp.int32, (seq_count // 2, seq_count), 1)
    chosen = (couples[:, :1] == seq_index).astype(log_ratio.dtype)
    rejected = (couples[:, 1:] == seq_index).astype(log_ratio.dtype)
    ratio_c = jnp.sum(chosen * log_ratio[None, :], axis=1)
    ratio_r = jnp.sum(rejected * log_ratio[None, :], axis=1)
    margin = CHI_BETA * (jnp.exp(ratio_c) + ratio_c - jnp.exp(ratio_r) - ratio_r)
    pull_scale = CHI_BETA * jax.nn.sigmoid(-margin)
    weight_c = -pull_scale * (jnp.exp(ratio_c) + 1.0)
    weight_r = pull_scale * (jnp.exp(ratio_r) + 1.0)
    return jnp.sum(chosen * weight_c[:, None] + rejected * weight_r[:, None], axis=0)


def exchange(x, axis):
    return lax.all_to_all(x, axis, split_axis=0, concat_axis=0, tiled=True)


def body(query_vectors, key_vectors, value_vectors, output_gate, log_decay, write_rate,
         out_weight, cotangent, lengths, pairing, log_ratio):
    q, k, v, gate = query_vectors[0], key_vectors[0], value_vectors[0], output_gate[0]
    ld, be = log_decay[0], write_rate[0]
    tokens = q.shape[0]
    count = lax.axis_size("ctx")
    seqs = lax.axis_size("fsdp")
    own_seq = lax.axis_index("fsdp")
    features = out_weight.shape[0]

    with jax.named_scope("scaled_cotangent"):
        weights = pair_weights(log_ratio, pairing)
        seq_ids = lax.broadcasted_iota(jnp.int32, weights.shape, 0)
        own_weight = jnp.sum(jnp.where(seq_ids == own_seq, weights, 0.0))
        own_length = jnp.sum(jnp.where(seq_ids == own_seq, lengths, 0))
        positions = lax.axis_index("ctx") * tokens + lax.broadcasted_iota(
            jnp.int32, (tokens, 1), 0)
        live = (positions < own_length).astype(F32)
        scaled = (cotangent[0].astype(F32) * (own_weight * live)).astype(BF16)
        every_scaled = lax.all_gather(scaled, "fsdp", axis=0, tiled=True)
    with jax.named_scope("back_grad"):
        bg_slice = lax.dot_general(every_scaled, out_weight, NT,
                                   preferred_element_type=F32).astype(BF16)
        bg_all = lax.all_gather(bg_slice, "fsdp", axis=0)
        bg = lax.dynamic_slice_in_dim(bg_all, own_seq * tokens, tokens, axis=1)
        bg = jnp.swapaxes(bg, 0, 1).reshape(tokens, seqs * features)

    ab, t, p, u0, kg, r, io = forward_local(q, k, v, ld, be)
    ab = exchange(ab, "ctx")
    entering = exchange(chain(chain_up_kernel, count, ab), "ctx").reshape(VALUE_HEADS, DV, DK)
    normed, gate_grad, d_out, u, g = gate_local(entering, gate, bg, io, u0, kg, r)
    with jax.named_scope("every_normed"):
        every_normed = lax.all_gather(normed, "fsdp", axis=0, tiled=True)
        rows = lax.dynamic_slice_in_dim(every_normed, own_seq * features, features, axis=1)
    with jax.named_scope("mixed_out"):
        mixed = lax.dot_general(rows, out_weight, NN, preferred_element_type=F32).astype(BF16)
        mixed = lax.psum_scatter(mixed, "fsdp", scatter_dimension=0, tiled=True)
    with jax.named_scope("weight_grad"):
        partial = lax.dot_general(rows, every_scaled, TN, preferred_element_type=F32).astype(BF16)
        weight_grad = lax.psum_scatter(
            partial, "ctx", scatter_dimension=0, tiled=True).astype(F32)
    g = exchange(g.reshape(count, HALF, DK), "ctx")
    leaving = exchange(chain(chain_down_kernel, count, ab, g), "ctx").reshape(VALUE_HEADS, DV, DK)
    dq, dk, dv = backward_local(q, k, ld, be, t, p, u, d_out, entering, leaving)
    return mixed[None], dq[None], dk[None], dv[None], gate_grad[None], weight_grad


def solution(mesh):
    tokens = P("fsdp", "ctx", None)
    return jax.shard_map(
        body,
        mesh=mesh,
        in_specs=(tokens,) * 6 + (P("fsdp", None), tokens, P(), P(), P()),
        out_specs=(tokens,) * 5 + (P(("fsdp", "ctx"), None),),
        check_vma=False,
    )
```

```python
import functools

import jax
import jax.numpy as jnp
from jax import lax
from jax.experimental import pallas as pl
from jax.experimental.pallas import tpu as pltpu
from jax.sharding import PartitionSpec as P

VALUE_HEADS = 16
HK = 8
DK = 128
DV = 128
T = 128
HALF = 64
TAIL = 16
CHI_BETA = 0.5
NORM_EPS = 1e-06
F32 = jnp.float32
BF16 = jnp.bfloat16

NN = (((1,), (0,)), ((), ()))
NT = (((1,), (1,)), ((), ()))
TN = (((0,), (0,)), ((), ()))


def dot1(a, b, dims=NN):
    return lax.dot_general(a.astype(BF16), b.astype(BF16), dims, preferred_element_type=F32)


def split(a):
    high = a.astype(BF16)
    return high, (a - high.astype(F32)).astype(BF16)


def dot3(a, b, dims=NN):
    a_high, a_low = split(a)
    b_high, b_low = split(b)
    return dot1(a_high, b_high, dims) + (dot1(a_low, b_high, dims) + dot1(a_high, b_low, dims))


def grid_index():
    row = lax.broadcasted_iota(jnp.int32, (T, T), 0)
    col = lax.broadcasted_iota(jnp.int32, (T, T), 1)
    return row, col


def unit(x):
    return lax.rsqrt(jnp.sum(x * x, axis=-1, keepdims=True) + NORM_EPS)


def cumulative_decay(decay, row, col):
    lower = (row >= col).astype(BF16)
    first, rest = decay.astype(BF16), decay
    rest = rest - first.astype(F32)
    second = rest.astype(BF16)
    third = (rest - second.astype(F32)).astype(BF16)
    return dot1(lower, first) + (dot1(lower, second) + dot1(lower, third))


def column(table, head):
    lane = lax.broadcasted_iota(jnp.int32, table.shape, 1)
    return jnp.sum(jnp.where(lane == head, table, 0.0), axis=1, keepdims=True)


def as_row(table_t, head):
    sub = lax.broadcasted_iota(jnp.int32, table_t.shape, 0)
    return jnp.sum(jnp.where(sub == head, table_t, 0.0), axis=0, keepdims=True)


def decay_within(cum_col, cum_row, causal):
    return jnp.where(causal, jnp.exp(jnp.where(causal, cum_col - cum_row, 0.0)), 0.0)


def invert(couplings, row, col):
    eye = (row == col).astype(F32)
    pairs = (row >> 1) == (col >> 1)
    inverses = [eye - jnp.where(pairs, c, 0.0) for c in couplings]
    for level in range(1, 7):
        mask = ((row >> (level + 1)) == (col >> (level + 1))) & ((row >> level) != (col >> level))
        offs = [jnp.where(mask, c, 0.0).astype(BF16) for c in couplings]
        low = [i.astype(BF16) for i in inverses]
        inner = [dot1(o, i) for o, i in zip(offs, low)]
        inverses = [x - dot1(i, n) for x, i, n in zip(inverses, low, inner)]
    residuals = [eye - i - dot3(c, i) for c, i in zip(couplings, inverses)]
    return [i + dot1(i, r) for i, r in zip(inverses, residuals)]


def total_rows(total):
    wide = jnp.broadcast_to(total, (TAIL, DK))
    high, low = split(wide)
    low2 = (wide - high.astype(F32) - low.astype(F32)).astype(BF16)
    sub_row = lax.broadcasted_iota(jnp.int32, (TAIL, DK), 0)
    tail = jnp.where(sub_row == 0, high.astype(F32),
                     jnp.where(sub_row == 1, low.astype(F32),
                               jnp.where(sub_row == 2, low2.astype(F32), 0.0)))
    return tail.astype(BF16)


def write_kernel(heads, k_ref, v_ref, ld_ref, be_ref, ab_ref, t_ref, u0_ref, kg_ref):
    group = pl.program_id(0)
    row, col = grid_index()
    causal, strict = row >= col, row > col
    cum = cumulative_decay(ld_ref[...], row, col)
    cum_t = cum.T
    beta = be_ref[...]
    kns, kks = [], []
    for key_head in range(heads):
        k = k_ref[:, key_head * DK:(key_head + 1) * DK].astype(F32)
        kn = k * unit(k)
        kns.append(kn)
        kks.append(dot3(kn, kn, NT))
    cols, rates, couplings = [], [], []
    for local in range(2 * heads):
        head = 2 * heads * group + local
        cum_col = column(cum, head)
        rate = column(beta, head)
        within = decay_within(cum_col, as_row(cum_t, head), causal)
        couplings.append(jnp.where(strict, kks[local // 2] * within, 0.0) * rate)
        cols.append(cum_col)
        rates.append(rate)
    inverses = [i.astype(BF16) for i in invert(couplings, row, col)]
    u0s = [dot1(i, rates[n] * v_ref[:, n * DV:(n + 1) * DV].astype(F32))
           for n, i in enumerate(inverses)]
    kgs = [dot1(i, (rates[n] * jnp.exp(cols[n])) * kns[n // 2]).astype(BF16)
           for n, i in enumerate(inverses)]
    for n in range(2 * heads):
        total = cols[n][T - 1:, :]
        carried = (jnp.exp(total - cols[n]) * kns[n // 2]).astype(BF16)
        transit = dot1(kgs[n], carried, TN).astype(BF16)
        written = dot1(u0s[n], carried, TN).astype(BF16)
        t_ref[n] = inverses[n]
        u0_ref[n] = u0s[n]
        kg_ref[n] = kgs[n]
        tail = total_rows(total)
        for half in range(2):
            slot = 2 * n + half
            ab_ref[slot, 0:DK, :] = transit
            ab_ref[slot, DK:DK + HALF, :] = written[half * HALF:(half + 1) * HALF]
            ab_ref[slot, DK + HALF:, :] = tail


def read_kernel(heads, q_ref, k_ref, ld_ref, u0_ref, kg_ref, p_ref, r_ref, io_ref):
    group = pl.program_id(0)
    row, col = grid_index()
    causal = row >= col
    cum = cumulative_decay(ld_ref[...], row, col)
    cum_t = cum.T
    qns, qks = [], []
    for key_head in range(heads):
        lanes = slice(key_head * DK, (key_head + 1) * DK)
        q = q_ref[:, lanes].astype(F32)
        k = k_ref[:, lanes].astype(F32)
        qn = q * unit(q) * DK ** (-0.5)
        qns.append(qn)
        qks.append(dot3(qn, k * unit(k), NT))
    cols, scores = [], []
    for local in range(2 * heads):
        head = 2 * heads * group + local
        cum_col = column(cum, head)
        cols.append(cum_col)
        scores.append(
            (qks[local // 2] * decay_within(cum_col, as_row(cum_t, head), causal)).astype(BF16))
    for n in range(2 * heads):
        p_ref[n] = scores[n]
        io_ref[n] = dot1(scores[n], u0_ref[n])
        r_ref[n] = (jnp.exp(cols[n]) * qns[n // 2] - dot1(scores[n], kg_ref[n])).astype(BF16)


def per_head(dtype):
    return jax.ShapeDtypeStruct((VALUE_HEADS, T, DK), dtype)


def head_block(count):
    return pl.BlockSpec((count, T, DK), lambda i: (i, 0, 0))


def flat_block(count):
    return pl.BlockSpec((T, count * DK), lambda i: (0, i))


WHOLE = pl.BlockSpec((T, VALUE_HEADS), lambda i: (0, 0))
PARAMS = pltpu.CompilerParams(vmem_limit_bytes=60 << 20)


def cost(gflops):
    return pl.CostEstimate(flops=int(gflops * 1e9), bytes_accessed=4 << 20, transcendentals=0)


def write_local(k, v, ld, be, heads=2):
    nv = 2 * heads
    rows = DK + HALF + TAIL
    return pl.pallas_call(
        functools.partial(write_kernel, heads),
        grid=(HK // heads,),
        in_specs=[flat_block(heads), flat_block(nv), WHOLE, WHOLE],
        out_specs=[pl.BlockSpec((2 * nv, rows, DK), lambda i: (i, 0, 0))] + [head_block(nv)] * 3,
        out_shape=[jax.ShapeDtypeStruct((2 * VALUE_HEADS, rows, DK), BF16),
                   per_head(BF16), per_head(F32), per_head(BF16)],
        compiler_params=PARAMS,
        cost_estimate=cost(20),
        name="write_local",
    )(k, v, ld, be)


def read_local(q, k, ld, u0, kg, heads=2):
    nv = 2 * heads
    return pl.pallas_call(
        functools.partial(read_kernel, heads),
        grid=(HK // heads,),
        in_specs=[flat_block(heads), flat_block(heads), WHOLE, head_block(nv), head_block(nv)],
        out_specs=[head_block(nv)] * 3,
        out_shape=[per_head(BF16), per_head(BF16), per_head(F32)],
        compiler_params=PARAMS,
        cost_estimate=cost(8),
        name="read_local",
    )(q, k, ld, u0, kg)


def chain_up_kernel(count, ab_ref, s_ref):
    def step(i, state):
        s_ref[i] = state.astype(BF16)
        tail = ab_ref[i, DK + HALF:, :].astype(F32)
        decay = jnp.exp(jnp.sum(tail, axis=0, keepdims=True))
        high, low = split(state)
        moved = dot1(jnp.concatenate([high, low], axis=0), ab_ref[i, 0:DK, :])
        written = ab_ref[i, DK:DK + HALF, :].astype(F32)
        return decay * state - (moved[:HALF] + moved[HALF:]) + written

    lax.fori_loop(0, count, step, jnp.zeros((HALF, DK), F32), unroll=True)


def chain_down_kernel(count, ab_ref, g_ref, l_ref):
    def step(j, state):
        i = count - 1 - j
        l_ref[i] = state.astype(BF16)
        tail = ab_ref[i, DK + HALF:, :].astype(F32)
        decay = jnp.exp(jnp.sum(tail, axis=0, keepdims=True))
        high, low = split(state)
        moved = dot1(jnp.concatenate([high, low], axis=0), ab_ref[i, 0:DK, :], NT)
        return decay * state - (moved[:HALF] + moved[HALF:]) + g_ref[i].astype(F32)

    lax.fori_loop(0, count, step, jnp.zeros((HALF, DK), F32), unroll=True)


def chain(kernel, count, *args):
    return pl.pallas_call(
        functools.partial(kernel, count),
        out_shape=jax.ShapeDtypeStruct((count, HALF, DK), BF16),
        compiler_params=PARAMS,
        cost_estimate=cost(4),
        name="chain",
    )(*args)


def gate_kernel(heads, me_ref, s_ref, gate_ref, bg_ref, io_ref, u0_ref, kg_ref, r_ref,
                normed_ref, gg_ref, do_ref, u_ref, g_ref):
    for local in range(heads):
        lanes = slice(local * DV, (local + 1) * DV)
        state = s_ref[local]
        reach = r_ref[local]
        out = io_ref[local] + dot1(reach, state, NT)
        u_ref[local] = (u0_ref[local] - dot1(kg_ref[local], state, NT)).astype(BF16)
        scale = lax.rsqrt(jnp.mean(out * out, axis=-1, keepdims=True) + NORM_EPS)
        z = out * scale
        gate = gate_ref[:, lanes].astype(F32)
        sig = 1.0 / (1.0 + jnp.exp(-gate))
        sil = gate * sig
        normed_ref[0, :, lanes] = (z * sil).astype(BF16)
        bg = bg_ref[0, :, lanes].astype(F32)
        gg_ref[:, lanes] = (bg * z * (sig + sil * (1.0 - sig))).astype(BF16)
        dz = bg * sil
        d_out = scale * (dz - z * jnp.mean(dz * z, axis=-1, keepdims=True))
        d_out = d_out.astype(BF16)
        do_ref[local] = d_out
        g_ref[local] = dot1(d_out, reach, TN).astype(BF16)


def gate_local(me, s, gate, bg, io, u0, kg, r, seqs):
    heads = VALUE_HEADS // seqs
    blocks = pl.BlockSpec((heads, T, DK), lambda i, me: (i, 0, 0))
    flat = pl.BlockSpec((T, heads * DV), lambda i, me: (0, i))
    crossed = pl.BlockSpec((1, T, heads * DV), lambda i, me: (i ^ me[0], 0, 0))
    tokens = jax.ShapeDtypeStruct((T, VALUE_HEADS * DV), BF16)
    return pl.pallas_call(
        functools.partial(gate_kernel, heads),
        grid_spec=pltpu.PrefetchScalarGridSpec(
            num_scalar_prefetch=1,
            grid=(seqs,),
            in_specs=[blocks, flat, crossed] + [blocks] * 4,
            out_specs=[crossed, flat] + [blocks] * 3,
        ),
        out_shape=[jax.ShapeDtypeStruct((seqs, T, heads * DV), BF16), tokens,
                   per_head(BF16), per_head(BF16), per_head(BF16)],
        compiler_params=PARAMS,
        cost_estimate=cost(5),
        name="gate_local",
    )(me, s, gate, bg, io, u0, kg, r)


def early_kernel(heads, q_ref, k_ref, ld_ref, p_ref, u_ref, do_ref, s_ref,
                 dq_ref, dk_ref, du_ref):
    group = pl.program_id(0)
    row, col = grid_index()
    causal = row >= col
    cum = cumulative_decay(ld_ref[...], row, col)
    cum_t = cum.T
    for key_head in range(heads):
        lanes = slice(key_head * DK, (key_head + 1) * DK)
        q = q_ref[:, lanes].astype(F32)
        k = k_ref[:, lanes].astype(F32)
        q_scale = unit(q)
        qn = (q * q_scale * DK ** (-0.5)).astype(BF16)
        kn = (k * unit(k)).astype(BF16)
        dqn = jnp.zeros((T, DK), F32)
        dkn = jnp.zeros((T, DK), F32)
        for sub in range(2):
            n = 2 * key_head + sub
            head = 2 * heads * group + n
            cum_col = column(cum, head)
            within = decay_within(cum_col, as_row(cum_t, head), causal)
            d_out = do_ref[n]
            du_ref[n] = dot1(p_ref[n], d_out, TN)
            d_scores = (dot1(d_out, u_ref[n], NT) * within).astype(BF16)
            dqn += jnp.exp(cum_col) * dot1(d_out, s_ref[n]) + dot1(d_scores, kn)
            dkn += dot1(d_scores, qn, TN)
        dq = q_scale * DK ** (-0.5) * (
            dqn - q * (q_scale * q_scale) * jnp.sum(q * dqn, axis=-1, keepdims=True))
        dq_ref[:, lanes] = dq.astype(BF16)
        dk_ref[:, lanes] = dkn


def late_kernel(heads, k_ref, ld_ref, be_ref, t_ref, u_ref, s_ref, l_ref, dkn_ref, du_ref,
                dk_ref, dv_ref):
    group = pl.program_id(0)
    row, col = grid_index()
    strict = row > col
    cum = cumulative_decay(ld_ref[...], row, col)
    cum_t = cum.T
    beta = be_ref[...]
    for key_head in range(heads):
        lanes = slice(key_head * DK, (key_head + 1) * DK)
        k = k_ref[:, lanes].astype(F32)
        k_scale = unit(k)
        kn = (k * k_scale).astype(BF16)
        dkn = dkn_ref[:, lanes]
        for sub in range(2):
            n = 2 * key_head + sub
            head = 2 * heads * group + n
            cum_col = column(cum, head)
            rate = column(beta, head)
            within = decay_within(cum_col, as_row(cum_t, head), strict)
            fade = jnp.exp(cum_col[T - 1:, :] - cum_col)
            u, leaving = u_ref[n], l_ref[n]
            du = du_ref[n] + fade * dot1(kn, leaving, NT)
            dx = dot1(t_ref[n], du, TN)
            dv_ref[:, n * DV:(n + 1) * DV] = (rate * dx).astype(BF16)
            dx = dx.astype(BF16)
            d_inter = dot1(dx, u, NT) * within * (-rate)
            dkn += (dot1(d_inter + d_inter.T, kn) + fade * dot1(u, leaving)
                    - (rate * jnp.exp(cum_col)) * dot1(dx, s_ref[n]))
        dk = k_scale * (dkn - k * (k_scale * k_scale) * jnp.sum(k * dkn, axis=-1, keepdims=True))
        dk_ref[:, lanes] = dk.astype(BF16)


def early_local(q, k, ld, p, u, d_out, s, heads=2):
    nv = 2 * heads
    keys = flat_block(heads)
    return pl.pallas_call(
        functools.partial(early_kernel, heads),
        grid=(HK // heads,),
        in_specs=[keys, keys, WHOLE] + [head_block(nv)] * 4,
        out_specs=[keys, keys, head_block(nv)],
        out_shape=[jax.ShapeDtypeStruct((T, HK * DK), BF16),
                   jax.ShapeDtypeStruct((T, HK * DK), F32), per_head(F32)],
        compiler_params=PARAMS,
        cost_estimate=cost(6),
        name="early_local",
    )(q, k, ld, p, u, d_out, s)


def late_local(k, ld, be, t, u, s, l, dkn, du, heads=2):
    nv = 2 * heads
    keys = flat_block(heads)
    return pl.pallas_call(
        functools.partial(late_kernel, heads),
        grid=(HK // heads,),
        in_specs=[keys, WHOLE, WHOLE] + [head_block(nv)] * 4 + [keys, head_block(nv)],
        out_specs=[keys, flat_block(nv)],
        out_shape=[jax.ShapeDtypeStruct((T, HK * DK), BF16),
                   jax.ShapeDtypeStruct((T, VALUE_HEADS * DV), BF16)],
        compiler_params=PARAMS,
        cost_estimate=cost(8),
        name="late_local",
    )(k, ld, be, t, u, s, l, dkn, du)


def scale_kernel(lengths_ref, pairing_ref, ratio_ref, cot_ref, scaled_ref):
    own = lax.axis_index("fsdp")
    tokens = cot_ref.shape[0]
    weight = jnp.zeros((8, 128), F32)
    for pair in range(pairing_ref.shape[0] // 2):
        chosen, rejected = pairing_ref[2 * pair], pairing_ref[2 * pair + 1]
        ratio_c = jnp.full((8, 128), ratio_ref[chosen], F32)
        ratio_r = jnp.full((8, 128), ratio_ref[rejected], F32)
        up_c, up_r = jnp.exp(ratio_c), jnp.exp(ratio_r)
        margin = CHI_BETA * (up_c + ratio_c - up_r - ratio_r)
        pull = CHI_BETA / (1.0 + jnp.exp(margin))
        weight = weight + jnp.where(chosen == own, -pull * (up_c + 1.0), 0.0)
        weight = weight + jnp.where(rejected == own, pull * (up_r + 1.0), 0.0)
    position = lax.axis_index("ctx") * tokens + lax.broadcasted_iota(jnp.int32, (tokens, 1), 0)
    live = (position < lengths_ref[own]).astype(F32)
    factor = weight[0:1, 0:1] * live
    scaled_ref[...] = (cot_ref[...].astype(F32) * factor).astype(BF16)


def scale_local(lengths, pairing, ratio, cot):
    scalars = pl.BlockSpec(memory_space=pltpu.SMEM)
    return pl.pallas_call(
        scale_kernel,
        in_specs=[scalars] * 3 + [pl.BlockSpec(memory_space=pltpu.VMEM)],
        out_specs=pl.BlockSpec(memory_space=pltpu.VMEM),
        out_shape=jax.ShapeDtypeStruct(cot.shape, BF16),
        compiler_params=PARAMS,
        cost_estimate=cost(1),
        name="scale_local",
    )(lengths, pairing, ratio, cot)


def weight_kernel(place_ref, rows_ref, scaled_ref, keep_ref, send_ref, part_ref):
    across, along, core = place_ref[0], place_ref[1], place_ref[2]
    part_ref[...] = dot1(rows_ref[...], scaled_ref[...], TN).astype(BF16)
    for x in range(4):
        for y in range(4):
            slot = (x ^ across) * 4 + (y ^ along)
            first = (x * 4 + y) * 32
            keep_ref[slot] = part_ref[pl.ds(pl.multiple_of(first + core * 16, 16), 16), :]
            send_ref[slot] = part_ref[pl.ds(pl.multiple_of(first + 16 - core * 16, 16), 16), :]


def weight_local(place, rows, scaled, width=512):
    features = rows.shape[1]
    tokens, columns = scaled.shape
    out = pl.BlockSpec((16, 16, width), lambda i: (0, 0, i))
    shape = jax.ShapeDtypeStruct((16, 16, columns), BF16)
    return pl.pallas_call(
        weight_kernel,
        grid=(columns // width,),
        in_specs=[pl.BlockSpec(memory_space=pltpu.SMEM),
                  pl.BlockSpec((tokens, features), lambda i: (0, 0)),
                  pl.BlockSpec((tokens, width), lambda i: (0, i))],
        out_specs=[out, out],
        out_shape=[shape, shape],
        scratch_shapes=[pltpu.VMEM((features, width), BF16)],
        compiler_params=PARAMS,
        cost_estimate=cost(4),
        name="weight_local",
    )(place, rows, scaled)


def exchange(x, axis):
    return lax.all_to_all(x, axis, split_axis=0, concat_axis=0, tiled=True)


def cross(x, axis, distance):
    count = lax.axis_size(axis)
    return lax.ppermute(x, axis, [(i, i ^ distance) for i in range(count)])


def tie(*values):
    return lax.optimization_barrier(values)


def add_up(parts):
    return functools.reduce(lambda a, b: a + b, [part.astype(F32) for part in parts])


def body(query_vectors, key_vectors, value_vectors, output_gate, log_decay, write_rate,
         out_weight, cotangent, lengths, pairing, log_ratio):
    q, k, v, gate = query_vectors[0], key_vectors[0], value_vectors[0], output_gate[0]
    ld, be = log_decay[0], write_rate[0]
    tokens = q.shape[0]
    count = lax.axis_size("ctx")
    seqs = lax.axis_size("fsdp")
    features = out_weight.shape[0]
    me = lax.axis_index("fsdp").reshape(1)
    spot = lax.axis_index("ctx")
    place = jnp.stack([spot // 8, (spot // 2) % 4, spot % 2])

    scaled = scale_local(lengths, pairing, log_ratio, cotangent[0])
    with jax.named_scope("every_scaled"):
        others = [cross(scaled, "fsdp", s) for s in range(1, seqs)]
    ab, t, u0, kg = write_local(k, v, ld, be)
    with jax.named_scope("back_grad"):
        others = list(tie(ab, *others)[1:])
        every_scaled = jnp.concatenate([scaled] + others, axis=0)
        bg = lax.dot_general(every_scaled, out_weight, NT, preferred_element_type=F32)
        bg = bg.astype(BF16).reshape(seqs, tokens, features)
    ab = exchange(ab, "ctx")
    p, r, io = read_local(q, k, ld, u0, kg)
    ab, p, r, io, bg = tie(ab, p, r, io, bg)
    with jax.named_scope("back_grad"):
        bg = jnp.stack([bg[0]] + [cross(bg[s], "fsdp", s) for s in range(1, seqs)])
    entering = exchange(chain(chain_up_kernel, count, ab), "ctx").reshape(VALUE_HEADS, DV, DK)
    normed, gate_grad, d_out, u, g = gate_local(me, entering, gate, bg, io, u0, kg, r, seqs)
    with jax.named_scope("every_normed"):
        rows = jnp.concatenate(
            [normed[0]] + [cross(normed[s], "fsdp", s) for s in range(1, seqs)], axis=0)
    g = exchange(g.reshape(count, HALF, DK), "ctx")
    dq, dkn, du = early_local(q, k, ld, p, u, d_out, entering)
    g, dq, dkn, du = tie(g, dq, dkn, du)
    leaving = exchange(chain(chain_down_kernel, count, ab, g), "ctx").reshape(VALUE_HEADS, DV, DK)
    with jax.named_scope("weight_grad"):
        keep, send = weight_local(place, rows, every_scaled)
        both = add_up([keep, cross(send, "ctx", 1)]).astype(BF16).reshape(4, 4, 16, -1)
    with jax.named_scope("mixed_out"):
        mixed = lax.dot_general(rows, out_weight, NN, preferred_element_type=F32)
        mixed = mixed.astype(BF16).reshape(seqs, tokens, -1)
    leaving, both, mixed = tie(leaving, both, mixed)
    with jax.named_scope("weight_grad"):
        line = add_up([both[:, 0]] + [cross(both[:, s], "ctx", 2 * s) for s in range(1, 4)])
        line = line.astype(BF16)
        weight_grad = add_up([line[0]] + [cross(line[s], "ctx", 8 * s) for s in range(1, 4)])
    with jax.named_scope("mixed_out"):
        mixed = add_up([mixed[0]] + [cross(mixed[s], "fsdp", s) for s in range(1, seqs)])
        mixed = mixed.astype(BF16)
    dk, dv = late_local(k, ld, be, t, u, entering, leaving, dkn, du)
    return mixed[None], dq[None], dk[None], dv[None], gate_grad[None], weight_grad


def solution(mesh):
    tokens = P("fsdp", "ctx", None)
    return jax.shard_map(
        body,
        mesh=mesh,
        in_specs=(tokens,) * 6 + (P("fsdp", None), tokens, P(), P(), P()),
        out_specs=(tokens,) * 5 + (P(("fsdp", "ctx"), None),),
        check_vma=False,
    )
```

```python
import functools

import jax
import jax.numpy as jnp
from jax import lax
from jax.experimental import pallas as pl
from jax.experimental.pallas import tpu as pltpu
from jax.sharding import PartitionSpec as P

VALUE_HEADS = 16
HK = 8
DK = 128
DV = 128
T = 128
HALF = 64
TAIL = 16
CHI_BETA = 0.5
NORM_EPS = 1e-06
F32 = jnp.float32
BF16 = jnp.bfloat16

NN = (((1,), (0,)), ((), ()))
NT = (((1,), (1,)), ((), ()))
TN = (((0,), (0,)), ((), ()))


def dot1(a, b, dims=NN):
    return lax.dot_general(a.astype(BF16), b.astype(BF16), dims, preferred_element_type=F32)


def split(a):
    high = a.astype(BF16)
    return high, (a - high.astype(F32)).astype(BF16)


def dot3(a, b, dims=NN):
    a_high, a_low = split(a)
    b_high, b_low = split(b)
    return dot1(a_high, b_high, dims) + (dot1(a_low, b_high, dims) + dot1(a_high, b_low, dims))


def grid_index():
    row = lax.broadcasted_iota(jnp.int32, (T, T), 0)
    col = lax.broadcasted_iota(jnp.int32, (T, T), 1)
    return row, col


def unit(x):
    return lax.rsqrt(jnp.sum(x * x, axis=-1, keepdims=True) + NORM_EPS)


def dot_exact_left(a, b):
    first = a.astype(BF16)
    rest = a - first.astype(F32)
    second = rest.astype(BF16)
    third = (rest - second.astype(F32)).astype(BF16)
    return dot1(first, b) + (dot1(second, b) + dot1(third, b))


def in_order(sc_ref, own, other):
    is_first = sc_ref[0] == 0
    return jnp.where(is_first, own, other), jnp.where(is_first, other, own)


def decay_tables(sc_ref, own_ref, other_ref, row, col):
    upper = (row <= col).astype(BF16)
    tables = []
    for table in in_order(sc_ref, own_ref[...], other_ref[...]):
        cum_t = dot_exact_left(table[:VALUE_HEADS], upper)
        tables.append((cum_t, cum_t.T, table[VALUE_HEADS:].T))
    return tables


def column(table, head):
    lane = lax.broadcasted_iota(jnp.int32, table.shape, 1)
    return jnp.sum(jnp.where(lane == head, table, 0.0), axis=1, keepdims=True)


def as_row(table_t, head):
    sub = lax.broadcasted_iota(jnp.int32, table_t.shape, 0)
    return jnp.sum(jnp.where(sub == head, table_t, 0.0), axis=0, keepdims=True)


def decay_within(cum_col, cum_row, mask):
    return jnp.where(mask, jnp.exp(jnp.where(mask, cum_col - cum_row, 0.0)), 0.0)


def invert(couplings, row, col):
    eye = (row == col).astype(F32)
    pairs = (row >> 1) == (col >> 1)
    inverses = [eye - jnp.where(pairs, c, 0.0) for c in couplings]
    for level in range(1, 7):
        mask = ((row >> (level + 1)) == (col >> (level + 1))) & ((row >> level) != (col >> level))
        offs = [jnp.where(mask, c, 0.0).astype(BF16) for c in couplings]
        low = [i.astype(BF16) for i in inverses]
        inner = [dot1(o, i) for o, i in zip(offs, low)]
        inverses = [x - dot1(i, n) for x, i, n in zip(inverses, low, inner)]
    residuals = [eye - i - dot3(c, i) for c, i in zip(couplings, inverses)]
    return [i + dot1(i, r) for i, r in zip(inverses, residuals)]


def total_rows(total):
    wide = jnp.broadcast_to(total, (TAIL, DK))
    high, low = split(wide)
    low2 = (wide - high.astype(F32) - low.astype(F32)).astype(BF16)
    sub_row = lax.broadcasted_iota(jnp.int32, (TAIL, DK), 0)
    tail = jnp.where(sub_row == 0, high.astype(F32),
                     jnp.where(sub_row == 1, low.astype(F32),
                               jnp.where(sub_row == 2, low2.astype(F32), 0.0)))
    return tail.astype(BF16)


UNITS = [(sub, block) for sub in range(2) for block in range(2)]


def first_head(sc_ref):
    return (VALUE_HEADS // 2) * sc_ref[0] + 2 * pl.program_id(0)


def write_kernel(sc_ref, ko_ref, vo_ref, lo_ref, kx_ref, vx_ref, lx_ref,
                 ab_ref, t_ref, u0_ref, kg_ref, a_ref, b_ref):
    row, col = grid_index()
    causal, strict = row >= col, row > col
    tables = decay_tables(sc_ref, lo_ref, lx_ref, row, col)
    ks = in_order(sc_ref, ko_ref[...].astype(F32), kx_ref[...].astype(F32))
    vs = in_order(sc_ref, vo_ref[...].astype(F32), vx_ref[...].astype(F32))
    kns = [k * unit(k) for k in ks]
    kks = [dot3(kn, kn, NT) for kn in kns]
    cols, rates, couplings = [], [], []
    for sub, block in UNITS:
        cum_t, cum, beta = tables[block]
        h = first_head(sc_ref) + sub
        cum_col, rate = column(cum, h), column(beta, h)
        within = decay_within(cum_col, as_row(cum_t, h), causal)
        couplings.append(jnp.where(strict, kks[block] * within, 0.0) * rate)
        cols.append(cum_col)
        rates.append(rate)
    inverses = [i.astype(BF16) for i in invert(couplings, row, col)]
    u0s, kgs, transits, writtens, totals = [], [], [], [], []
    for n, (sub, block) in enumerate(UNITS):
        u0s.append(dot1(inverses[n], rates[n] * vs[block][:, sub * DV:(sub + 1) * DV]))
        kgs.append(dot1(inverses[n], (rates[n] * jnp.exp(cols[n])) * kns[block]).astype(BF16))
    for n, (sub, block) in enumerate(UNITS):
        total = cols[n][T - 1:, :]
        carried = (jnp.exp(total - cols[n]) * kns[block]).astype(BF16)
        transits.append(dot1(kgs[n], carried, TN))
        writtens.append(dot1(u0s[n], carried, TN))
        totals.append(total)
        t_ref[n] = inverses[n]
        u0_ref[n] = u0s[n].astype(BF16)
        kg_ref[n] = kgs[n]
        a_ref[n] = transits[n].astype(BF16)
    for sub in range(2):
        f, s = 2 * sub, 2 * sub + 1
        e_f, e_s = jnp.exp(totals[f]), jnp.exp(totals[s])
        stacked = jnp.concatenate([transits[f], writtens[f]], axis=0)
        moved = dot3(stacked, transits[s])
        transit = (e_f * transits[s] + e_s * transits[f] - moved[:DK]).astype(BF16)
        written = (e_s * writtens[f] - moved[DK:] + writtens[s]).astype(BF16)
        b_ref[sub] = writtens[f].astype(BF16)
        tail = total_rows(totals[f] + totals[s])
        for half in range(2):
            slot = 2 * sub + half
            ab_ref[slot, 0:DK, :] = transit
            ab_ref[slot, DK:DK + HALF, :] = written[half * HALF:(half + 1) * HALF]
            ab_ref[slot, DK + HALF:, :] = tail


def read_kernel(sc_ref, qo_ref, ko_ref, lo_ref, qx_ref, kx_ref, lx_ref, u0_ref, kg_ref,
                p_ref, r_ref, io_ref):
    row, col = grid_index()
    causal = row >= col
    tables = decay_tables(sc_ref, lo_ref, lx_ref, row, col)
    qs = in_order(sc_ref, qo_ref[...].astype(F32), qx_ref[...].astype(F32))
    ks = in_order(sc_ref, ko_ref[...].astype(F32), kx_ref[...].astype(F32))
    qns = [q * unit(q) * DK ** (-0.5) for q in qs]
    qks = [dot3(qn, k * unit(k), NT) for qn, k in zip(qns, ks)]
    cols, scores = [], []
    for sub, block in UNITS:
        cum_t, cum, _ = tables[block]
        h = first_head(sc_ref) + sub
        cum_col = column(cum, h)
        cols.append(cum_col)
        scores.append((qks[block] * decay_within(cum_col, as_row(cum_t, h), causal)).astype(BF16))
    for n, (sub, block) in enumerate(UNITS):
        p_ref[n] = scores[n]
        io_ref[n] = dot1(scores[n], u0_ref[n]).astype(BF16)
        r_ref[n] = (jnp.exp(cols[n]) * qns[block] - dot1(scores[n], kg_ref[n])).astype(BF16)


def gate_kernel(sc_ref, s_ref, go_ref, lo_ref, gx_ref, lx_ref, bo_ref, bx_ref,
                a_ref, b_ref, io_ref, u0_ref, kg_ref, r_ref,
                n0_ref, n1_ref, n2_ref, n3_ref, no_ref, nx_ref, gg_ref, ggx_ref, do_ref, u_ref, ss_ref, g_ref, gs_ref):
    gates = in_order(sc_ref, go_ref[...].astype(F32), gx_ref[...].astype(F32))
    me, step = sc_ref[1], pl.program_id(0)
    bgs = in_order(sc_ref, bo_ref[...].astype(F32), bx_ref[...].astype(F32))
    decays = in_order(sc_ref, lo_ref[:VALUE_HEADS], lx_ref[:VALUE_HEADS])[0]
    states, fades = [], []
    for sub in range(2):
        state = s_ref[sub]
        fade = jnp.exp(jnp.sum(as_row(decays, first_head(sc_ref) + sub), axis=1, keepdims=True))
        second = (fade * state.astype(F32) - dot1(state, a_ref[2 * sub])
                  + b_ref[sub].astype(F32)).astype(BF16)
        ss_ref[sub] = second
        states += [state, second]
        fades.append(fade)
    outs = [io_ref[n] + dot1(r_ref[n], states[n], NT) for n in range(4)]
    normeds, gate_grads, d_outs = [], [], []
    for n, (sub, block) in enumerate(UNITS):
        lanes = slice(sub * DV, (sub + 1) * DV)
        u_ref[n] = (u0_ref[n] - dot1(kg_ref[n], states[n], NT)).astype(BF16)
        out = outs[n]
        scale = lax.rsqrt(jnp.mean(out * out, axis=-1, keepdims=True) + NORM_EPS)
        z = out * scale
        gate = gates[block][:, lanes]
        sig = 1.0 / (1.0 + jnp.exp(-gate))
        sil = gate * sig
        normeds.append(z * sil)
        bg = bgs[block][:, lanes]
        gate_grads.append(bg * z * (sig + sil * (1.0 - sig)))
        dz = bg * sil
        d_out = scale * (dz - z * jnp.mean(dz * z, axis=-1, keepdims=True))
        d_outs.append(d_out.astype(BF16))
        do_ref[n] = d_outs[n]
    grads = [dot1(d_outs[n], r_ref[n], TN) for n in range(4)]
    for sub in range(2):
        lanes = slice(sub * DV, (sub + 1) * DV)
        f, s = 2 * sub, 2 * sub + 1
        g_ref[sub] = (grads[f] + fades[sub] * grads[s]
                      - dot1(grads[s], a_ref[f], NT)).astype(BF16)
        gs_ref[sub] = grads[s].astype(BF16)
        own, other = in_order(sc_ref, gate_grads[f], gate_grads[s])
        gg_ref[:, lanes] = own.astype(BF16)
        ggx_ref[:, lanes] = other.astype(BF16)
    columns = pl.ds(pl.multiple_of((step % 2) * 2 * DV, 2 * DV), 2 * DV)
    blocks = [jnp.concatenate([normeds[tau], normeds[2 + tau]], axis=1).astype(BF16)
              for tau in range(2)]
    no_ref[...], nx_ref[...] = in_order(sc_ref, *blocks)
    for n, ref in enumerate((n0_ref, n1_ref, n2_ref, n3_ref)):
        code = me ^ n

        @pl.when(code // 2 == step // 2)
        def _():
            ref[:, columns] = jnp.where(code % 2 == 0, blocks[0], blocks[1])


def early_kernel(sc_ref, qo_ref, ko_ref, lo_ref, qx_ref, kx_ref, lx_ref,
                 p_ref, u_ref, do_ref, s_ref, ss_ref,
                 dq_ref, dqx_ref, dk_ref, du_ref):
    row, col = grid_index()
    causal = row >= col
    tables = decay_tables(sc_ref, lo_ref, lx_ref, row, col)
    qs = in_order(sc_ref, qo_ref[...].astype(F32), qx_ref[...].astype(F32))
    ks = in_order(sc_ref, ko_ref[...].astype(F32), kx_ref[...].astype(F32))
    q_scales = [unit(q) for q in qs]
    qns = [(q * scale * DK ** (-0.5)).astype(BF16) for q, scale in zip(qs, q_scales)]
    kns = [(k * unit(k)).astype(BF16) for k in ks]
    raw = [dot1(do_ref[n], u_ref[n], NT) for n in range(4)]
    cols, d_scores = [], []
    for n, (sub, block) in enumerate(UNITS):
        cum_t, cum, _ = tables[block]
        h = first_head(sc_ref) + sub
        cols.append(column(cum, h))
        d_scores.append((raw[n] * decay_within(cols[n], as_row(cum_t, h), causal)).astype(BF16))
    dqs, dkns = [], []
    for n, (sub, block) in enumerate(UNITS):
        state = s_ref[sub] if block == 0 else ss_ref[sub]
        du_ref[n] = dot1(p_ref[n], do_ref[n], TN).astype(BF16)
        dqs.append(jnp.exp(cols[n]) * dot1(do_ref[n], state) + dot1(d_scores[n], kns[block]))
        dkns.append(dot1(d_scores[n], qns[block], TN))
    results = []
    for block in range(2):
        q, scale, dqn = qs[block], q_scales[block], dqs[block] + dqs[2 + block]
        dk_ref[block] = dkns[block] + dkns[2 + block]
        results.append(scale * DK ** (-0.5) * (
            dqn - q * (scale * scale) * jnp.sum(q * dqn, axis=-1, keepdims=True)))
    own, other = in_order(sc_ref, *results)
    dq_ref[...] = own.astype(BF16)
    dqx_ref[...] = other.astype(BF16)


def late_kernel(sc_ref, ko_ref, lo_ref, kx_ref, lx_ref, t_ref, u_ref, a_ref, s_ref, ss_ref,
                l_ref, gs_ref, dkn_ref, du_ref,
                dk_ref, dv_ref, dkx_ref, dvx_ref):
    row, col = grid_index()
    strict = row > col
    tables = decay_tables(sc_ref, lo_ref, lx_ref, row, col)
    ks = in_order(sc_ref, ko_ref[...].astype(F32), kx_ref[...].astype(F32))
    scales = [unit(k) for k in ks]
    kns = [(k * scale).astype(BF16) for k, scale in zip(ks, scales)]
    cols, rates, withins, leavings = [], [], [], []
    for n, (sub, block) in enumerate(UNITS):
        cum_t, cum, beta = tables[block]
        h = first_head(sc_ref) + sub
        cols.append(column(cum, h))
        rates.append(column(beta, h))
        withins.append(decay_within(cols[n], as_row(cum_t, h), strict) * (-rates[n]))
    for sub in range(2):
        last = l_ref[sub]
        fade = jnp.exp(cols[2 * sub + 1][T - 1:, :])
        leavings.append((gs_ref[sub].astype(F32) + fade * last.astype(F32)
                         - dot1(last, a_ref[2 * sub + 1], NT)).astype(BF16))
        leavings.append(last)
    fades = [jnp.exp(c[T - 1:, :] - c) for c in cols]
    dus = [du_ref[n] + fades[n] * dot1(kns[block], leavings[n], NT)
           for n, (sub, block) in enumerate(UNITS)]
    dxs = [dot1(t_ref[n], dus[n], TN) for n in range(4)]
    dx_bs = [dx.astype(BF16) for dx in dxs]
    d_inters = [dot1(dx_bs[n], u_ref[n], NT) * withins[n] for n in range(4)]
    dkns = []
    for n, (sub, block) in enumerate(UNITS):
        state = s_ref[sub] if block == 0 else ss_ref[sub]
        dkns.append(dot1(d_inters[n] + d_inters[n].T, kns[block])
                    + fades[n] * dot1(u_ref[n], leavings[n])
                    - (rates[n] * jnp.exp(cols[n])) * dot1(dx_bs[n], state))
    results = []
    for block in range(2):
        k, scale = ks[block], scales[block]
        dkn = dkn_ref[block] + dkns[block] + dkns[2 + block]
        results.append(
            scale * (dkn - k * (scale * scale) * jnp.sum(k * dkn, axis=-1, keepdims=True)))
    own, other = in_order(sc_ref, *results)
    dk_ref[...] = own.astype(BF16)
    dkx_ref[...] = other.astype(BF16)
    for sub in range(2):
        lanes = slice(sub * DV, (sub + 1) * DV)
        f, s = 2 * sub, 2 * sub + 1
        own, other = in_order(sc_ref, rates[f] * dxs[f], rates[s] * dxs[s])
        dv_ref[:, lanes] = own.astype(BF16)
        dvx_ref[:, lanes] = other.astype(BF16)


HEADS = VALUE_HEADS // 2
KEYS = HK // 2
PARAMS = pltpu.CompilerParams(vmem_limit_bytes=64 << 20)


def shape(dims, dtype=BF16):
    return jax.ShapeDtypeStruct(dims, dtype)


def block(dims, place):
    return pl.BlockSpec(dims, place)


OWN_KEY = block((T, DK), lambda i, sc: (0, KEYS * sc[0] + i))
OTHER_KEY = block((T, DK), lambda i, sc: (0, i))
OWN_VALUE = block((T, 2 * DV), lambda i, sc: (0, KEYS * sc[0] + i))
OTHER_VALUE = block((T, 2 * DV), lambda i, sc: (0, i))
PACKED_VALUE = block((T, 2 * DV), lambda i, sc: (0, KEYS // 2 + i))
TABLE = block((2 * VALUE_HEADS, T), lambda i, sc: (0, 0))
UNIT = block((4, T, DK), lambda i, sc: (i, 0, 0))
PAIR = block((2, T, DK), lambda i, sc: (i, 0, 0))
SLICE = block((T, 4 * DV), lambda i, sc: (0, 0))
UNIT_SHAPE, PAIR_SHAPE = (2 * HEADS, T, DK), (HEADS, T, DK)


def cost(gflops):
    return pl.CostEstimate(flops=int(gflops * 1e9), bytes_accessed=4 << 20, transcendentals=0)


def per_key(kernel, name, gflops, in_specs, out_specs, out_shape):
    return pl.pallas_call(
        kernel,
        grid_spec=pltpu.PrefetchScalarGridSpec(
            num_scalar_prefetch=1, grid=(KEYS,), in_specs=in_specs, out_specs=out_specs),
        out_shape=out_shape,
        compiler_params=PARAMS,
        cost_estimate=cost(gflops),
        name=name,
    )


ROWS = DK + HALF + TAIL
write_local = per_key(
    write_kernel, "write_local", 18,
    [OWN_KEY, OWN_VALUE, TABLE, OTHER_KEY, PACKED_VALUE, TABLE],
    [block((4, ROWS, DK), lambda i, sc: (i, 0, 0)), UNIT, UNIT, UNIT, UNIT, PAIR],
    [shape((2 * HEADS, ROWS, DK)), shape(UNIT_SHAPE), shape(UNIT_SHAPE), shape(UNIT_SHAPE),
     shape(UNIT_SHAPE), shape(PAIR_SHAPE)])
read_local = per_key(
    read_kernel, "read_local", 6,
    [OWN_KEY, OWN_KEY, TABLE, OTHER_KEY, OTHER_KEY, TABLE, UNIT, UNIT],
    [UNIT] * 3,
    [shape(UNIT_SHAPE)] * 3)
gate_local = per_key(
    gate_kernel, "gate_local", 7,
    [PAIR, OWN_VALUE, TABLE, PACKED_VALUE, TABLE, OTHER_VALUE, OTHER_VALUE, UNIT, PAIR]
    + [UNIT] * 4,
    [SLICE] * 4 + [OTHER_VALUE, OTHER_VALUE, OWN_VALUE, OTHER_VALUE, UNIT, UNIT]
    + [PAIR] * 3,
    [shape((T, 4 * DV))] * 4 + [shape((T, HEADS * DV))] * 2
    + [shape((T, VALUE_HEADS * DV)),
     shape((T, HEADS * DV)), shape(UNIT_SHAPE), shape(UNIT_SHAPE), shape(PAIR_SHAPE),
     shape(PAIR_SHAPE), shape(PAIR_SHAPE)])
BLOCK_KEY = block((2, T, DK), lambda i, sc: (0, 0, i))
early_local = per_key(
    early_kernel, "early_local", 7,
    [OWN_KEY, OWN_KEY, TABLE, OTHER_KEY, OTHER_KEY, TABLE, UNIT, UNIT, UNIT, PAIR, PAIR],
    [OWN_KEY, OTHER_KEY, BLOCK_KEY, UNIT],
    [shape((T, HK * DK)), shape((T, KEYS * DK)), shape((2, T, KEYS * DK), F32),
     shape(UNIT_SHAPE)])
late_local = per_key(
    late_kernel, "late_local", 9,
    [OWN_KEY, TABLE, OTHER_KEY, TABLE, UNIT, UNIT, UNIT, PAIR, PAIR, PAIR, PAIR, BLOCK_KEY, UNIT],
    [OWN_KEY, OWN_VALUE, OTHER_KEY, OTHER_VALUE],
    [shape((T, HK * DK)), shape((T, VALUE_HEADS * DV)), shape((T, KEYS * DK)),
     shape((T, HEADS * DV))])


def chain_up_kernel(count, ab_ref, s_ref):
    def step(i, state):
        s_ref[i] = state.astype(BF16)
        tail = ab_ref[i, DK + HALF:, :].astype(F32)
        decay = jnp.exp(jnp.sum(tail, axis=0, keepdims=True))
        high, low = split(state)
        moved = dot1(jnp.concatenate([high, low], axis=0), ab_ref[i, 0:DK, :])
        written = ab_ref[i, DK:DK + HALF, :].astype(F32)
        return decay * state - (moved[:HALF] + moved[HALF:]) + written

    lax.fori_loop(0, count, step, jnp.zeros((HALF, DK), F32), unroll=True)


def chain_down_kernel(count, ab_ref, g_ref, l_ref):
    def step(j, state):
        i = count - 1 - j
        l_ref[i] = state.astype(BF16)
        tail = ab_ref[i, DK + HALF:, :].astype(F32)
        decay = jnp.exp(jnp.sum(tail, axis=0, keepdims=True))
        high, low = split(state)
        moved = dot1(jnp.concatenate([high, low], axis=0), ab_ref[i, 0:DK, :], NT)
        return decay * state - (moved[:HALF] + moved[HALF:]) + g_ref[i].astype(F32)

    lax.fori_loop(0, count, step, jnp.zeros((HALF, DK), F32), unroll=True)


def chain(kernel, count, *args):
    return pl.pallas_call(
        functools.partial(kernel, count),
        out_shape=shape((count, HALF, DK)),
        compiler_params=PARAMS,
        cost_estimate=cost(3),
        name="chain",
    )(*args)


def pack_kernel(sc_ref, lengths_ref, pairing_ref, ratio_ref, cot_ref, ld_ref, be_ref,
                q_ref, k_ref, v_ref, gate_ref,
                scaled_ref, kv_ref, qg_ref, table_ref):
    own = sc_ref[1]
    tokens = cot_ref.shape[0]
    start = sc_ref[2] * T + pl.program_id(0) * tokens
    weight = jnp.zeros((8, 128), F32)
    for pair in range(pairing_ref.shape[0] // 2):
        chosen, rejected = pairing_ref[2 * pair], pairing_ref[2 * pair + 1]
        ratio_c = jnp.full((8, 128), ratio_ref[chosen], F32)
        ratio_r = jnp.full((8, 128), ratio_ref[rejected], F32)
        up_c, up_r = jnp.exp(ratio_c), jnp.exp(ratio_r)
        margin = CHI_BETA * (up_c + ratio_c - up_r - ratio_r)
        pull = CHI_BETA / (1.0 + jnp.exp(margin))
        weight = weight + jnp.where(chosen == own, -pull * (up_c + 1.0), 0.0)
        weight = weight + jnp.where(rejected == own, pull * (up_r + 1.0), 0.0)
    position = start + lax.broadcasted_iota(jnp.int32, (tokens, 1), 0)
    live = (position < lengths_ref[own]).astype(F32)
    factor = weight[0:1, 0:1] * live
    scaled_ref[...] = (cot_ref[...].astype(F32) * factor).astype(BF16)
    keys = KEYS * DK
    kv_ref[:, :keys] = k_ref[...]
    kv_ref[:, keys:] = v_ref[...]
    qg_ref[:, :keys] = q_ref[...]
    qg_ref[:, keys:] = gate_ref[...]
    table_ref[:VALUE_HEADS] = ld_ref[...]
    table_ref[VALUE_HEADS:] = be_ref[...]


def pack_local(sc, lengths, pairing, ratio, cot, ld, be, q, k, v, gate):
    scalars = pl.BlockSpec(memory_space=pltpu.SMEM)
    whole = lambda dims: block(dims, lambda i, sc: (0, 0))
    some = T // 2
    rows = lambda dims: block((some,) + dims[1:], lambda i, sc: (i, 0))
    half = lambda width: block((some, width), lambda i, sc: (i, 1 - sc[0]))
    keys, values = KEYS * DK, HEADS * DV
    packed = (T, keys + values)
    table = (2 * VALUE_HEADS, T)
    return pl.pallas_call(
        pack_kernel,
        grid_spec=pltpu.PrefetchScalarGridSpec(
            num_scalar_prefetch=1,
            grid=(T // some,),
            in_specs=[scalars] * 3 + [rows(cot.shape), whole(ld.shape), whole(be.shape),
                                      half(keys), half(keys), half(values), half(values)],
            out_specs=[rows(cot.shape), rows(packed), rows(packed), whole(table)],
        ),
        out_shape=[shape(cot.shape), shape(packed), shape(packed), shape(table, F32)],
        compiler_params=PARAMS,
        cost_estimate=cost(1),
        name="pack_local",
    )(sc, lengths, pairing, ratio, cot, ld, be, q, k, v, gate)


def turn(sc_ref):
    core, me = sc_ref[0], sc_ref[1]
    return (2 * (me % 2) + core) ^ me


def back_kernel(sc_ref, own_ref, other_ref, *refs):
    bo_ref, bx_ref = refs[8:]
    scaled = jnp.concatenate([own_ref[...], other_ref[...]], axis=0)
    first = pl.program_id(0) < 2
    weight = jnp.concatenate(
        [jnp.where(first, refs[n][...], refs[4 + n][...]) for n in range(4)], axis=1)
    product = dot1(scaled, weight, NT).astype(BF16)
    bo_ref[...] = product[:T]
    bx_ref[...] = product[T:]


def back_local(sc, own, other, weights):
    features, columns = weights[0].shape
    width, part = features // 2, columns // 4
    tokens = block((T, columns), lambda i, sc: (0, 0))
    out = block((T, width), lambda i, sc: (0, 2 * ((i // 2) ^ (sc[1] % 2)) + i % 2))
    early = [block((width, part), lambda i, sc, n=n: (jnp.minimum(i, 1), n)) for n in range(4)]
    late = [block((width, part), lambda i, sc, n=n: (jnp.maximum(i - 2, 0), n)) for n in range(4)]
    return pl.pallas_call(
        back_kernel,
        grid_spec=pltpu.PrefetchScalarGridSpec(
            num_scalar_prefetch=1,
            grid=(4,),
            in_specs=[tokens, tokens] + early + late,
            out_specs=[out, out],
        ),
        out_shape=[shape((T, 2 * features))] * 2,
        compiler_params=PARAMS,
        cost_estimate=cost(3),
        name="back_local",
    )(sc, own, other, *[weights[0]] * 4, *[weights[1]] * 4)


def mixed_kernel(sc_ref, no_ref, nx_ref, *refs):
    own_ref, other_ref = refs[8:]
    features = 4 * refs[0].shape[0]
    odd = sc_ref[1] % 2
    first = pl.ds(pl.multiple_of(odd * features, features), features)
    second = pl.ds(pl.multiple_of((1 - odd) * features, features), features)
    weights = [jnp.concatenate([ref[...] for ref in refs[4 * n:4 * n + 4]], axis=0)
               for n in range(2)]
    product = (dot1(jnp.concatenate([no_ref[:, first], nx_ref[:, first]], axis=0), weights[0])
               + dot1(jnp.concatenate([no_ref[:, second], nx_ref[:, second]], axis=0), weights[1]))
    own_ref[...] = product[:T]
    other_ref[...] = product[T:].astype(BF16)


def mixed_local(sc, own, other, weights, width=512):
    features, columns = weights[0].shape
    tokens = block((T, 2 * features), lambda i, sc: (0, 0))
    rows = [block((features // 4, width), lambda i, sc, n=n: (n, i)) for n in range(4)]
    out = block((T, width), lambda i, sc: (0, i))
    return pl.pallas_call(
        mixed_kernel,
        grid_spec=pltpu.PrefetchScalarGridSpec(
            num_scalar_prefetch=1,
            grid=(columns // width,),
            in_specs=[tokens, tokens] + rows + rows,
            out_specs=[out, out],
        ),
        out_shape=[shape((T, columns), F32), shape((T, columns))],
        compiler_params=PARAMS,
        cost_estimate=cost(3),
        name="mixed_local",
    )(sc, own, other, *[weights[0]] * 4, *[weights[1]] * 4)


def weight_kernel(sc_ref, *refs):
    keep_ref, send_ref, rows_ref, part_ref, sems = refs[8:]
    for n in range(4):
        rows_ref[n ^ turn(sc_ref)] = refs[n][...]
    rows = rows_ref[...].reshape(4 * T, rows_ref.shape[2])
    chips, cores, height, columns = part_ref.shape
    width, some = columns // 4, chips // 2
    core = lax.axis_index("ctx") % 2
    copies = []
    for n in range(4):
        lanes = slice(n * width, (n + 1) * width)
        scaled = jnp.concatenate([ref[:, lanes] for ref in refs[4:8]], axis=0)
        part_ref[:, :, :, lanes] = dot1(rows, scaled, TN).astype(BF16).reshape(
            chips, cores, height, width)
        for m in range(2):
            group, lane = pl.ds(m * some, some), pl.ds(n * width, width)
            for to_ref, row in ((keep_ref, core), (send_ref, 1 - core)):
                copies.append(pltpu.make_async_copy(
                    part_ref.at[group, row, :, lane], to_ref.at[group, :, lane],
                    sems.at[len(copies)]))
                copies[-1].start()
    for copy in copies:
        copy.wait()


def weight_local(sc, rows, scaled):
    features, columns = rows[0].shape[1], scaled[0].shape[1]
    same = lambda part: block(part.shape, lambda i, sc: (0, 0))
    return pl.pallas_call(
        weight_kernel,
        grid_spec=pltpu.PrefetchScalarGridSpec(
            num_scalar_prefetch=1,
            grid=(1,),
            in_specs=[same(part) for part in rows + scaled],
            out_specs=[pl.BlockSpec(memory_space=pl.ANY)] * 2,
            scratch_shapes=[pltpu.VMEM((4, T, features), BF16),
                            pltpu.VMEM((features // 32, 2, 16, columns), BF16),
                            pltpu.SemaphoreType.DMA((16,))],
        ),
        out_shape=[shape((features // 32, 16, columns))] * 2,
        compiler_params=PARAMS,
        cost_estimate=cost(4),
        name="weight_local",
    )(sc, *rows, *scaled)


def join_kernel(*refs):
    for n in range(2):
        refs[4][4 * n:4 * n + 4] = (
            refs[n][...].astype(F32) + refs[2 + n][...].astype(F32)).astype(BF16)


def join(a, b):
    streams = [block((4,) + a.shape[1:], lambda i, n=n: (2 * i + n, 0, 0)) for n in range(2)]
    return pl.pallas_call(
        join_kernel,
        grid=(a.shape[0] // 8,),
        in_specs=streams * 2,
        out_specs=block((8,) + a.shape[1:], lambda i: (i, 0, 0)),
        out_shape=shape(a.shape),
        compiler_params=PARAMS,
        cost_estimate=cost(1),
        name="join",
    )(a, a, b, b)


def total_kernel(*refs):
    refs[-1][...] = functools.reduce(
        lambda a, b: a + b, [jnp.sum(ref[...].astype(F32), axis=0) for ref in refs[:-1]])


def total(parts, streams=8):
    count, rows, columns = parts.shape
    return pl.pallas_call(
        total_kernel,
        grid=(1,),
        in_specs=[block((count // streams, rows, columns), lambda i, n=n: (n, 0, 0))
                  for n in range(streams)],
        out_specs=block((rows, columns), lambda i: (0, 0)),
        out_shape=shape((rows, columns), F32),
        compiler_params=PARAMS,
        cost_estimate=cost(1),
        name="total",
    )(*[parts] * streams)


def fill_kernel(sc_ref, *refs):
    count = (len(refs) - 4) // 3
    owns, other_ref, mixed_ref = refs[:2], refs[2], refs[3 + 2 * count]
    for part_ref, out_ref in zip(refs[3 + count:3 + 2 * count], refs[4 + 2 * count:]):
        out_ref[...] = part_ref[...]
    width = owns[0].shape[1]
    for n in range(2):
        lanes = slice(n * width, (n + 1) * width)
        mixed_ref[:, lanes] = (owns[n][...] + other_ref[:, lanes].astype(F32)).astype(BF16)


def fill(sc, mixed, wholes, parts):
    count, steps = len(wholes), 2
    columns = mixed[1].shape[1]
    some = lambda part: block((T, part.shape[1] // steps), lambda i, sc: (0, i))
    return pl.pallas_call(
        fill_kernel,
        grid_spec=pltpu.PrefetchScalarGridSpec(
            num_scalar_prefetch=1,
            grid=(steps,),
            in_specs=[block((T, columns // 4), lambda i, sc, n=n: (0, 2 * i + n))
                      for n in range(2)]
            + [some(mixed[1])] + [pl.BlockSpec(memory_space=pl.ANY)] * count
            + [some(part) for part in parts],
            out_specs=[some(mixed[1])]
            + [block((T, part.shape[1] // steps), lambda i, sc: (0, steps * (1 - sc[0]) + i))
               for part in parts],
        ),
        out_shape=[shape(mixed[1].shape)] + [shape(whole.shape) for whole in wholes],
        input_output_aliases={4 + n: 1 + n for n in range(count)},
        compiler_params=PARAMS,
        cost_estimate=cost(1),
        name="fill",
    )(sc, mixed[0], *mixed, *wholes, *parts)


def exchange(x):
    count = lax.axis_size("ctx")
    groups = [list(range(core, count, 2)) for core in range(2)]
    return lax.all_to_all(x, "ctx", split_axis=0, concat_axis=0, tiled=True,
                          axis_index_groups=groups)


def cross(x, axis, distance):
    count = lax.axis_size(axis)
    return lax.ppermute(x, axis, [(i, i ^ distance) for i in range(count)])


def sibling(x):
    return cross(x, "ctx", 1)


def tie(*values):
    return lax.optimization_barrier(values)


def place_of(z, chip, core, chips):
    return (z * chips + chip) * 2 + core


def feature_round(x, n, seqs):
    chips = lax.axis_size("ctx") // 2
    pairs = [(place_of(z, chip, core, chips),
              place_of(2 * core + (z ^ n) // 2, chip, (z ^ n) % 2, chips))
             for z in range(seqs) for chip in range(chips) for core in range(2)]
    return lax.ppermute(x, ("fsdp", "ctx"), pairs)


def weight_round(x, n, seqs):
    chips = lax.axis_size("ctx") // 2
    pairs = [(place_of(2 * core + (z ^ n) % 2, chip, 1 - z // 2, chips),
              place_of(z, chip, core, chips))
             for z in range(seqs) for chip in range(chips) for core in range(2)]
    return lax.ppermute(x, ("fsdp", "ctx"), pairs)


def body(query_vectors, key_vectors, value_vectors, output_gate, log_decay, write_rate,
         out_weight, cotangent, lengths, pairing, log_ratio):
    q, k, v, gate = query_vectors[0], key_vectors[0], value_vectors[0], output_gate[0]
    spot = lax.axis_index("ctx")
    core, chips = spot % 2, lax.axis_size("ctx") // 2
    me = lax.axis_index("fsdp")
    seqs = lax.axis_size("fsdp")
    sc = jnp.stack([core, me, spot])

    scaled, kv, qg, table = pack_local(
        sc, lengths, pairing, log_ratio, cotangent[0], log_decay[0].T, write_rate[0].T,
        q, k, v, gate)
    with jax.named_scope("swap_heads"):
        kv_x, table_x, qg_x, scaled_x = sibling(kv), sibling(table), sibling(qg), sibling(scaled)
    with jax.named_scope("out_weight"):
        heads_weight = [weight_round(out_weight, n, seqs) for n in range(2)]
    ab, t, u0, kg, a, b = write_local(sc, k, v, table, kv_x, kv_x, table_x)
    with jax.named_scope("every_scaled"):
        own_scaled = tie(ab, scaled)[1]
        every_scaled = [scaled] + [cross(own_scaled, "fsdp", s) for s in range(1, seqs)]
    ab = exchange(ab)
    p, r, io = read_local(sc, q, k, table, qg_x, kv_x, table_x, u0, kg)
    ab, p, r, io = tie(ab, p, r, io)
    states = chain(chain_up_kernel, chips, ab)
    entering = exchange(states).reshape(PAIR_SHAPE)
    with jax.named_scope("back_grad"):
        bg = back_local(sc, tie(states, scaled)[1], scaled_x, heads_weight)
    *rows, normed, normed_x, gate_grad, gate_grad_x, d_out, u, second, g, gs = gate_local(
        sc, entering, gate, table, qg_x, table_x, *bg, a, b, io, u0, kg, r)
    g = exchange(g.reshape(2 * HEADS, HALF, DK))
    with jax.named_scope("every_normed"):
        rows = [feature_round(rows[n], n, seqs) for n in range(seqs)]
    dq, dq_x, dkn, du = early_local(sc, q, k, table, qg_x, kv_x, table_x, p, u, d_out,
                                    entering, second)
    with jax.named_scope("weight_grad"):
        keep, send = weight_local(sc, rows, every_scaled)
    g, dq, dq_x, dkn, du, send = tie(g, dq, dq_x, dkn, du, send)
    leaving = exchange(chain(chain_down_kernel, chips, ab, g)).reshape(PAIR_SHAPE)
    with jax.named_scope("weight_grad"):
        leaving, terms = tie(leaving, join(keep, sibling(send)))
        weight_grad = total(exchange(terms))
    with jax.named_scope("swap_back"):
        others = [sibling(gate_grad_x), sibling(dq_x)]
    dk, dv, dk_x, dv_x = late_local(sc, k, table, kv_x, table_x, t, u, a, entering, second,
                                    leaving, gs, dkn, du)
    with jax.named_scope("mixed_out"):
        mixed, mixed_x = mixed_local(sc, normed, normed_x, heads_weight)
        mixed_x = sibling(mixed_x)
    with jax.named_scope("swap_back"):
        mixed, gate_grad, dq, dk, dv = fill(
            sc, [mixed, mixed_x], [gate_grad, dq, dk, dv], others + [sibling(dk_x), sibling(dv_x)])
    return mixed[None], dq[None], dk[None], dv[None], gate_grad[None], weight_grad


def solution(mesh):
    tokens = P("fsdp", "ctx", None)
    return jax.shard_map(
        body,
        mesh=mesh,
        in_specs=(tokens,) * 6 + (P("fsdp", None), tokens, P(), P(), P()),
        out_specs=(tokens,) * 5 + (P(("fsdp", "ctx"), None),),
        check_vma=False,
    )
```

```python
import functools

import jax
import jax.numpy as jnp
from jax import lax
from jax.experimental import pallas as pl
from jax.experimental.pallas import tpu as pltpu
from jax.sharding import PartitionSpec as P

VALUE_HEADS = 16
HK = 8
DK = 128
DV = 128
T = 128
HALF = 64
TAIL = 16
CHI_BETA = 0.5
NORM_EPS = 1e-06
F32 = jnp.float32
BF16 = jnp.bfloat16

NN = (((1,), (0,)), ((), ()))
NT = (((1,), (1,)), ((), ()))
TN = (((0,), (0,)), ((), ()))


def dot1(a, b, dims=NN):
    return lax.dot_general(a.astype(BF16), b.astype(BF16), dims, preferred_element_type=F32)


def split(a):
    high = a.astype(BF16)
    return high, (a - high.astype(F32)).astype(BF16)


def dot3(a, b, dims=NN):
    a_high, a_low = split(a)
    b_high, b_low = split(b)
    return dot1(a_high, b_high, dims) + (dot1(a_low, b_high, dims) + dot1(a_high, b_low, dims))


def grid_index():
    row = lax.broadcasted_iota(jnp.int32, (T, T), 0)
    col = lax.broadcasted_iota(jnp.int32, (T, T), 1)
    return row, col


def unit(x):
    return lax.rsqrt(jnp.sum(x * x, axis=-1, keepdims=True) + NORM_EPS)


def dot_exact_left(a, b):
    first = a.astype(BF16)
    rest = a - first.astype(F32)
    second = rest.astype(BF16)
    third = (rest - second.astype(F32)).astype(BF16)
    return dot1(first, b) + (dot1(second, b) + dot1(third, b))


def in_order(sc_ref, own, other):
    is_first = sc_ref[0] == 0
    return jnp.where(is_first, own, other), jnp.where(is_first, other, own)


def decay_tables(sc_ref, lo_ref, ro_ref, lx_ref, rx_ref, row, col):
    upper = (row <= col).astype(BF16)
    tables = []
    for decay, rate in zip(in_order(sc_ref, lo_ref[...], lx_ref[...]),
                           in_order(sc_ref, ro_ref[...], rx_ref[...])):
        cum_t = dot_exact_left(decay, upper)
        tables.append((cum_t, cum_t.T, rate.T))
    return tables


def column(table, head):
    lane = lax.broadcasted_iota(jnp.int32, table.shape, 1)
    return jnp.sum(jnp.where(lane == head, table, 0.0), axis=1, keepdims=True)


def as_row(table_t, head):
    sub = lax.broadcasted_iota(jnp.int32, table_t.shape, 0)
    return jnp.sum(jnp.where(sub == head, table_t, 0.0), axis=0, keepdims=True)


def decay_within(cum_col, cum_row, mask):
    return jnp.where(mask, jnp.exp(jnp.where(mask, cum_col - cum_row, 0.0)), 0.0)


def stripes(x, size, first):
    return jnp.concatenate(
        [x[start:start + size] for start in range(first * size, T, 2 * size)], axis=0)


def weave(even, odd, size):
    parts = []
    for start in range(0, T // 2, size):
        parts += [even[start:start + size], odd[start:start + size]]
    return jnp.concatenate(parts, axis=0)


def invert(couplings, row, col):
    eye = (row == col).astype(F32)
    pairs = (row >> 1) == (col >> 1)
    inverses = [eye - jnp.where(pairs, c, 0.0) for c in couplings]
    for level in range(1, 3):
        mask = ((row >> (level + 1)) == (col >> (level + 1))) & ((row >> level) != (col >> level))
        offs = [jnp.where(mask, c, 0.0).astype(BF16) for c in couplings]
        low = [i.astype(BF16) for i in inverses]
        inner = [dot1(o, i) for o, i in zip(offs, low)]
        inverses = [x - dot1(i, n) for x, i, n in zip(inverses, low, inner)]
    for level in range(3, 7):
        size = 1 << level
        mask = (stripes(row, size, 1) >> level) == (stripes(col, size, 1) >> level) + 1
        zeros = jnp.zeros((T // 2, T), F32)
        odds = [stripes(i, size, 1) for i in inverses]
        inner = [dot1(jnp.where(mask, stripes(c, size, 1), 0.0), i)
                 for c, i in zip(couplings, inverses)]
        odds = [o - dot1(o, weave(zeros, n, size)) for o, n in zip(odds, inner)]
        inverses = [weave(stripes(i, size, 0), o, size) for i, o in zip(inverses, odds)]
    return inverses


def total_rows(total):
    wide = jnp.broadcast_to(total, (TAIL, DK))
    high, low = split(wide)
    low2 = (wide - high.astype(F32) - low.astype(F32)).astype(BF16)
    sub_row = lax.broadcasted_iota(jnp.int32, (TAIL, DK), 0)
    tail = jnp.where(sub_row == 0, high.astype(F32),
                     jnp.where(sub_row == 1, low.astype(F32),
                               jnp.where(sub_row == 2, low2.astype(F32), 0.0)))
    return tail.astype(BF16)


def units(keys):
    return [(sub, block, 2 * (sub // 2) + block) for sub in range(2 * keys) for block in range(2)]


def first_head(sc_ref, keys):
    return (VALUE_HEADS // 2) * sc_ref[0] + 2 * keys * pl.program_id(0)


def per_head(sc_ref, keys, own_ref, other_ref):
    found = []
    for key in range(keys):
        lanes = slice(key * DK, (key + 1) * DK)
        found += in_order(sc_ref, own_ref[:, lanes].astype(F32), other_ref[:, lanes].astype(F32))
    return found


def write_kernel(keys, sc_ref, ko_ref, vo_ref, lo_ref, ro_ref, kx_ref, vx_ref, lx_ref, rx_ref,
                 ab_ref, t_ref, u0_ref, kg_ref, a_ref, b_ref):
    row, col = grid_index()
    causal, strict = row >= col, row > col
    tables = decay_tables(sc_ref, lo_ref, ro_ref, lx_ref, rx_ref, row, col)
    ks = per_head(sc_ref, keys, ko_ref, kx_ref)
    vs = in_order(sc_ref, vo_ref[...].astype(F32), vx_ref[...].astype(F32))
    kns = [k * unit(k) for k in ks]
    kks = [dot3(kn, kn, NT) for kn in kns]
    cols, rates, couplings = [], [], []
    for sub, block, kb in units(keys):
        cum_t, cum, beta = tables[block]
        h = first_head(sc_ref, keys) + sub
        cum_col, rate = column(cum, h), column(beta, h)
        within = decay_within(cum_col, as_row(cum_t, h), causal)
        couplings.append(jnp.where(strict, kks[kb] * within, 0.0) * rate)
        cols.append(cum_col)
        rates.append(rate)
    inverses = [i.astype(BF16) for i in invert(couplings, row, col)]
    u0s, kgs, transits, writtens, totals = [], [], [], [], []
    for n, (sub, block, kb) in enumerate(units(keys)):
        u0s.append(dot1(inverses[n], rates[n] * vs[block][:, sub * DV:(sub + 1) * DV]))
        kgs.append(dot1(inverses[n], (rates[n] * jnp.exp(cols[n])) * kns[kb]).astype(BF16))
    for n, (sub, block, kb) in enumerate(units(keys)):
        total = cols[n][T - 1:, :]
        carried = (jnp.exp(total - cols[n]) * kns[kb]).astype(BF16)
        transits.append(dot1(kgs[n], carried, TN))
        writtens.append(dot1(u0s[n], carried, TN))
        totals.append(total)
        t_ref[n] = inverses[n]
        u0_ref[n] = u0s[n].astype(BF16)
        kg_ref[n] = kgs[n]
        a_ref[n] = transits[n].astype(BF16)
    for sub in range(2 * keys):
        f, s = 2 * sub, 2 * sub + 1
        e_f, e_s = jnp.exp(totals[f]), jnp.exp(totals[s])
        stacked = jnp.concatenate([transits[f], writtens[f]], axis=0)
        moved = dot3(stacked, transits[s])
        transit = (e_f * transits[s] + e_s * transits[f] - moved[:DK]).astype(BF16)
        written = (e_s * writtens[f] - moved[DK:] + writtens[s]).astype(BF16)
        b_ref[sub] = writtens[f].astype(BF16)
        tail = total_rows(totals[f] + totals[s])
        for half in range(2):
            slot = 2 * sub + half
            ab_ref[slot, 0:DK, :] = transit
            ab_ref[slot, DK:DK + HALF, :] = written[half * HALF:(half + 1) * HALF]
            ab_ref[slot, DK + HALF:, :] = tail


def read_kernel(keys, sc_ref, qo_ref, ko_ref, lo_ref, ro_ref, qx_ref, kx_ref, lx_ref, rx_ref, u0_ref, kg_ref,
                p_ref, r_ref, io_ref):
    row, col = grid_index()
    causal = row >= col
    tables = decay_tables(sc_ref, lo_ref, ro_ref, lx_ref, rx_ref, row, col)
    qs = per_head(sc_ref, keys, qo_ref, qx_ref)
    ks = per_head(sc_ref, keys, ko_ref, kx_ref)
    qns = [q * unit(q) * DK ** (-0.5) for q in qs]
    qks = [dot3(qn, k * unit(k), NT) for qn, k in zip(qns, ks)]
    cols, scores = [], []
    for sub, block, kb in units(keys):
        cum_t, cum, _ = tables[block]
        h = first_head(sc_ref, keys) + sub
        cum_col = column(cum, h)
        cols.append(cum_col)
        scores.append((qks[kb] * decay_within(cum_col, as_row(cum_t, h), causal)).astype(BF16))
    for n, (sub, block, kb) in enumerate(units(keys)):
        p_ref[n] = scores[n]
        io_ref[n] = dot1(scores[n], u0_ref[n]).astype(BF16)
        r_ref[n] = (jnp.exp(cols[n]) * qns[kb] - dot1(scores[n], kg_ref[n])).astype(BF16)


def gate_kernel(keys, sc_ref, s_ref, go_ref, lo_ref, ro_ref, gx_ref, lx_ref, rx_ref, bo_ref, bx_ref,
                a_ref, b_ref, io_ref, u0_ref, kg_ref, r_ref, p_ref, qo_ref, ko_ref, qx_ref, kx_ref,
                n0_ref, n1_ref, n2_ref, n3_ref, no_ref, nx_ref, gg_ref, ggx_ref,
                u_ref, ss_ref, g_ref, gs_ref, dq_ref, dqx_ref, dk_ref, du_ref):
    gates = in_order(sc_ref, go_ref[...].astype(F32), gx_ref[...].astype(F32))
    me, step = sc_ref[1], pl.program_id(0)
    steps = KEYS // (2 * keys)
    bgs = in_order(sc_ref, bo_ref[...].astype(F32), bx_ref[...].astype(F32))
    row, col = grid_index()
    causal = row >= col
    tables = decay_tables(sc_ref, lo_ref, ro_ref, lx_ref, rx_ref, row, col)
    qs = per_head(sc_ref, keys, qo_ref, qx_ref)
    ks = per_head(sc_ref, keys, ko_ref, kx_ref)
    q_scales = [unit(q) for q in qs]
    qns = [(q * scale * DK ** (-0.5)).astype(BF16) for q, scale in zip(qs, q_scales)]
    kns = [(k * unit(k)).astype(BF16) for k in ks]
    cols = [column(tables[block][1], first_head(sc_ref, keys) + sub) for sub, block, kb in units(keys)]
    states, fades = [], []
    for sub in range(2 * keys):
        state = s_ref[sub]
        fade = jnp.exp(cols[2 * sub][T - 1:, :])
        second = (fade * state.astype(F32) - dot1(state, a_ref[2 * sub])
                  + b_ref[sub].astype(F32)).astype(BF16)
        ss_ref[sub] = second
        states += [state, second]
        fades.append(fade)
    outs = [io_ref[n] + dot1(r_ref[n], states[n], NT) for n in range(4 * keys)]
    normeds, gate_grads, d_outs, us = [], [], [], []
    for n, (sub, block, kb) in enumerate(units(keys)):
        lanes = slice(sub * DV, (sub + 1) * DV)
        us.append((u0_ref[n] - dot1(kg_ref[n], states[n], NT)).astype(BF16))
        u_ref[n] = us[n]
        out = outs[n]
        scale = lax.rsqrt(jnp.mean(out * out, axis=-1, keepdims=True) + NORM_EPS)
        z = out * scale
        gate = gates[block][:, lanes]
        sig = 1.0 / (1.0 + jnp.exp(-gate))
        sil = gate * sig
        normeds.append(z * sil)
        bg = bgs[block][:, lanes]
        gate_grads.append(bg * z * (sig + sil * (1.0 - sig)))
        dz = bg * sil
        d_out = scale * (dz - z * jnp.mean(dz * z, axis=-1, keepdims=True))
        d_outs.append(d_out.astype(BF16))
    grads = [dot1(d_outs[n], r_ref[n], TN) for n in range(4 * keys)]
    for sub in range(2 * keys):
        lanes = slice(sub * DV, (sub + 1) * DV)
        f, s = 2 * sub, 2 * sub + 1
        g_ref[sub] = (grads[f] + fades[sub] * grads[s]
                      - dot1(grads[s], a_ref[f], NT)).astype(BF16)
        gs_ref[sub] = grads[s].astype(BF16)
        own, other = in_order(sc_ref, gate_grads[f], gate_grads[s])
        gg_ref[:, lanes] = own.astype(BF16)
        ggx_ref[:, lanes] = other.astype(BF16)
    width = 2 * keys * DV
    columns = pl.ds(pl.multiple_of((step % steps) * width, width), width)
    blocks = [jnp.concatenate(normeds[tau::2], axis=1).astype(BF16) for tau in range(2)]
    no_ref[...], nx_ref[...] = in_order(sc_ref, *blocks)
    for n, ref in enumerate((n0_ref, n1_ref, n2_ref, n3_ref)):
        code = me ^ n

        @pl.when(code // 2 == step // steps)
        def _():
            ref[:, columns] = jnp.where(code % 2 == 0, blocks[0], blocks[1])
    raw = [dot1(d_outs[n], us[n], NT) for n in range(4 * keys)]
    d_scores = []
    for n, (sub, block, kb) in enumerate(units(keys)):
        cum_t, h = tables[block][0], first_head(sc_ref, keys) + sub
        d_scores.append((raw[n] * decay_within(cols[n], as_row(cum_t, h), causal)).astype(BF16))
    dqs, dkns = [], []
    for n, (sub, block, kb) in enumerate(units(keys)):
        du_ref[n] = dot1(p_ref[n], d_outs[n], TN).astype(BF16)
        dqs.append(jnp.exp(cols[n]) * dot1(d_outs[n], states[n]) + dot1(d_scores[n], kns[kb]))
        dkns.append(dot1(d_scores[n], qns[kb], TN))
    for key in range(keys):
        lanes = slice(key * DK, (key + 1) * DK)
        results = []
        for block in range(2):
            n, kb = 4 * key + block, 2 * key + block
            q, scale, dqn = qs[kb], q_scales[kb], dqs[n] + dqs[n + 2]
            dk_ref[block, :, lanes] = dkns[n] + dkns[n + 2]
            results.append(scale * DK ** (-0.5) * (
                dqn - q * (scale * scale) * jnp.sum(q * dqn, axis=-1, keepdims=True)))
        own, other = in_order(sc_ref, *results)
        dq_ref[:, lanes] = own.astype(BF16)
        dqx_ref[:, lanes] = other.astype(BF16)


def late_kernel(keys, sc_ref, ko_ref, lo_ref, ro_ref, kx_ref, lx_ref, rx_ref, t_ref, u_ref, a_ref, s_ref, ss_ref,
                l_ref, gs_ref, dkn_ref, du_ref,
                dk_ref, dv_ref, dkx_ref, dvx_ref):
    row, col = grid_index()
    strict = row > col
    tables = decay_tables(sc_ref, lo_ref, ro_ref, lx_ref, rx_ref, row, col)
    ks = per_head(sc_ref, keys, ko_ref, kx_ref)
    scales = [unit(k) for k in ks]
    kns = [(k * scale).astype(BF16) for k, scale in zip(ks, scales)]
    cols, rates, withins, leavings = [], [], [], []
    for n, (sub, block, kb) in enumerate(units(keys)):
        cum_t, cum, beta = tables[block]
        h = first_head(sc_ref, keys) + sub
        cols.append(column(cum, h))
        rates.append(column(beta, h))
        withins.append(decay_within(cols[n], as_row(cum_t, h), strict) * (-rates[n]))
    for sub in range(2 * keys):
        last = l_ref[sub]
        fade = jnp.exp(cols[2 * sub + 1][T - 1:, :])
        leavings.append((gs_ref[sub].astype(F32) + fade * last.astype(F32)
                         - dot1(last, a_ref[2 * sub + 1], NT)).astype(BF16))
        leavings.append(last)
    fades = [jnp.exp(c[T - 1:, :] - c) for c in cols]
    dus = [du_ref[n] + fades[n] * dot1(kns[kb], leavings[n], NT)
           for n, (sub, block, kb) in enumerate(units(keys))]
    dxs = [dot1(t_ref[n], dus[n], TN) for n in range(4 * keys)]
    dx_bs = [dx.astype(BF16) for dx in dxs]
    d_inters = [dot1(dx_bs[n], u_ref[n], NT) * withins[n] for n in range(4 * keys)]
    dkns = []
    for n, (sub, block, kb) in enumerate(units(keys)):
        state = s_ref[sub] if block == 0 else ss_ref[sub]
        dkns.append(dot1(d_inters[n] + d_inters[n].T, kns[kb])
                    + fades[n] * dot1(u_ref[n], leavings[n])
                    - (rates[n] * jnp.exp(cols[n])) * dot1(dx_bs[n], state))
    for key in range(keys):
        lanes = slice(key * DK, (key + 1) * DK)
        results = []
        for block in range(2):
            n, kb = 4 * key + block, 2 * key + block
            k, scale = ks[kb], scales[kb]
            dkn = dkn_ref[block, :, lanes] + dkns[n] + dkns[n + 2]
            results.append(
                scale * (dkn - k * (scale * scale) * jnp.sum(k * dkn, axis=-1, keepdims=True)))
        own, other = in_order(sc_ref, *results)
        dk_ref[:, lanes] = own.astype(BF16)
        dkx_ref[:, lanes] = other.astype(BF16)
    for sub in range(2 * keys):
        lanes = slice(sub * DV, (sub + 1) * DV)
        f, s = 2 * sub, 2 * sub + 1
        own, other = in_order(sc_ref, rates[f] * dxs[f], rates[s] * dxs[s])
        dv_ref[:, lanes] = own.astype(BF16)
        dvx_ref[:, lanes] = other.astype(BF16)


HEADS = VALUE_HEADS // 2
KEYS = HK // 2
PARAMS = pltpu.CompilerParams(vmem_limit_bytes=64 << 20)


def shape(dims, dtype=BF16):
    return jax.ShapeDtypeStruct(dims, dtype)


def block(dims, place):
    return pl.BlockSpec(dims, place)


def own(keys, width):
    return block((T, keys * width), lambda i, sc: (0, KEYS // keys * sc[0] + i))


def other(keys, width):
    return block((T, keys * width), lambda i, sc: (0, i))


def leading(count):
    return block((count, T, DK), lambda i, sc: (i, 0, 0))


TABLE = block((VALUE_HEADS, T), lambda i, sc: (0, 0))
SLICE = block((T, 4 * DV), lambda i, sc: (0, 0))
UNIT_SHAPE, PAIR_SHAPE = (2 * HEADS, T, DK), (HEADS, T, DK)


def cost(gflops):
    return pl.CostEstimate(flops=int(gflops * 1e9), bytes_accessed=1 << 16, transcendentals=0)


def per_key(kernel, name, gflops, keys, in_specs, out_specs, out_shape):
    return pl.pallas_call(
        functools.partial(kernel, keys),
        grid_spec=pltpu.PrefetchScalarGridSpec(
            num_scalar_prefetch=1, grid=(KEYS // keys,), in_specs=in_specs, out_specs=out_specs),
        out_shape=out_shape,
        compiler_params=PARAMS,
        cost_estimate=cost(gflops),
        name=name,
    )


ROWS = DK + HALF + TAIL
write_local = per_key(
    write_kernel, "write_local", 18, 2,
    [own(2, DK), own(2, 2 * DV), TABLE, TABLE, own(2, DK), own(2, 2 * DV), TABLE, TABLE],
    [block((8, ROWS, DK), lambda i, sc: (i, 0, 0)), leading(8), leading(8), leading(8), leading(8), leading(4)],
    [shape((2 * HEADS, ROWS, DK)), shape(UNIT_SHAPE), shape(UNIT_SHAPE), shape(UNIT_SHAPE),
     shape(UNIT_SHAPE), shape(PAIR_SHAPE)])
read_local = per_key(
    read_kernel, "read_local", 0.01, 2,
    [own(2, DK), own(2, DK), TABLE, TABLE, own(2, DK), own(2, DK), TABLE, TABLE, leading(8), leading(8)],
    [leading(8)] * 3,
    [shape(UNIT_SHAPE)] * 3)
gate_local = per_key(
    gate_kernel, "gate_local", 12, 2,
    [leading(4), own(2, 2 * DV), TABLE, TABLE, own(2, 2 * DV), TABLE, TABLE, other(2, 2 * DV), other(2, 2 * DV), leading(8), leading(4)]
    + [leading(8)] * 5 + [own(2, DK)] * 4,
    [SLICE] * 4 + [other(2, 2 * DV), other(2, 2 * DV), own(2, 2 * DV), other(2, 2 * DV), leading(8)] + [leading(4)] * 3
    + [own(2, DK), other(2, DK), block((2, T, 2 * DK), lambda i, sc: (0, 0, i)), leading(8)],
    [shape((T, 4 * DV))] * 4 + [shape((T, HEADS * DV))] * 2
    + [shape((T, VALUE_HEADS * DV)), shape((T, HEADS * DV)), shape(UNIT_SHAPE)]
    + [shape(PAIR_SHAPE)] * 3
    + [shape((T, HK * DK)), shape((T, KEYS * DK)), shape((2, T, KEYS * DK), F32),
       shape(UNIT_SHAPE)])
late_local = per_key(
    late_kernel, "late_local", 50, 2,
    [own(2, DK), TABLE, TABLE, own(2, DK), TABLE, TABLE, leading(8), leading(8), leading(8), leading(4), leading(4), leading(4), leading(4), block((2, T, 2 * DK), lambda i, sc: (0, 0, i)), leading(8)],
    [own(2, DK), own(2, 2 * DV), other(2, DK), other(2, 2 * DV)],
    [shape((T, HK * DK)), shape((T, VALUE_HEADS * DV)), shape((T, KEYS * DK)),
     shape((T, HEADS * DV))])


STREAMS = 4


def chain_step(ab_ref, i, state, dims, added):
    tail = ab_ref[i, DK + HALF:, :].astype(F32)
    decay = jnp.exp(jnp.sum(tail, axis=0, keepdims=True))
    high, low = split(state)
    moved = dot1(jnp.concatenate([high, low], axis=0), ab_ref[i, 0:DK, :], dims)
    return decay * state - (moved[:HALF] + moved[HALF:]) + added.astype(F32)


def chain_up_kernel(*refs):
    count = refs[0].shape[0]
    state = jnp.zeros((HALF, DK), F32)
    for i in range(STREAMS * count):
        refs[-1][i] = state.astype(BF16)
        ab_ref, n = refs[i // count], i % count
        state = chain_step(ab_ref, n, state, NN, ab_ref[n, DK:DK + HALF, :])


def chain_down_kernel(*refs):
    count = refs[0].shape[0]
    state = jnp.zeros((HALF, DK), F32)
    for i in reversed(range(STREAMS * count)):
        refs[-1][i] = state.astype(BF16)
        state = chain_step(refs[i // count], i % count, state, NT, refs[STREAMS][i])


def chain(kernel, ab, *args):
    count = ab.shape[0]
    streams = [block((count // STREAMS,) + ab.shape[1:], lambda i, n=n: (n, 0, 0))
               for n in range(STREAMS)]
    whole = block((count, HALF, DK), lambda i: (0, 0, 0))
    return pl.pallas_call(
        kernel,
        grid=(1,),
        in_specs=streams + [whole] * len(args),
        out_specs=whole,
        out_shape=shape((count, HALF, DK)),
        compiler_params=PARAMS,
        cost_estimate=cost(0.01),
        name="chain",
    )(*[ab] * STREAMS, *args)


def scale_kernel(sc_ref, lengths_ref, pairing_ref, ratio_ref, cot_ref, scaled_ref):
    own = sc_ref[1]
    tokens = cot_ref.shape[0]
    start = sc_ref[2] * T + pl.program_id(0) * tokens
    weight = jnp.zeros((8, 128), F32)
    for pair in range(pairing_ref.shape[0] // 2):
        chosen, rejected = pairing_ref[2 * pair], pairing_ref[2 * pair + 1]
        ratio_c = jnp.full((8, 128), ratio_ref[chosen], F32)
        ratio_r = jnp.full((8, 128), ratio_ref[rejected], F32)
        up_c, up_r = jnp.exp(ratio_c), jnp.exp(ratio_r)
        margin = CHI_BETA * (up_c + ratio_c - up_r - ratio_r)
        pull = CHI_BETA / (1.0 + jnp.exp(margin))
        weight = weight + jnp.where(chosen == own, -pull * (up_c + 1.0), 0.0)
        weight = weight + jnp.where(rejected == own, pull * (up_r + 1.0), 0.0)
    position = start + lax.broadcasted_iota(jnp.int32, (tokens, 1), 0)
    live = (position < lengths_ref[own]).astype(F32)
    factor = weight[0:1, 0:1] * live
    scaled_ref[...] = (cot_ref[...].astype(F32) * factor).astype(BF16)


def scale_local(sc, lengths, pairing, ratio, cot, steps=2):
    scalars = pl.BlockSpec(memory_space=pltpu.SMEM)
    rows = block((T // steps,) + cot.shape[1:], lambda i, sc: (i, 0))
    return pl.pallas_call(
        scale_kernel,
        grid_spec=pltpu.PrefetchScalarGridSpec(
            num_scalar_prefetch=1,
            grid=(steps,),
            in_specs=[scalars] * 3 + [rows],
            out_specs=rows,
        ),
        out_shape=shape(cot.shape),
        compiler_params=PARAMS,
        cost_estimate=cost(0.01),
        name="scale_local",
    )(sc, lengths, pairing, ratio, cot)


def turn(sc_ref):
    core, me = sc_ref[0], sc_ref[1]
    return (2 * (me % 2) + core) ^ me


def back_kernel(sc_ref, own_ref, other_ref, *refs):
    bo_ref, bx_ref = refs[8:]
    scaled = jnp.concatenate([own_ref[...], other_ref[...]], axis=0)
    first = pl.program_id(0) < 2
    weight = jnp.concatenate(
        [jnp.where(first, refs[n][...], refs[4 + n][...]) for n in range(4)], axis=1)
    product = dot1(scaled, weight, NT).astype(BF16)
    bo_ref[...] = product[:T]
    bx_ref[...] = product[T:]


def back_local(sc, own, other, weights):
    features, columns = weights[0].shape
    width, part = features // 2, columns // 4
    tokens = block((T, columns), lambda i, sc: (0, 0))
    out = block((T, width), lambda i, sc: (0, 2 * ((i // 2) ^ (sc[1] % 2)) + i % 2))
    early = [block((width, part), lambda i, sc, n=n: (jnp.minimum(i, 1), n)) for n in range(4)]
    late = [block((width, part), lambda i, sc, n=n: (jnp.maximum(i - 2, 0), n)) for n in range(4)]
    return pl.pallas_call(
        back_kernel,
        grid_spec=pltpu.PrefetchScalarGridSpec(
            num_scalar_prefetch=1,
            grid=(4,),
            in_specs=[tokens, tokens] + early + late,
            out_specs=[out, out],
        ),
        out_shape=[shape((T, 2 * features))] * 2,
        compiler_params=PARAMS,
        cost_estimate=cost(0.01),
        name="back_local",
    )(sc, own, other, *[weights[0]] * 4, *[weights[1]] * 4)


def mixed_kernel(sc_ref, no_ref, nx_ref, *refs):
    own_ref, other_ref = refs[8:]
    features = 4 * refs[0].shape[0]
    odd = sc_ref[1] % 2
    first = pl.ds(pl.multiple_of(odd * features, features), features)
    second = pl.ds(pl.multiple_of((1 - odd) * features, features), features)
    weights = [jnp.concatenate([ref[...] for ref in refs[4 * n:4 * n + 4]], axis=0)
               for n in range(2)]
    product = (dot1(jnp.concatenate([no_ref[:, first], nx_ref[:, first]], axis=0), weights[0])
               + dot1(jnp.concatenate([no_ref[:, second], nx_ref[:, second]], axis=0), weights[1]))
    own_ref[...] = product[:T]
    other_ref[...] = product[T:].astype(BF16)


def mixed_local(sc, own, other, weights, width=512):
    features, columns = weights[0].shape
    tokens = block((T, 2 * features), lambda i, sc: (0, 0))
    rows = [block((features // 4, width), lambda i, sc, n=n: (n, i)) for n in range(4)]
    out = block((T, width), lambda i, sc: (0, i))
    return pl.pallas_call(
        mixed_kernel,
        grid_spec=pltpu.PrefetchScalarGridSpec(
            num_scalar_prefetch=1,
            grid=(columns // width,),
            in_specs=[tokens, tokens] + rows + rows,
            out_specs=[out, out],
        ),
        out_shape=[shape((T, columns), F32), shape((T, columns))],
        compiler_params=PARAMS,
        cost_estimate=cost(0.01),
        name="mixed_local",
    )(sc, own, other, *[weights[0]] * 4, *[weights[1]] * 4)


def weight_kernel(sc_ref, *refs):
    keep_ref, send_ref, rows_ref, part_ref, sems = refs[8:]
    for n in range(4):
        rows_ref[n ^ turn(sc_ref)] = refs[n][...]
    rows = rows_ref[...].reshape(4 * T, rows_ref.shape[2])
    chips, cores, height, columns = part_ref.shape
    width, some = columns // 4, chips // 2
    core = lax.axis_index("ctx") % 2
    copies = []
    for n in range(4):
        lanes = slice(n * width, (n + 1) * width)
        scaled = jnp.concatenate([ref[:, lanes] for ref in refs[4:8]], axis=0)
        part_ref[:, :, :, lanes] = dot1(rows, scaled, TN).astype(BF16).reshape(
            chips, cores, height, width)
        for m in range(2):
            group, lane = pl.ds(m * some, some), pl.ds(n * width, width)
            for to_ref, row in ((keep_ref, core), (send_ref, 1 - core)):
                copies.append(pltpu.make_async_copy(
                    part_ref.at[group, row, :, lane], to_ref.at[group, :, lane],
                    sems.at[len(copies)]))
                copies[-1].start()
    for copy in copies:
        copy.wait()


def weight_local(sc, rows, scaled):
    features, columns = rows[0].shape[1], scaled[0].shape[1]
    same = lambda part: block(part.shape, lambda i, sc: (0, 0))
    return pl.pallas_call(
        weight_kernel,
        grid_spec=pltpu.PrefetchScalarGridSpec(
            num_scalar_prefetch=1,
            grid=(1,),
            in_specs=[same(part) for part in rows + scaled],
            out_specs=[pl.BlockSpec(memory_space=pl.ANY)] * 2,
            scratch_shapes=[pltpu.VMEM((4, T, features), BF16),
                            pltpu.VMEM((features // 32, 2, 16, columns), BF16),
                            pltpu.SemaphoreType.DMA((16,))],
        ),
        out_shape=[shape((features // 32, 16, columns))] * 2,
        compiler_params=PARAMS,
        cost_estimate=cost(4),
        name="weight_local",
    )(sc, *rows, *scaled)


def join_kernel(*refs):
    for n in range(2):
        refs[4][4 * n:4 * n + 4] = (
            refs[n][...].astype(F32) + refs[2 + n][...].astype(F32)).astype(BF16)


def join(a, b):
    streams = [block((4,) + a.shape[1:], lambda i, n=n: (2 * i + n, 0, 0)) for n in range(2)]
    return pl.pallas_call(
        join_kernel,
        grid=(a.shape[0] // 8,),
        in_specs=streams * 2,
        out_specs=block((8,) + a.shape[1:], lambda i: (i, 0, 0)),
        out_shape=shape(a.shape),
        compiler_params=PARAMS,
        cost_estimate=cost(0.01),
        name="join",
    )(a, a, b, b)


def total_kernel(*refs):
    refs[-1][...] = functools.reduce(
        lambda a, b: a + b, [jnp.sum(ref[...].astype(F32), axis=0) for ref in refs[:-1]])


def total(parts, streams=8):
    count, rows, columns = parts.shape
    return pl.pallas_call(
        total_kernel,
        grid=(1,),
        in_specs=[block((count // streams, rows, columns), lambda i, n=n: (n, 0, 0))
                  for n in range(streams)],
        out_specs=block((rows, columns), lambda i: (0, 0)),
        out_shape=shape((rows, columns), F32),
        compiler_params=PARAMS,
        cost_estimate=cost(0.01),
        name="total",
    )(*[parts] * streams)


def fill_kernel(sc_ref, *refs):
    count = len(refs) // 3
    for part_ref, out_ref in zip(refs[count:2 * count], refs[2 * count:]):
        out_ref[...] = part_ref[...]


def fill(sc, wholes, parts):
    count = len(wholes)
    return pl.pallas_call(
        fill_kernel,
        grid_spec=pltpu.PrefetchScalarGridSpec(
            num_scalar_prefetch=1,
            grid=(1,),
            in_specs=[pl.BlockSpec(memory_space=pl.ANY)] * count
            + [block(part.shape, lambda i, sc: (0, 0)) for part in parts],
            out_specs=[block(part.shape, lambda i, sc: (0, 1 - sc[0])) for part in parts],
        ),
        out_shape=[shape(whole.shape) for whole in wholes],
        input_output_aliases={1 + n: n for n in range(count)},
        compiler_params=PARAMS,
        cost_estimate=cost(0.01),
        name="fill",
    )(sc, *wholes, *parts)


def sum_kernel(a_ref, b_ref, c_ref, out_ref):
    width = a_ref.shape[1]
    out_ref[:, :width] = (a_ref[...] + c_ref[:, :width].astype(F32)).astype(BF16)
    out_ref[:, width:] = (b_ref[...] + c_ref[:, width:].astype(F32)).astype(BF16)


def sum_shares(own, other, steps=2):
    rows, columns = own.shape
    part = columns // (2 * steps)
    halves = [block((rows, part), lambda i, n=n: (0, 2 * i + n)) for n in range(2)]
    whole = block((rows, 2 * part), lambda i: (0, i))
    return pl.pallas_call(
        sum_kernel,
        grid=(steps,),
        in_specs=halves + [whole],
        out_specs=whole,
        out_shape=shape(own.shape),
        compiler_params=PARAMS,
        cost_estimate=cost(0.01),
        name="sum_shares",
    )(own, own, other)


def exchange(x):
    count = lax.axis_size("ctx")
    groups = [list(range(core, count, 2)) for core in range(2)]
    return lax.all_to_all(x, "ctx", split_axis=0, concat_axis=0, tiled=True,
                          axis_index_groups=groups)


def cross(x, axis, distance):
    count = lax.axis_size(axis)
    return lax.ppermute(x, axis, [(i, i ^ distance) for i in range(count)])


def sibling(x):
    return cross(x, "ctx", 1)


def tie(*values):
    return lax.optimization_barrier(values)


def place_of(z, chip, core, chips):
    return (z * chips + chip) * 2 + core


def feature_round(x, n, seqs):
    chips = lax.axis_size("ctx") // 2
    pairs = [(place_of(z, chip, core, chips),
              place_of(2 * core + (z ^ n) // 2, chip, (z ^ n) % 2, chips))
             for z in range(seqs) for chip in range(chips) for core in range(2)]
    return lax.ppermute(x, ("fsdp", "ctx"), pairs)


def weight_round(x, n, seqs):
    chips = lax.axis_size("ctx") // 2
    pairs = [(place_of(2 * core + (z ^ n) % 2, chip, 1 - z // 2, chips),
              place_of(z, chip, core, chips))
             for z in range(seqs) for chip in range(chips) for core in range(2)]
    return lax.ppermute(x, ("fsdp", "ctx"), pairs)


def body(query_vectors, key_vectors, value_vectors, output_gate, log_decay, write_rate,
         out_weight, cotangent, lengths, pairing, log_ratio):
    q, k, v, gate = query_vectors[0], key_vectors[0], value_vectors[0], output_gate[0]
    spot = lax.axis_index("ctx")
    core, chips = spot % 2, lax.axis_size("ctx") // 2
    me = lax.axis_index("fsdp")
    seqs = lax.axis_size("fsdp")
    sc = jnp.stack([core, me, spot])

    with jax.named_scope("swap_heads"):
        ld, be = log_decay[0].T, write_rate[0].T
        k_x, v_x, ld_x, be_x = (sibling(part) for part in (k, v, ld, be))
    with jax.named_scope("out_weight"):
        heads_weight = [weight_round(out_weight, n, seqs) for n in range(2)]
    ab, t, u0, kg, a, b = write_local(sc, k, v, ld, be, k_x, v_x, ld_x, be_x)
    with jax.named_scope("every_scaled"):
        cotangent = tie(ab, cotangent)[1]
        scaled = scale_local(sc, lengths, pairing, log_ratio, cotangent[0])
    with jax.named_scope("swap_heads"):
        q_x, gate_x, scaled_x = sibling(q), sibling(gate), sibling(scaled)
    ab = exchange(ab)
    p, r, io = read_local(sc, q, k, ld, be, q_x, k_x, ld_x, be_x, u0, kg)
    ab, p, r, io, scaled = tie(ab, p, r, io, scaled)
    states = chain(chain_up_kernel, ab)
    entering = exchange(states).reshape(PAIR_SHAPE)
    with jax.named_scope("back_grad"):
        bg = back_local(sc, scaled, scaled_x, heads_weight)
    with jax.named_scope("every_scaled"):
        own_scaled = tie(heads_weight[0], heads_weight[1], scaled)[2]
        every_scaled = [scaled] + [cross(own_scaled, "fsdp", s) for s in range(1, seqs)]
    *rows, normed, normed_x, gate_grad, gate_grad_x, u, second, g, gs, dq, dq_x, dkn, du = gate_local(
        sc, entering, gate, ld, be, gate_x, ld_x, be_x, *bg, a, b, io, u0, kg, r, p, q, k, q_x, k_x)
    g = exchange(g.reshape(2 * HEADS, HALF, DK))
    with jax.named_scope("every_normed"):
        rows = [feature_round(rows[n], n, seqs) for n in range(seqs)]
    g, *every_scaled = tie(g, *every_scaled)
    states = chain(chain_down_kernel, ab, g)
    leaving = exchange(states).reshape(PAIR_SHAPE)
    with jax.named_scope("weight_grad"):
        rows = list(tie(states, *rows)[1:])
        keep, send = weight_local(sc, rows, every_scaled)
        send = sibling(send)
    with jax.named_scope("swap_back"):
        others = [sibling(gate_grad_x), sibling(dq_x)]
    dk, dv, dk_x, dv_x = late_local(sc, k, ld, be, k_x, ld_x, be_x, t, u, a, entering, second,
                                    leaving, gs, dkn, du)
    with jax.named_scope("weight_grad"):
        dk, keep = tie(dk, keep)
        weight_grad = total(exchange(join(keep, send)))
    with jax.named_scope("mixed_out"):
        dk, normed, normed_x = tie(dk, normed, normed_x)
        mixed, mixed_x = mixed_local(sc, normed, normed_x, heads_weight)
    with jax.named_scope("swap_back"):
        gate_grad, dq, dk, dv = fill(
            sc, [gate_grad, dq, dk, dv], others + [sibling(dk_x), sibling(dv_x)])
    with jax.named_scope("mixed_out"):
        mixed = sum_shares(mixed, sibling(mixed_x))
    return mixed[None], dq[None], dk[None], dv[None], gate_grad[None], weight_grad


def solution(mesh):
    tokens = P("fsdp", "ctx", None)
    return jax.shard_map(
        body,
        mesh=mesh,
        in_specs=(tokens,) * 6 + (P("fsdp", None), tokens, P(), P(), P()),
        out_specs=(tokens,) * 5 + (P(("fsdp", "ctx"), None),),
        check_vma=False,
    )
```

```python
import functools

import jax
import jax.numpy as jnp
from jax import lax
from jax.experimental import pallas as pl
from jax.experimental.pallas import tpu as pltpu
from jax.sharding import PartitionSpec as P

VALUE_HEADS = 16
HK = 8
DK = 128
DV = 128
T = 128
HALF = 64
TAIL = 16
CHI_BETA = 0.5
NORM_EPS = 1e-06
F32 = jnp.float32
BF16 = jnp.bfloat16

NN = (((1,), (0,)), ((), ()))
NT = (((1,), (1,)), ((), ()))
TN = (((0,), (0,)), ((), ()))


def dot1(a, b, dims=NN):
    return lax.dot_general(a.astype(BF16), b.astype(BF16), dims, preferred_element_type=F32)


def split(a):
    high = a.astype(BF16)
    return high, (a - high.astype(F32)).astype(BF16)


def dot3(a, b, dims=NN):
    a_high, a_low = split(a)
    b_high, b_low = split(b)
    return dot1(a_high, b_high, dims) + (dot1(a_low, b_high, dims) + dot1(a_high, b_low, dims))


def grid_index():
    row = lax.broadcasted_iota(jnp.int32, (T, T), 0)
    col = lax.broadcasted_iota(jnp.int32, (T, T), 1)
    return row, col


def unit(x):
    return lax.rsqrt(jnp.sum(x * x, axis=-1, keepdims=True) + NORM_EPS)


def dot_exact_left(a, b):
    first = a.astype(BF16)
    rest = a - first.astype(F32)
    second = rest.astype(BF16)
    third = (rest - second.astype(F32)).astype(BF16)
    return dot1(first, b) + (dot1(second, b) + dot1(third, b))


def in_order(sc_ref, own, other):
    is_first = sc_ref[0] == 0
    return jnp.where(is_first, own, other), jnp.where(is_first, other, own)


def decay_tables(sc_ref, lo_ref, ro_ref, lx_ref, rx_ref, row, col):
    upper = (row <= col).astype(BF16)
    tables = []
    for decay, rate in zip(in_order(sc_ref, lo_ref[...], lx_ref[...]),
                           in_order(sc_ref, ro_ref[...], rx_ref[...])):
        cum_t = dot_exact_left(decay, upper)
        tables.append((cum_t, cum_t.T, rate.T))
    return tables


def column(table, head):
    lane = lax.broadcasted_iota(jnp.int32, table.shape, 1)
    return jnp.sum(jnp.where(lane == head, table, 0.0), axis=1, keepdims=True)


def as_row(table_t, head):
    sub = lax.broadcasted_iota(jnp.int32, table_t.shape, 0)
    return jnp.sum(jnp.where(sub == head, table_t, 0.0), axis=0, keepdims=True)


def decay_within(cum_col, cum_row, mask):
    return jnp.where(mask, jnp.exp(jnp.where(mask, cum_col - cum_row, 0.0)), 0.0)


def stripes(x, size, first):
    return jnp.concatenate(
        [x[start:start + size] for start in range(first * size, T, 2 * size)], axis=0)


def weave(even, odd, size):
    parts = []
    for start in range(0, T // 2, size):
        parts += [even[start:start + size], odd[start:start + size]]
    return jnp.concatenate(parts, axis=0)


def invert(couplings, row, col):
    eye = (row == col).astype(F32)
    pairs = (row >> 1) == (col >> 1)
    inverses = [eye - jnp.where(pairs, c, 0.0) for c in couplings]
    for level in range(1, 3):
        mask = ((row >> (level + 1)) == (col >> (level + 1))) & ((row >> level) != (col >> level))
        offs = [jnp.where(mask, c, 0.0).astype(BF16) for c in couplings]
        low = [i.astype(BF16) for i in inverses]
        inner = [dot1(o, i) for o, i in zip(offs, low)]
        inverses = [x - dot1(i, n) for x, i, n in zip(inverses, low, inner)]
    for level in range(3, 7):
        size = 1 << level
        mask = (stripes(row, size, 1) >> level) == (stripes(col, size, 1) >> level) + 1
        zeros = jnp.zeros((T // 2, T), F32)
        odds = [stripes(i, size, 1) for i in inverses]
        inner = [dot1(jnp.where(mask, stripes(c, size, 1), 0.0), i)
                 for c, i in zip(couplings, inverses)]
        odds = [o - dot1(o, weave(zeros, n, size)) for o, n in zip(odds, inner)]
        inverses = [weave(stripes(i, size, 0), o, size) for i, o in zip(inverses, odds)]
    return inverses


def total_rows(total):
    wide = jnp.broadcast_to(total, (TAIL, DK))
    high, low = split(wide)
    low2 = (wide - high.astype(F32) - low.astype(F32)).astype(BF16)
    sub_row = lax.broadcasted_iota(jnp.int32, (TAIL, DK), 0)
    tail = jnp.where(sub_row == 0, high.astype(F32),
                     jnp.where(sub_row == 1, low.astype(F32),
                               jnp.where(sub_row == 2, low2.astype(F32), 0.0)))
    return tail.astype(BF16)


def units(keys):
    return [(sub, block, 2 * (sub // 2) + block) for sub in range(2 * keys) for block in range(2)]


def first_head(sc_ref, keys):
    return (VALUE_HEADS // 2) * sc_ref[0] + 2 * keys * pl.program_id(0)


def per_head(sc_ref, keys, own_ref, other_ref):
    found = []
    for key in range(keys):
        lanes = slice(key * DK, (key + 1) * DK)
        found += in_order(sc_ref, own_ref[:, lanes].astype(F32), other_ref[:, lanes].astype(F32))
    return found


def write_kernel(keys, sc_ref, ko_ref, vo_ref, lo_ref, ro_ref, kx_ref, vx_ref, lx_ref, rx_ref,
                 ab_ref, t_ref, u0_ref, kg_ref, a_ref, b_ref):
    row, col = grid_index()
    causal, strict = row >= col, row > col
    tables = decay_tables(sc_ref, lo_ref, ro_ref, lx_ref, rx_ref, row, col)
    ks = per_head(sc_ref, keys, ko_ref, kx_ref)
    vs = in_order(sc_ref, vo_ref[...].astype(F32), vx_ref[...].astype(F32))
    kns = [k * unit(k) for k in ks]
    kks = [dot3(kn, kn, NT) for kn in kns]
    cols, rates, couplings = [], [], []
    for sub, block, kb in units(keys):
        cum_t, cum, beta = tables[block]
        h = first_head(sc_ref, keys) + sub
        cum_col, rate = column(cum, h), column(beta, h)
        within = decay_within(cum_col, as_row(cum_t, h), causal)
        couplings.append(jnp.where(strict, kks[kb] * within, 0.0) * rate)
        cols.append(cum_col)
        rates.append(rate)
    inverses = [i.astype(BF16) for i in invert(couplings, row, col)]
    u0s, kgs, transits, writtens, totals = [], [], [], [], []
    for n, (sub, block, kb) in enumerate(units(keys)):
        u0s.append(dot1(inverses[n], rates[n] * vs[block][:, sub * DV:(sub + 1) * DV]))
        kgs.append(dot1(inverses[n], (rates[n] * jnp.exp(cols[n])) * kns[kb]).astype(BF16))
    for n, (sub, block, kb) in enumerate(units(keys)):
        total = cols[n][T - 1:, :]
        carried = (jnp.exp(total - cols[n]) * kns[kb]).astype(BF16)
        transits.append(dot1(kgs[n], carried, TN))
        writtens.append(dot1(u0s[n], carried, TN))
        totals.append(total)
        t_ref[n] = inverses[n]
        u0_ref[n] = u0s[n].astype(BF16)
        kg_ref[n] = kgs[n]
        a_ref[n] = transits[n].astype(BF16)
    for sub in range(2 * keys):
        f, s = 2 * sub, 2 * sub + 1
        e_f, e_s = jnp.exp(totals[f]), jnp.exp(totals[s])
        stacked = jnp.concatenate([transits[f], writtens[f]], axis=0)
        moved = dot3(stacked, transits[s])
        transit = (e_f * transits[s] + e_s * transits[f] - moved[:DK]).astype(BF16)
        written = (e_s * writtens[f] - moved[DK:] + writtens[s]).astype(BF16)
        b_ref[sub] = writtens[f].astype(BF16)
        tail = total_rows(totals[f] + totals[s])
        for half in range(2):
            slot = 2 * sub + half
            ab_ref[slot, 0:DK, :] = transit
            ab_ref[slot, DK:DK + HALF, :] = written[half * HALF:(half + 1) * HALF]
            ab_ref[slot, DK + HALF:, :] = tail


def read_kernel(keys, sc_ref, qo_ref, ko_ref, lo_ref, ro_ref, qx_ref, kx_ref, lx_ref, rx_ref, u0_ref, kg_ref,
                p_ref, r_ref, io_ref):
    row, col = grid_index()
    causal = row >= col
    tables = decay_tables(sc_ref, lo_ref, ro_ref, lx_ref, rx_ref, row, col)
    qs = per_head(sc_ref, keys, qo_ref, qx_ref)
    ks = per_head(sc_ref, keys, ko_ref, kx_ref)
    qns = [q * unit(q) * DK ** (-0.5) for q in qs]
    qks = [dot3(qn, k * unit(k), NT) for qn, k in zip(qns, ks)]
    cols, scores = [], []
    for sub, block, kb in units(keys):
        cum_t, cum, _ = tables[block]
        h = first_head(sc_ref, keys) + sub
        cum_col = column(cum, h)
        cols.append(cum_col)
        scores.append((qks[kb] * decay_within(cum_col, as_row(cum_t, h), causal)).astype(BF16))
    for n, (sub, block, kb) in enumerate(units(keys)):
        p_ref[n] = scores[n]
        io_ref[n] = dot1(scores[n], u0_ref[n]).astype(BF16)
        r_ref[n] = (jnp.exp(cols[n]) * qns[kb] - dot1(scores[n], kg_ref[n])).astype(BF16)


def gate_kernel(keys, sc_ref, s_ref, go_ref, lo_ref, ro_ref, gx_ref, lx_ref, rx_ref, bo_ref, bx_ref,
                a_ref, b_ref, io_ref, u0_ref, kg_ref, r_ref, p_ref, qo_ref, ko_ref, qx_ref, kx_ref,
                n0_ref, n1_ref, n2_ref, n3_ref, no_ref, nx_ref, gg_ref, ggx_ref,
                u_ref, ss_ref, g_ref, gs_ref, dq_ref, dqx_ref, dk_ref, du_ref):
    gates = in_order(sc_ref, go_ref[...].astype(F32), gx_ref[...].astype(F32))
    me, step = sc_ref[1], pl.program_id(0)
    steps = KEYS // (2 * keys)
    bgs = in_order(sc_ref, bo_ref[...].astype(F32), bx_ref[...].astype(F32))
    row, col = grid_index()
    causal = row >= col
    tables = decay_tables(sc_ref, lo_ref, ro_ref, lx_ref, rx_ref, row, col)
    qs = per_head(sc_ref, keys, qo_ref, qx_ref)
    ks = per_head(sc_ref, keys, ko_ref, kx_ref)
    q_scales = [unit(q) for q in qs]
    qns = [(q * scale * DK ** (-0.5)).astype(BF16) for q, scale in zip(qs, q_scales)]
    kns = [(k * unit(k)).astype(BF16) for k in ks]
    cols = [column(tables[block][1], first_head(sc_ref, keys) + sub) for sub, block, kb in units(keys)]
    states, fades = [], []
    for sub in range(2 * keys):
        state = s_ref[sub]
        fade = jnp.exp(cols[2 * sub][T - 1:, :])
        second = (fade * state.astype(F32) - dot1(state, a_ref[2 * sub])
                  + b_ref[sub].astype(F32)).astype(BF16)
        ss_ref[sub] = second
        states += [state, second]
        fades.append(fade)
    outs = [io_ref[n] + dot1(r_ref[n], states[n], NT) for n in range(4 * keys)]
    normeds, gate_grads, d_outs, us = [], [], [], []
    for n, (sub, block, kb) in enumerate(units(keys)):
        lanes = slice(sub * DV, (sub + 1) * DV)
        us.append((u0_ref[n] - dot1(kg_ref[n], states[n], NT)).astype(BF16))
        u_ref[n] = us[n]
        out = outs[n]
        scale = lax.rsqrt(jnp.mean(out * out, axis=-1, keepdims=True) + NORM_EPS)
        z = out * scale
        gate = gates[block][:, lanes]
        sig = 1.0 / (1.0 + jnp.exp(-gate))
        sil = gate * sig
        normeds.append(z * sil)
        bg = bgs[block][:, lanes]
        gate_grads.append(bg * z * (sig + sil * (1.0 - sig)))
        dz = bg * sil
        d_out = scale * (dz - z * jnp.mean(dz * z, axis=-1, keepdims=True))
        d_outs.append(d_out.astype(BF16))
    grads = [dot1(d_outs[n], r_ref[n], TN) for n in range(4 * keys)]
    for sub in range(2 * keys):
        lanes = slice(sub * DV, (sub + 1) * DV)
        f, s = 2 * sub, 2 * sub + 1
        g_ref[sub] = (grads[f] + fades[sub] * grads[s]
                      - dot1(grads[s], a_ref[f], NT)).astype(BF16)
        gs_ref[sub] = grads[s].astype(BF16)
        own, other = in_order(sc_ref, gate_grads[f], gate_grads[s])
        gg_ref[:, lanes] = own.astype(BF16)
        ggx_ref[:, lanes] = other.astype(BF16)
    width = 2 * keys * DV
    columns = pl.ds(pl.multiple_of((step % steps) * width, width), width)
    blocks = [jnp.concatenate(normeds[tau::2], axis=1).astype(BF16) for tau in range(2)]
    no_ref[...], nx_ref[...] = in_order(sc_ref, *blocks)
    for n, ref in enumerate((n0_ref, n1_ref, n2_ref, n3_ref)):
        code = me ^ n

        @pl.when(code // 2 == step // steps)
        def _():
            ref[:, columns] = jnp.where(code % 2 == 0, blocks[0], blocks[1])
    raw = [dot1(d_outs[n], us[n], NT) for n in range(4 * keys)]
    d_scores = []
    for n, (sub, block, kb) in enumerate(units(keys)):
        cum_t, h = tables[block][0], first_head(sc_ref, keys) + sub
        d_scores.append((raw[n] * decay_within(cols[n], as_row(cum_t, h), causal)).astype(BF16))
    dqs, dkns = [], []
    for n, (sub, block, kb) in enumerate(units(keys)):
        du_ref[n] = dot1(p_ref[n], d_outs[n], TN).astype(BF16)
        dqs.append(jnp.exp(cols[n]) * dot1(d_outs[n], states[n]) + dot1(d_scores[n], kns[kb]))
        dkns.append(dot1(d_scores[n], qns[kb], TN))
    for key in range(keys):
        lanes = slice(key * DK, (key + 1) * DK)
        results = []
        for block in range(2):
            n, kb = 4 * key + block, 2 * key + block
            q, scale, dqn = qs[kb], q_scales[kb], dqs[n] + dqs[n + 2]
            dk_ref[block, :, lanes] = dkns[n] + dkns[n + 2]
            results.append(scale * DK ** (-0.5) * (
                dqn - q * (scale * scale) * jnp.sum(q * dqn, axis=-1, keepdims=True)))
        own, other = in_order(sc_ref, *results)
        dq_ref[:, lanes] = own.astype(BF16)
        dqx_ref[:, lanes] = other.astype(BF16)


def late_kernel(keys, sc_ref, ko_ref, lo_ref, ro_ref, kx_ref, lx_ref, rx_ref, t_ref, u_ref, a_ref, s_ref, ss_ref,
                l_ref, gs_ref, dkn_ref, du_ref,
                dk_ref, dv_ref, dkx_ref, dvx_ref):
    row, col = grid_index()
    strict = row > col
    tables = decay_tables(sc_ref, lo_ref, ro_ref, lx_ref, rx_ref, row, col)
    ks = per_head(sc_ref, keys, ko_ref, kx_ref)
    scales = [unit(k) for k in ks]
    kns = [(k * scale).astype(BF16) for k, scale in zip(ks, scales)]
    cols, rates, withins, leavings = [], [], [], []
    for n, (sub, block, kb) in enumerate(units(keys)):
        cum_t, cum, beta = tables[block]
        h = first_head(sc_ref, keys) + sub
        cols.append(column(cum, h))
        rates.append(column(beta, h))
        withins.append(decay_within(cols[n], as_row(cum_t, h), strict) * (-rates[n]))
    for sub in range(2 * keys):
        last = l_ref[sub]
        fade = jnp.exp(cols[2 * sub + 1][T - 1:, :])
        leavings.append((gs_ref[sub].astype(F32) + fade * last.astype(F32)
                         - dot1(last, a_ref[2 * sub + 1], NT)).astype(BF16))
        leavings.append(last)
    fades = [jnp.exp(c[T - 1:, :] - c) for c in cols]
    dus = [du_ref[n] + fades[n] * dot1(kns[kb], leavings[n], NT)
           for n, (sub, block, kb) in enumerate(units(keys))]
    dxs = [dot1(t_ref[n], dus[n], TN) for n in range(4 * keys)]
    dx_bs = [dx.astype(BF16) for dx in dxs]
    d_inters = [dot1(dx_bs[n], u_ref[n], NT) * withins[n] for n in range(4 * keys)]
    dkns = []
    for n, (sub, block, kb) in enumerate(units(keys)):
        state = s_ref[sub] if block == 0 else ss_ref[sub]
        dkns.append(dot1(d_inters[n] + d_inters[n].T, kns[kb])
                    + fades[n] * dot1(u_ref[n], leavings[n])
                    - (rates[n] * jnp.exp(cols[n])) * dot1(dx_bs[n], state))
    for key in range(keys):
        lanes = slice(key * DK, (key + 1) * DK)
        results = []
        for block in range(2):
            n, kb = 4 * key + block, 2 * key + block
            k, scale = ks[kb], scales[kb]
            dkn = dkn_ref[block, :, lanes] + dkns[n] + dkns[n + 2]
            results.append(
                scale * (dkn - k * (scale * scale) * jnp.sum(k * dkn, axis=-1, keepdims=True)))
        own, other = in_order(sc_ref, *results)
        dk_ref[:, lanes] = own.astype(BF16)
        dkx_ref[:, lanes] = other.astype(BF16)
    for sub in range(2 * keys):
        lanes = slice(sub * DV, (sub + 1) * DV)
        f, s = 2 * sub, 2 * sub + 1
        own, other = in_order(sc_ref, rates[f] * dxs[f], rates[s] * dxs[s])
        dv_ref[:, lanes] = own.astype(BF16)
        dvx_ref[:, lanes] = other.astype(BF16)


HEADS = VALUE_HEADS // 2
KEYS = HK // 2
PARAMS = pltpu.CompilerParams(vmem_limit_bytes=64 << 20)


def shape(dims, dtype=BF16):
    return jax.ShapeDtypeStruct(dims, dtype)


def block(dims, place):
    return pl.BlockSpec(dims, place)


def own(keys, width):
    return block((T, keys * width), lambda i, sc: (0, KEYS // keys * sc[0] + i))


def other(keys, width):
    return block((T, keys * width), lambda i, sc: (0, i))


def leading(count):
    return block((count, T, DK), lambda i, sc: (i, 0, 0))


TABLE = block((VALUE_HEADS, T), lambda i, sc: (0, 0))
SLICE = block((T, 4 * DV), lambda i, sc: (0, 0))
UNIT_SHAPE, PAIR_SHAPE = (2 * HEADS, T, DK), (HEADS, T, DK)


def cost(gflops):
    return pl.CostEstimate(flops=int(gflops * 1e9), bytes_accessed=1 << 16, transcendentals=0)


def per_key(kernel, name, gflops, keys, in_specs, out_specs, out_shape):
    return pl.pallas_call(
        functools.partial(kernel, keys),
        grid_spec=pltpu.PrefetchScalarGridSpec(
            num_scalar_prefetch=1, grid=(KEYS // keys,), in_specs=in_specs, out_specs=out_specs),
        out_shape=out_shape,
        compiler_params=PARAMS,
        cost_estimate=cost(gflops),
        name=name,
    )


ROWS = DK + HALF + TAIL
write_local = per_key(
    write_kernel, "write_local", 18, 2,
    [own(2, DK), own(2, 2 * DV), TABLE, TABLE, own(2, DK), own(2, 2 * DV), TABLE, TABLE],
    [block((8, ROWS, DK), lambda i, sc: (i, 0, 0)), leading(8), leading(8), leading(8), leading(8), leading(4)],
    [shape((2 * HEADS, ROWS, DK)), shape(UNIT_SHAPE), shape(UNIT_SHAPE), shape(UNIT_SHAPE),
     shape(UNIT_SHAPE), shape(PAIR_SHAPE)])
read_local = per_key(
    read_kernel, "read_local", 0.01, 2,
    [own(2, DK), own(2, DK), TABLE, TABLE, own(2, DK), own(2, DK), TABLE, TABLE, leading(8), leading(8)],
    [leading(8)] * 3,
    [shape(UNIT_SHAPE)] * 3)
gate_local = per_key(
    gate_kernel, "gate_local", 12, 2,
    [leading(4), own(2, 2 * DV), TABLE, TABLE, own(2, 2 * DV), TABLE, TABLE, other(2, 2 * DV), other(2, 2 * DV), leading(8), leading(4)]
    + [leading(8)] * 5 + [own(2, DK)] * 4,
    [SLICE] * 4 + [other(2, 2 * DV), other(2, 2 * DV), own(2, 2 * DV), other(2, 2 * DV), leading(8)] + [leading(4)] * 3
    + [own(2, DK), other(2, DK), block((2, T, 2 * DK), lambda i, sc: (0, 0, i)), leading(8)],
    [shape((T, 4 * DV))] * 4 + [shape((T, HEADS * DV))] * 2
    + [shape((T, VALUE_HEADS * DV)), shape((T, HEADS * DV)), shape(UNIT_SHAPE)]
    + [shape(PAIR_SHAPE)] * 3
    + [shape((T, HK * DK)), shape((T, KEYS * DK)), shape((2, T, KEYS * DK), F32),
       shape(UNIT_SHAPE)])
late_local = per_key(
    late_kernel, "late_local", 50, 2,
    [own(2, DK), TABLE, TABLE, own(2, DK), TABLE, TABLE, leading(8), leading(8), leading(8), leading(4), leading(4), leading(4), leading(4), block((2, T, 2 * DK), lambda i, sc: (0, 0, i)), leading(8)],
    [own(2, DK), own(2, 2 * DV), other(2, DK), other(2, 2 * DV)],
    [shape((T, HK * DK)), shape((T, VALUE_HEADS * DV)), shape((T, KEYS * DK)),
     shape((T, HEADS * DV))])


STREAMS = 4


def chain_step(ab_ref, i, state, dims, added):
    tail = ab_ref[i, DK + HALF:, :].astype(F32)
    decay = jnp.exp(jnp.sum(tail, axis=0, keepdims=True))
    high, low = split(state)
    moved = dot1(jnp.concatenate([high, low], axis=0), ab_ref[i, 0:DK, :], dims)
    return decay * state - (moved[:HALF] + moved[HALF:]) + added.astype(F32)


def chain_up_kernel(*refs):
    count = refs[0].shape[0]
    state = jnp.zeros((HALF, DK), F32)
    for i in range(STREAMS * count):
        refs[-1][i] = state.astype(BF16)
        ab_ref, n = refs[i // count], i % count
        state = chain_step(ab_ref, n, state, NN, ab_ref[n, DK:DK + HALF, :])


def chain_down_kernel(*refs):
    count = refs[0].shape[0]
    state = jnp.zeros((HALF, DK), F32)
    for i in reversed(range(STREAMS * count)):
        refs[-1][i] = state.astype(BF16)
        state = chain_step(refs[i // count], i % count, state, NT, refs[STREAMS][i])


def chain(kernel, ab, *args):
    count = ab.shape[0]
    streams = [block((count // STREAMS,) + ab.shape[1:], lambda i, n=n: (n, 0, 0))
               for n in range(STREAMS)]
    whole = block((count, HALF, DK), lambda i: (0, 0, 0))
    return pl.pallas_call(
        kernel,
        grid=(1,),
        in_specs=streams + [whole] * len(args),
        out_specs=whole,
        out_shape=shape((count, HALF, DK)),
        compiler_params=PARAMS,
        cost_estimate=cost(0.01),
        name="chain",
    )(*[ab] * STREAMS, *args)


def scale_kernel(sc_ref, lengths_ref, pairing_ref, ratio_ref, cot_ref, scaled_ref):
    own = sc_ref[1]
    tokens = cot_ref.shape[0]
    start = sc_ref[2] * T + pl.program_id(0) * tokens
    weight = jnp.zeros((8, 128), F32)
    for pair in range(pairing_ref.shape[0] // 2):
        chosen, rejected = pairing_ref[2 * pair], pairing_ref[2 * pair + 1]
        ratio_c = jnp.full((8, 128), ratio_ref[chosen], F32)
        ratio_r = jnp.full((8, 128), ratio_ref[rejected], F32)
        up_c, up_r = jnp.exp(ratio_c), jnp.exp(ratio_r)
        margin = CHI_BETA * (up_c + ratio_c - up_r - ratio_r)
        pull = CHI_BETA / (1.0 + jnp.exp(margin))
        weight = weight + jnp.where(chosen == own, -pull * (up_c + 1.0), 0.0)
        weight = weight + jnp.where(rejected == own, pull * (up_r + 1.0), 0.0)
    position = start + lax.broadcasted_iota(jnp.int32, (tokens, 1), 0)
    live = (position < lengths_ref[own]).astype(F32)
    factor = weight[0:1, 0:1] * live
    scaled_ref[...] = (cot_ref[...].astype(F32) * factor).astype(BF16)


def scale_local(sc, lengths, pairing, ratio, cot, steps=2):
    scalars = pl.BlockSpec(memory_space=pltpu.SMEM)
    rows = block((T // steps,) + cot.shape[1:], lambda i, sc: (i, 0))
    return pl.pallas_call(
        scale_kernel,
        grid_spec=pltpu.PrefetchScalarGridSpec(
            num_scalar_prefetch=1,
            grid=(steps,),
            in_specs=[scalars] * 3 + [rows],
            out_specs=rows,
        ),
        out_shape=shape(cot.shape),
        compiler_params=PARAMS,
        cost_estimate=cost(0.01),
        name="scale_local",
    )(sc, lengths, pairing, ratio, cot)


def turn(sc_ref):
    core, me = sc_ref[0], sc_ref[1]
    return (2 * (me % 2) + core) ^ me


def back_kernel(sc_ref, own_ref, other_ref, *refs):
    bo_ref, bx_ref = refs[8:]
    scaled = jnp.concatenate([own_ref[...], other_ref[...]], axis=0)
    first = pl.program_id(0) < 2
    weight = jnp.concatenate(
        [jnp.where(first, refs[n][...], refs[4 + n][...]) for n in range(4)], axis=1)
    product = dot1(scaled, weight, NT).astype(BF16)
    bo_ref[...] = product[:T]
    bx_ref[...] = product[T:]


def back_local(sc, own, other, weights):
    features, columns = weights[0].shape
    width, part = features // 2, columns // 4
    tokens = block((T, columns), lambda i, sc: (0, 0))
    out = block((T, width), lambda i, sc: (0, 2 * ((i // 2) ^ (sc[1] % 2)) + i % 2))
    early = [block((width, part), lambda i, sc, n=n: (jnp.minimum(i, 1), n)) for n in range(4)]
    late = [block((width, part), lambda i, sc, n=n: (jnp.maximum(i - 2, 0), n)) for n in range(4)]
    return pl.pallas_call(
        back_kernel,
        grid_spec=pltpu.PrefetchScalarGridSpec(
            num_scalar_prefetch=1,
            grid=(4,),
            in_specs=[tokens, tokens] + early + late,
            out_specs=[out, out],
        ),
        out_shape=[shape((T, 2 * features))] * 2,
        compiler_params=PARAMS,
        cost_estimate=cost(0.01),
        name="back_local",
    )(sc, own, other, *[weights[0]] * 4, *[weights[1]] * 4)


def mixed_kernel(sc_ref, no_ref, nx_ref, *refs):
    own_ref, other_ref = refs[8:]
    features = 4 * refs[0].shape[0]
    odd = sc_ref[1] % 2
    first = pl.ds(pl.multiple_of(odd * features, features), features)
    second = pl.ds(pl.multiple_of((1 - odd) * features, features), features)
    weights = [jnp.concatenate([ref[...] for ref in refs[4 * n:4 * n + 4]], axis=0)
               for n in range(2)]
    product = (dot1(jnp.concatenate([no_ref[:, first], nx_ref[:, first]], axis=0), weights[0])
               + dot1(jnp.concatenate([no_ref[:, second], nx_ref[:, second]], axis=0), weights[1]))
    own_ref[...] = product[:T]
    other_ref[...] = product[T:].astype(BF16)


def mixed_local(sc, own, other, weights, width=512):
    features, columns = weights[0].shape
    tokens = block((T, 2 * features), lambda i, sc: (0, 0))
    rows = [block((features // 4, width), lambda i, sc, n=n: (n, i)) for n in range(4)]
    out = block((T, width), lambda i, sc: (0, i))
    return pl.pallas_call(
        mixed_kernel,
        grid_spec=pltpu.PrefetchScalarGridSpec(
            num_scalar_prefetch=1,
            grid=(columns // width,),
            in_specs=[tokens, tokens] + rows + rows,
            out_specs=[out, out],
        ),
        out_shape=[shape((T, columns), F32), shape((T, columns))],
        compiler_params=PARAMS,
        cost_estimate=cost(0.01),
        name="mixed_local",
    )(sc, own, other, *[weights[0]] * 4, *[weights[1]] * 4)


def weight_kernel(sc_ref, *refs):
    keep_ref, send_ref, rows_ref, part_ref, sems = refs[8:]
    for n in range(4):
        rows_ref[n ^ turn(sc_ref)] = refs[n][...]
    rows = rows_ref[...].reshape(4 * T, rows_ref.shape[2])
    chips, cores, height, columns = part_ref.shape
    width, some = columns // 4, chips // 2
    core = lax.axis_index("ctx") % 2
    copies = []
    for n in range(4):
        lanes = slice(n * width, (n + 1) * width)
        scaled = jnp.concatenate([ref[:, lanes] for ref in refs[4:8]], axis=0)
        part_ref[:, :, :, lanes] = dot1(rows, scaled, TN).astype(BF16).reshape(
            chips, cores, height, width)
        for m in range(2):
            group, lane = pl.ds(m * some, some), pl.ds(n * width, width)
            for to_ref, row in ((keep_ref, core), (send_ref, 1 - core)):
                copies.append(pltpu.make_async_copy(
                    part_ref.at[group, row, :, lane], to_ref.at[group, :, lane],
                    sems.at[len(copies)]))
                copies[-1].start()
    for copy in copies:
        copy.wait()


def weight_local(sc, rows, scaled):
    features, columns = rows[0].shape[1], scaled[0].shape[1]
    same = lambda part: block(part.shape, lambda i, sc: (0, 0))
    return pl.pallas_call(
        weight_kernel,
        grid_spec=pltpu.PrefetchScalarGridSpec(
            num_scalar_prefetch=1,
            grid=(1,),
            in_specs=[same(part) for part in rows + scaled],
            out_specs=[pl.BlockSpec(memory_space=pl.ANY)] * 2,
            scratch_shapes=[pltpu.VMEM((4, T, features), BF16),
                            pltpu.VMEM((features // 32, 2, 16, columns), BF16),
                            pltpu.SemaphoreType.DMA((16,))],
        ),
        out_shape=[shape((features // 32, 16, columns))] * 2,
        compiler_params=PARAMS,
        cost_estimate=cost(4),
        name="weight_local",
    )(sc, *rows, *scaled)


def join_kernel(*refs):
    for n in range(2):
        refs[4][4 * n:4 * n + 4] = (
            refs[n][...].astype(F32) + refs[2 + n][...].astype(F32)).astype(BF16)


def join(a, b):
    streams = [block((4,) + a.shape[1:], lambda i, n=n: (2 * i + n, 0, 0)) for n in range(2)]
    return pl.pallas_call(
        join_kernel,
        grid=(a.shape[0] // 8,),
        in_specs=streams * 2,
        out_specs=block((8,) + a.shape[1:], lambda i: (i, 0, 0)),
        out_shape=shape(a.shape),
        compiler_params=PARAMS,
        cost_estimate=cost(0.01),
        name="join",
    )(a, a, b, b)


def total_kernel(*refs):
    refs[-1][...] = functools.reduce(
        lambda a, b: a + b, [jnp.sum(ref[...].astype(F32), axis=0) for ref in refs[:-1]])


def total(parts, streams=8):
    count, rows, columns = parts.shape
    return pl.pallas_call(
        total_kernel,
        grid=(1,),
        in_specs=[block((count // streams, rows, columns), lambda i, n=n: (n, 0, 0))
                  for n in range(streams)],
        out_specs=block((rows, columns), lambda i: (0, 0)),
        out_shape=shape((rows, columns), F32),
        compiler_params=PARAMS,
        cost_estimate=cost(0.01),
        name="total",
    )(*[parts] * streams)


def fill_kernel(sc_ref, *refs):
    count = len(refs) // 3
    for part_ref, out_ref in zip(refs[count:2 * count], refs[2 * count:]):
        out_ref[...] = part_ref[...]


def fill(sc, wholes, parts, gflops):
    count = len(wholes)
    return pl.pallas_call(
        fill_kernel,
        grid_spec=pltpu.PrefetchScalarGridSpec(
            num_scalar_prefetch=1,
            grid=(1,),
            in_specs=[pl.BlockSpec(memory_space=pl.ANY)] * count
            + [block(part.shape, lambda i, sc: (0, 0)) for part in parts],
            out_specs=[block(part.shape, lambda i, sc: (0, 1 - sc[0])) for part in parts],
        ),
        out_shape=[shape(whole.shape) for whole in wholes],
        input_output_aliases={1 + n: n for n in range(count)},
        compiler_params=PARAMS,
        cost_estimate=cost(gflops),
        name="fill",
    )(sc, *wholes, *parts)


def finish_kernel(sc_ref, *refs):
    count = (len(refs) - 4) // 3
    owns, other_ref, mixed_ref = refs[:2], refs[2], refs[3 + 2 * count]
    for part_ref, out_ref in zip(refs[3 + count:3 + 2 * count], refs[4 + 2 * count:]):
        out_ref[...] = part_ref[...]
    width = owns[0].shape[1]
    for n in range(2):
        lanes = slice(n * width, (n + 1) * width)
        mixed_ref[:, lanes] = (owns[n][...] + other_ref[:, lanes].astype(F32)).astype(BF16)


def finish(sc, mixed, wholes, parts):
    count, steps = len(wholes), 2
    columns = mixed[1].shape[1]
    some = lambda part: block((T, part.shape[1] // steps), lambda i, sc: (0, i))
    return pl.pallas_call(
        finish_kernel,
        grid_spec=pltpu.PrefetchScalarGridSpec(
            num_scalar_prefetch=1,
            grid=(steps,),
            in_specs=[block((T, columns // 4), lambda i, sc, n=n: (0, 2 * i + n))
                      for n in range(2)]
            + [some(mixed[1])] + [pl.BlockSpec(memory_space=pl.ANY)] * count
            + [some(part) for part in parts],
            out_specs=[some(mixed[1])]
            + [block((T, part.shape[1] // steps), lambda i, sc: (0, steps * (1 - sc[0]) + i))
               for part in parts],
        ),
        out_shape=[shape(mixed[1].shape)] + [shape(whole.shape) for whole in wholes],
        input_output_aliases={4 + n: 1 + n for n in range(count)},
        compiler_params=PARAMS,
        cost_estimate=cost(0.01),
        name="finish",
    )(sc, mixed[0], *mixed, *wholes, *parts)


def exchange(x):
    count = lax.axis_size("ctx")
    groups = [list(range(core, count, 2)) for core in range(2)]
    return lax.all_to_all(x, "ctx", split_axis=0, concat_axis=0, tiled=True,
                          axis_index_groups=groups)


def cross(x, axis, distance):
    count = lax.axis_size(axis)
    return lax.ppermute(x, axis, [(i, i ^ distance) for i in range(count)])


def sibling(x):
    return cross(x, "ctx", 1)


def tie(*values):
    return lax.optimization_barrier(values)


def place_of(z, chip, core, chips):
    return (z * chips + chip) * 2 + core


def feature_round(x, n, seqs):
    chips = lax.axis_size("ctx") // 2
    pairs = [(place_of(z, chip, core, chips),
              place_of(2 * core + (z ^ n) // 2, chip, (z ^ n) % 2, chips))
             for z in range(seqs) for chip in range(chips) for core in range(2)]
    return lax.ppermute(x, ("fsdp", "ctx"), pairs)


def weight_round(x, n, seqs):
    chips = lax.axis_size("ctx") // 2
    pairs = [(place_of(2 * core + (z ^ n) % 2, chip, 1 - z // 2, chips),
              place_of(z, chip, core, chips))
             for z in range(seqs) for chip in range(chips) for core in range(2)]
    return lax.ppermute(x, ("fsdp", "ctx"), pairs)


def body(query_vectors, key_vectors, value_vectors, output_gate, log_decay, write_rate,
         out_weight, cotangent, lengths, pairing, log_ratio):
    q, k, v, gate = query_vectors[0], key_vectors[0], value_vectors[0], output_gate[0]
    spot = lax.axis_index("ctx")
    core, chips = spot % 2, lax.axis_size("ctx") // 2
    me = lax.axis_index("fsdp")
    seqs = lax.axis_size("fsdp")
    sc = jnp.stack([core, me, spot])

    with jax.named_scope("swap_heads"):
        ld, be = log_decay[0].T, write_rate[0].T
        k_x, v_x, ld_x, be_x = (sibling(part) for part in (k, v, ld, be))
    with jax.named_scope("out_weight"):
        heads_weight = [weight_round(out_weight, n, seqs) for n in range(2)]
    ab, t, u0, kg, a, b = write_local(sc, k, v, ld, be, k_x, v_x, ld_x, be_x)
    with jax.named_scope("every_scaled"):
        cotangent = tie(ab, cotangent)[1]
        scaled = scale_local(sc, lengths, pairing, log_ratio, cotangent[0])
    with jax.named_scope("swap_heads"):
        q_x, gate_x, scaled_x = sibling(q), sibling(gate), sibling(scaled)
    ab = exchange(ab)
    p, r, io = read_local(sc, q, k, ld, be, q_x, k_x, ld_x, be_x, u0, kg)
    ab, p, r, io, scaled = tie(ab, p, r, io, scaled)
    states = chain(chain_up_kernel, ab)
    entering = exchange(states).reshape(PAIR_SHAPE)
    with jax.named_scope("back_grad"):
        bg = back_local(sc, scaled, scaled_x, heads_weight)
    with jax.named_scope("every_scaled"):
        own_scaled = tie(heads_weight[0], heads_weight[1], scaled)[2]
        every_scaled = [scaled] + [cross(own_scaled, "fsdp", s) for s in range(1, seqs)]
    *rows, normed, normed_x, gate_grad, gate_grad_x, u, second, g, gs, dq, dq_x, dkn, du = gate_local(
        sc, entering, gate, ld, be, gate_x, ld_x, be_x, *bg, a, b, io, u0, kg, r, p, q, k, q_x, k_x)
    g = exchange(g.reshape(2 * HEADS, HALF, DK))
    with jax.named_scope("every_normed"):
        rows = [feature_round(rows[n], n, seqs) for n in range(seqs)]
    g, *every_scaled = tie(g, *every_scaled)
    states = chain(chain_down_kernel, ab, g)
    leaving = exchange(states).reshape(PAIR_SHAPE)
    with jax.named_scope("weight_grad"):
        rows = list(tie(states, *rows)[1:])
        keep, send = weight_local(sc, rows, every_scaled)
        send = sibling(send)
        gate_grad, dq = fill(sc, [gate_grad, dq], [sibling(gate_grad_x), sibling(dq_x)], 25)
        keep, gate_grad = tie(keep, gate_grad)
        terms = join(keep, send)
        weight_grad = total(exchange(terms))
        leaving, terms = tie(leaving, terms)
    dk, dv, dk_x, dv_x = late_local(sc, k, ld, be, k_x, ld_x, be_x, t, u, a, entering, second,
                                    leaving, gs, dkn, du)
    with jax.named_scope("mixed_out"):
        dk, normed, normed_x = tie(dk, normed, normed_x)
        mixed, mixed_x = mixed_local(sc, normed, normed_x, heads_weight)
    with jax.named_scope("swap_back"):
        mixed, dk, dv = finish(
            sc, [mixed, sibling(mixed_x)], [dk, dv], [sibling(dk_x), sibling(dv_x)])
    return mixed[None], dq[None], dk[None], dv[None], gate_grad[None], weight_grad


def solution(mesh):
    tokens = P("fsdp", "ctx", None)
    return jax.shard_map(
        body,
        mesh=mesh,
        in_specs=(tokens,) * 6 + (P("fsdp", None), tokens, P(), P(), P()),
        out_specs=(tokens,) * 5 + (P(("fsdp", "ctx"), None),),
        check_vma=False,
    )
```

```python
import functools

import jax
import jax.numpy as jnp
from jax import lax
from jax.experimental import pallas as pl
from jax.experimental.pallas import tpu as pltpu
from jax.sharding import PartitionSpec as P

VALUE_HEADS = 16
HK = 8
DK = 128
DV = 128
T = 128
HALF = 64
TAIL = 16
CHI_BETA = 0.5
NORM_EPS = 1e-06
F32 = jnp.float32
BF16 = jnp.bfloat16

NN = (((1,), (0,)), ((), ()))
NT = (((1,), (1,)), ((), ()))
TN = (((0,), (0,)), ((), ()))


def dot1(a, b, dims=NN):
    return lax.dot_general(a.astype(BF16), b.astype(BF16), dims, preferred_element_type=F32)


def split(a):
    high = a.astype(BF16)
    return high, (a - high.astype(F32)).astype(BF16)


def dot3(a, b, dims=NN):
    a_high, a_low = split(a)
    b_high, b_low = split(b)
    return dot1(a_high, b_high, dims) + (dot1(a_low, b_high, dims) + dot1(a_high, b_low, dims))


def grid_index():
    row = lax.broadcasted_iota(jnp.int32, (T, T), 0)
    col = lax.broadcasted_iota(jnp.int32, (T, T), 1)
    return row, col


def unit(x):
    return lax.rsqrt(jnp.sum(x * x, axis=-1, keepdims=True) + NORM_EPS)


def dot_exact_left(a, b):
    first = a.astype(BF16)
    rest = a - first.astype(F32)
    second = rest.astype(BF16)
    third = (rest - second.astype(F32)).astype(BF16)
    return dot1(first, b) + (dot1(second, b) + dot1(third, b))


def in_order(sc_ref, own, other):
    is_first = sc_ref[0] == 0
    return jnp.where(is_first, own, other), jnp.where(is_first, other, own)


def decay_tables(sc_ref, lo_ref, ro_ref, lx_ref, rx_ref, row, col):
    upper = (row <= col).astype(BF16)
    tables = []
    for decay, rate in zip(in_order(sc_ref, lo_ref[...], lx_ref[...]),
                           in_order(sc_ref, ro_ref[...], rx_ref[...])):
        cum_t = dot_exact_left(decay, upper)
        tables.append((cum_t, cum_t.T, rate.T))
    return tables


def column(table, head):
    lane = lax.broadcasted_iota(jnp.int32, table.shape, 1)
    return jnp.sum(jnp.where(lane == head, table, 0.0), axis=1, keepdims=True)


def as_row(table_t, head):
    sub = lax.broadcasted_iota(jnp.int32, table_t.shape, 0)
    return jnp.sum(jnp.where(sub == head, table_t, 0.0), axis=0, keepdims=True)


def decay_within(cum_col, cum_row, mask):
    return jnp.where(mask, jnp.exp(jnp.where(mask, cum_col - cum_row, 0.0)), 0.0)


def stripes(x, size, first):
    return jnp.concatenate(
        [x[start:start + size] for start in range(first * size, T, 2 * size)], axis=0)


def weave(even, odd, size):
    parts = []
    for start in range(0, T // 2, size):
        parts += [even[start:start + size], odd[start:start + size]]
    return jnp.concatenate(parts, axis=0)


def invert(couplings, row, col):
    eye = (row == col).astype(F32)
    pairs = (row >> 1) == (col >> 1)
    inverses = [eye - jnp.where(pairs, c, 0.0) for c in couplings]
    for level in range(1, 3):
        mask = ((row >> (level + 1)) == (col >> (level + 1))) & ((row >> level) != (col >> level))
        offs = [jnp.where(mask, c, 0.0).astype(BF16) for c in couplings]
        low = [i.astype(BF16) for i in inverses]
        inner = [dot1(o, i) for o, i in zip(offs, low)]
        inverses = [x - dot1(i, n) for x, i, n in zip(inverses, low, inner)]
    for level in range(3, 7):
        size = 1 << level
        mask = (stripes(row, size, 1) >> level) == (stripes(col, size, 1) >> level) + 1
        zeros = jnp.zeros((T // 2, T), F32)
        odds = [stripes(i, size, 1) for i in inverses]
        inner = [dot1(jnp.where(mask, stripes(c, size, 1), 0.0), i)
                 for c, i in zip(couplings, inverses)]
        odds = [o - dot1(o, weave(zeros, n, size)) for o, n in zip(odds, inner)]
        inverses = [weave(stripes(i, size, 0), o, size) for i, o in zip(inverses, odds)]
    return inverses


def total_rows(total):
    wide = jnp.broadcast_to(total, (TAIL, DK))
    high, low = split(wide)
    low2 = (wide - high.astype(F32) - low.astype(F32)).astype(BF16)
    sub_row = lax.broadcasted_iota(jnp.int32, (TAIL, DK), 0)
    tail = jnp.where(sub_row == 0, high.astype(F32),
                     jnp.where(sub_row == 1, low.astype(F32),
                               jnp.where(sub_row == 2, low2.astype(F32), 0.0)))
    return tail.astype(BF16)


def units(keys):
    return [(sub, block, 2 * (sub // 2) + block) for sub in range(2 * keys) for block in range(2)]


def first_head(sc_ref, keys):
    return (VALUE_HEADS // 2) * sc_ref[0] + 2 * keys * pl.program_id(0)


def per_head(sc_ref, keys, own_ref, other_ref):
    found = []
    for key in range(keys):
        lanes = slice(key * DK, (key + 1) * DK)
        found += in_order(sc_ref, own_ref[:, lanes].astype(F32), other_ref[:, lanes].astype(F32))
    return found


def write_kernel(keys, sc_ref, ko_ref, vo_ref, lo_ref, ro_ref, kx_ref, vx_ref, lx_ref, rx_ref,
                 ab_ref, t_ref, u0_ref, kg_ref, a_ref, b_ref):
    row, col = grid_index()
    causal, strict = row >= col, row > col
    tables = decay_tables(sc_ref, lo_ref, ro_ref, lx_ref, rx_ref, row, col)
    ks = per_head(sc_ref, keys, ko_ref, kx_ref)
    vs = in_order(sc_ref, vo_ref[...].astype(F32), vx_ref[...].astype(F32))
    kns = [k * unit(k) for k in ks]
    kks = [dot3(kn, kn, NT) for kn in kns]
    cols, rates, couplings = [], [], []
    for sub, block, kb in units(keys):
        cum_t, cum, beta = tables[block]
        h = first_head(sc_ref, keys) + sub
        cum_col, rate = column(cum, h), column(beta, h)
        within = decay_within(cum_col, as_row(cum_t, h), causal)
        couplings.append(jnp.where(strict, kks[kb] * within, 0.0) * rate)
        cols.append(cum_col)
        rates.append(rate)
    inverses = [i.astype(BF16) for i in invert(couplings, row, col)]
    u0s, kgs, transits, writtens, totals = [], [], [], [], []
    for n, (sub, block, kb) in enumerate(units(keys)):
        u0s.append(dot1(inverses[n], rates[n] * vs[block][:, sub * DV:(sub + 1) * DV]))
        kgs.append(dot1(inverses[n], (rates[n] * jnp.exp(cols[n])) * kns[kb]).astype(BF16))
    for n, (sub, block, kb) in enumerate(units(keys)):
        total = cols[n][T - 1:, :]
        carried = (jnp.exp(total - cols[n]) * kns[kb]).astype(BF16)
        transits.append(dot1(kgs[n], carried, TN))
        writtens.append(dot1(u0s[n], carried, TN))
        totals.append(total)
        t_ref[n] = inverses[n]
        u0_ref[n] = u0s[n].astype(BF16)
        kg_ref[n] = kgs[n]
        a_ref[n] = transits[n].astype(BF16)
    for sub in range(2 * keys):
        f, s = 2 * sub, 2 * sub + 1
        e_f, e_s = jnp.exp(totals[f]), jnp.exp(totals[s])
        stacked = jnp.concatenate([transits[f], writtens[f]], axis=0)
        moved = dot3(stacked, transits[s])
        transit = (e_f * transits[s] + e_s * transits[f] - moved[:DK]).astype(BF16)
        written = (e_s * writtens[f] - moved[DK:] + writtens[s]).astype(BF16)
        b_ref[sub] = writtens[f].astype(BF16)
        tail = total_rows(totals[f] + totals[s])
        for half in range(2):
            slot = 2 * sub + half
            ab_ref[slot, 0:DK, :] = transit
            ab_ref[slot, DK:DK + HALF, :] = written[half * HALF:(half + 1) * HALF]
            ab_ref[slot, DK + HALF:, :] = tail


def read_kernel(keys, sc_ref, qo_ref, ko_ref, lo_ref, ro_ref, qx_ref, kx_ref, lx_ref, rx_ref, u0_ref, kg_ref,
                p_ref, r_ref, io_ref):
    row, col = grid_index()
    causal = row >= col
    tables = decay_tables(sc_ref, lo_ref, ro_ref, lx_ref, rx_ref, row, col)
    qs = per_head(sc_ref, keys, qo_ref, qx_ref)
    ks = per_head(sc_ref, keys, ko_ref, kx_ref)
    qns = [q * unit(q) * DK ** (-0.5) for q in qs]
    qks = [dot3(qn, k * unit(k), NT) for qn, k in zip(qns, ks)]
    cols, scores = [], []
    for sub, block, kb in units(keys):
        cum_t, cum, _ = tables[block]
        h = first_head(sc_ref, keys) + sub
        cum_col = column(cum, h)
        cols.append(cum_col)
        scores.append((qks[kb] * decay_within(cum_col, as_row(cum_t, h), causal)).astype(BF16))
    for n, (sub, block, kb) in enumerate(units(keys)):
        p_ref[n] = scores[n]
        io_ref[n] = dot1(scores[n], u0_ref[n]).astype(BF16)
        r_ref[n] = (jnp.exp(cols[n]) * qns[kb] - dot1(scores[n], kg_ref[n])).astype(BF16)


def gate_kernel(keys, sc_ref, s_ref, go_ref, lo_ref, ro_ref, gx_ref, lx_ref, rx_ref, bo_ref, bx_ref,
                a_ref, b_ref, io_ref, u0_ref, kg_ref, r_ref, p_ref, qo_ref, ko_ref, qx_ref, kx_ref,
                n0_ref, n1_ref, n2_ref, n3_ref, no_ref, nx_ref, gg_ref, ggx_ref,
                u_ref, ss_ref, g_ref, gs_ref, dq_ref, dqx_ref, dk_ref, du_ref):
    gates = in_order(sc_ref, go_ref[...].astype(F32), gx_ref[...].astype(F32))
    me, step = sc_ref[1], pl.program_id(0)
    steps = KEYS // (2 * keys)
    bgs = in_order(sc_ref, bo_ref[...].astype(F32), bx_ref[...].astype(F32))
    row, col = grid_index()
    causal = row >= col
    tables = decay_tables(sc_ref, lo_ref, ro_ref, lx_ref, rx_ref, row, col)
    qs = per_head(sc_ref, keys, qo_ref, qx_ref)
    ks = per_head(sc_ref, keys, ko_ref, kx_ref)
    q_scales = [unit(q) for q in qs]
    qns = [(q * scale * DK ** (-0.5)).astype(BF16) for q, scale in zip(qs, q_scales)]
    kns = [(k * unit(k)).astype(BF16) for k in ks]
    cols = [column(tables[block][1], first_head(sc_ref, keys) + sub) for sub, block, kb in units(keys)]
    states, fades = [], []
    for sub in range(2 * keys):
        state = s_ref[sub]
        fade = jnp.exp(cols[2 * sub][T - 1:, :])
        second = (fade * state.astype(F32) - dot1(state, a_ref[2 * sub])
                  + b_ref[sub].astype(F32)).astype(BF16)
        ss_ref[sub] = second
        states += [state, second]
        fades.append(fade)
    outs = [io_ref[n] + dot1(r_ref[n], states[n], NT) for n in range(4 * keys)]
    normeds, gate_grads, d_outs, us = [], [], [], []
    for n, (sub, block, kb) in enumerate(units(keys)):
        lanes = slice(sub * DV, (sub + 1) * DV)
        us.append((u0_ref[n] - dot1(kg_ref[n], states[n], NT)).astype(BF16))
        u_ref[n] = us[n]
        out = outs[n]
        scale = lax.rsqrt(jnp.mean(out * out, axis=-1, keepdims=True) + NORM_EPS)
        z = out * scale
        gate = gates[block][:, lanes]
        sig = 1.0 / (1.0 + jnp.exp(-gate))
        sil = gate * sig
        normeds.append(z * sil)
        bg = bgs[block][:, lanes]
        gate_grads.append(bg * z * (sig + sil * (1.0 - sig)))
        dz = bg * sil
        d_out = scale * (dz - z * jnp.mean(dz * z, axis=-1, keepdims=True))
        d_outs.append(d_out.astype(BF16))
    grads = [dot1(d_outs[n], r_ref[n], TN) for n in range(4 * keys)]
    for sub in range(2 * keys):
        lanes = slice(sub * DV, (sub + 1) * DV)
        f, s = 2 * sub, 2 * sub + 1
        g_ref[sub] = (grads[f] + fades[sub] * grads[s]
                      - dot1(grads[s], a_ref[f], NT)).astype(BF16)
        gs_ref[sub] = grads[s].astype(BF16)
        own, other = in_order(sc_ref, gate_grads[f], gate_grads[s])
        gg_ref[:, lanes] = own.astype(BF16)
        ggx_ref[:, lanes] = other.astype(BF16)
    width = 2 * keys * DV
    columns = pl.ds(pl.multiple_of((step % steps) * width, width), width)
    blocks = [jnp.concatenate(normeds[tau::2], axis=1).astype(BF16) for tau in range(2)]
    no_ref[...], nx_ref[...] = in_order(sc_ref, *blocks)
    for n, ref in enumerate((n0_ref, n1_ref, n2_ref, n3_ref)):
        code = me ^ n

        @pl.when(code // 2 == step // steps)
        def _():
            ref[:, columns] = jnp.where(code % 2 == 0, blocks[0], blocks[1])
    raw = [dot1(d_outs[n], us[n], NT) for n in range(4 * keys)]
    d_scores = []
    for n, (sub, block, kb) in enumerate(units(keys)):
        cum_t, h = tables[block][0], first_head(sc_ref, keys) + sub
        d_scores.append((raw[n] * decay_within(cols[n], as_row(cum_t, h), causal)).astype(BF16))
    dqs, dkns = [], []
    for n, (sub, block, kb) in enumerate(units(keys)):
        du_ref[n] = dot1(p_ref[n], d_outs[n], TN).astype(BF16)
        dqs.append(jnp.exp(cols[n]) * dot1(d_outs[n], states[n]) + dot1(d_scores[n], kns[kb]))
        dkns.append(dot1(d_scores[n], qns[kb], TN))
    for key in range(keys):
        lanes = slice(key * DK, (key + 1) * DK)
        results = []
        for block in range(2):
            n, kb = 4 * key + block, 2 * key + block
            q, scale, dqn = qs[kb], q_scales[kb], dqs[n] + dqs[n + 2]
            dk_ref[block, :, lanes] = dkns[n] + dkns[n + 2]
            results.append(scale * DK ** (-0.5) * (
                dqn - q * (scale * scale) * jnp.sum(q * dqn, axis=-1, keepdims=True)))
        own, other = in_order(sc_ref, *results)
        dq_ref[:, lanes] = own.astype(BF16)
        dqx_ref[:, lanes] = other.astype(BF16)


def late_kernel(keys, sc_ref, ko_ref, lo_ref, ro_ref, kx_ref, lx_ref, rx_ref, t_ref, u_ref, a_ref, s_ref, ss_ref,
                l_ref, gs_ref, dkn_ref, du_ref,
                dk_ref, dv_ref, dkx_ref, dvx_ref):
    row, col = grid_index()
    strict = row > col
    tables = decay_tables(sc_ref, lo_ref, ro_ref, lx_ref, rx_ref, row, col)
    ks = per_head(sc_ref, keys, ko_ref, kx_ref)
    scales = [unit(k) for k in ks]
    kns = [(k * scale).astype(BF16) for k, scale in zip(ks, scales)]
    cols, rates, withins, leavings = [], [], [], []
    for n, (sub, block, kb) in enumerate(units(keys)):
        cum_t, cum, beta = tables[block]
        h = first_head(sc_ref, keys) + sub
        cols.append(column(cum, h))
        rates.append(column(beta, h))
        withins.append(decay_within(cols[n], as_row(cum_t, h), strict) * (-rates[n]))
    for sub in range(2 * keys):
        last = l_ref[sub]
        fade = jnp.exp(cols[2 * sub + 1][T - 1:, :])
        leavings.append((gs_ref[sub].astype(F32) + fade * last.astype(F32)
                         - dot1(last, a_ref[2 * sub + 1], NT)).astype(BF16))
        leavings.append(last)
    fades = [jnp.exp(c[T - 1:, :] - c) for c in cols]
    dus = [du_ref[n] + fades[n] * dot1(kns[kb], leavings[n], NT)
           for n, (sub, block, kb) in enumerate(units(keys))]
    dxs = [dot1(t_ref[n], dus[n], TN) for n in range(4 * keys)]
    dx_bs = [dx.astype(BF16) for dx in dxs]
    d_inters = [dot1(dx_bs[n], u_ref[n], NT) * withins[n] for n in range(4 * keys)]
    dkns = []
    for n, (sub, block, kb) in enumerate(units(keys)):
        state = s_ref[sub] if block == 0 else ss_ref[sub]
        dkns.append(dot1(d_inters[n] + d_inters[n].T, kns[kb])
                    + fades[n] * dot1(u_ref[n], leavings[n])
                    - (rates[n] * jnp.exp(cols[n])) * dot1(dx_bs[n], state))
    for key in range(keys):
        lanes = slice(key * DK, (key + 1) * DK)
        results = []
        for block in range(2):
            n, kb = 4 * key + block, 2 * key + block
            k, scale = ks[kb], scales[kb]
            dkn = dkn_ref[block, :, lanes] + dkns[n] + dkns[n + 2]
            results.append(
                scale * (dkn - k * (scale * scale) * jnp.sum(k * dkn, axis=-1, keepdims=True)))
        own, other = in_order(sc_ref, *results)
        dk_ref[:, lanes] = own.astype(BF16)
        dkx_ref[:, lanes] = other.astype(BF16)
    for sub in range(2 * keys):
        lanes = slice(sub * DV, (sub + 1) * DV)
        f, s = 2 * sub, 2 * sub + 1
        own, other = in_order(sc_ref, rates[f] * dxs[f], rates[s] * dxs[s])
        dv_ref[:, lanes] = own.astype(BF16)
        dvx_ref[:, lanes] = other.astype(BF16)


HEADS = VALUE_HEADS // 2
KEYS = HK // 2
PARAMS = pltpu.CompilerParams(vmem_limit_bytes=64 << 20)


def shape(dims, dtype=BF16):
    return jax.ShapeDtypeStruct(dims, dtype)


def block(dims, place):
    return pl.BlockSpec(dims, place)


def own(keys, width):
    return block((T, keys * width), lambda i, sc: (0, KEYS // keys * sc[0] + i))


def other(keys, width):
    return block((T, keys * width), lambda i, sc: (0, i))


def leading(count):
    return block((count, T, DK), lambda i, sc: (i, 0, 0))


TABLE = block((VALUE_HEADS, T), lambda i, sc: (0, 0))
SLICE = block((T, 4 * DV), lambda i, sc: (0, 0))
UNIT_SHAPE, PAIR_SHAPE = (2 * HEADS, T, DK), (HEADS, T, DK)


def cost(gflops):
    return pl.CostEstimate(flops=int(gflops * 1e9), bytes_accessed=1 << 16, transcendentals=0)


def per_key(kernel, name, gflops, keys, in_specs, out_specs, out_shape):
    return pl.pallas_call(
        functools.partial(kernel, keys),
        grid_spec=pltpu.PrefetchScalarGridSpec(
            num_scalar_prefetch=1, grid=(KEYS // keys,), in_specs=in_specs, out_specs=out_specs),
        out_shape=out_shape,
        compiler_params=PARAMS,
        cost_estimate=cost(gflops),
        name=name,
    )


ROWS = DK + HALF + TAIL
write_local = per_key(
    write_kernel, "write_local", 18, 2,
    [own(2, DK), own(2, 2 * DV), TABLE, TABLE, own(2, DK), own(2, 2 * DV), TABLE, TABLE],
    [block((8, ROWS, DK), lambda i, sc: (i, 0, 0)), leading(8), leading(8), leading(8), leading(8), leading(4)],
    [shape((2 * HEADS, ROWS, DK)), shape(UNIT_SHAPE), shape(UNIT_SHAPE), shape(UNIT_SHAPE),
     shape(UNIT_SHAPE), shape(PAIR_SHAPE)])
read_local = per_key(
    read_kernel, "read_local", 0.01, 2,
    [own(2, DK), own(2, DK), TABLE, TABLE, own(2, DK), own(2, DK), TABLE, TABLE, leading(8), leading(8)],
    [leading(8)] * 3,
    [shape(UNIT_SHAPE)] * 3)
gate_local = per_key(
    gate_kernel, "gate_local", 12, 2,
    [leading(4), own(2, 2 * DV), TABLE, TABLE, own(2, 2 * DV), TABLE, TABLE, other(2, 2 * DV), other(2, 2 * DV), leading(8), leading(4)]
    + [leading(8)] * 5 + [own(2, DK)] * 4,
    [SLICE] * 4 + [other(2, 2 * DV), other(2, 2 * DV), own(2, 2 * DV), other(2, 2 * DV), leading(8)] + [leading(4)] * 3
    + [own(2, DK), other(2, DK), block((2, T, 2 * DK), lambda i, sc: (0, 0, i)), leading(8)],
    [shape((T, 4 * DV))] * 4 + [shape((T, HEADS * DV))] * 2
    + [shape((T, VALUE_HEADS * DV)), shape((T, HEADS * DV)), shape(UNIT_SHAPE)]
    + [shape(PAIR_SHAPE)] * 3
    + [shape((T, HK * DK)), shape((T, KEYS * DK)), shape((2, T, KEYS * DK), F32),
       shape(UNIT_SHAPE)])
late_local = per_key(
    late_kernel, "late_local", 50, 2,
    [own(2, DK), TABLE, TABLE, own(2, DK), TABLE, TABLE, leading(8), leading(8), leading(8), leading(4), leading(4), leading(4), leading(4), block((2, T, 2 * DK), lambda i, sc: (0, 0, i)), leading(8)],
    [own(2, DK), own(2, 2 * DV), other(2, DK), other(2, 2 * DV)],
    [shape((T, HK * DK)), shape((T, VALUE_HEADS * DV)), shape((T, KEYS * DK)),
     shape((T, HEADS * DV))])


STREAMS = 4


def chain_step(ab_ref, i, state, dims, added):
    tail = ab_ref[i, DK + HALF:, :].astype(F32)
    decay = jnp.exp(jnp.sum(tail, axis=0, keepdims=True))
    high, low = split(state)
    moved = dot1(jnp.concatenate([high, low], axis=0), ab_ref[i, 0:DK, :], dims)
    return decay * state - (moved[:HALF] + moved[HALF:]) + added.astype(F32)


def chain_up_kernel(*refs):
    count = refs[0].shape[0]
    state = jnp.zeros((HALF, DK), F32)
    for i in range(STREAMS * count):
        refs[-1][i] = state.astype(BF16)
        ab_ref, n = refs[i // count], i % count
        state = chain_step(ab_ref, n, state, NN, ab_ref[n, DK:DK + HALF, :])


def chain_down_kernel(*refs):
    count = refs[0].shape[0]
    state = jnp.zeros((HALF, DK), F32)
    for i in reversed(range(STREAMS * count)):
        refs[-1][i] = state.astype(BF16)
        state = chain_step(refs[i // count], i % count, state, NT, refs[STREAMS][i])


def chain(kernel, ab, *args):
    count = ab.shape[0]
    streams = [block((count // STREAMS,) + ab.shape[1:], lambda i, n=n: (n, 0, 0))
               for n in range(STREAMS)]
    whole = block((count, HALF, DK), lambda i: (0, 0, 0))
    return pl.pallas_call(
        kernel,
        grid=(1,),
        in_specs=streams + [whole] * len(args),
        out_specs=whole,
        out_shape=shape((count, HALF, DK)),
        compiler_params=PARAMS,
        cost_estimate=cost(0.01),
        name="chain",
    )(*[ab] * STREAMS, *args)


def scale_kernel(sc_ref, lengths_ref, pairing_ref, ratio_ref, cot_ref, scaled_ref):
    own = sc_ref[1]
    tokens = cot_ref.shape[0]
    start = sc_ref[2] * T + pl.program_id(0) * tokens
    weight = jnp.zeros((8, 128), F32)
    for pair in range(pairing_ref.shape[0] // 2):
        chosen, rejected = pairing_ref[2 * pair], pairing_ref[2 * pair + 1]
        ratio_c = jnp.full((8, 128), ratio_ref[chosen], F32)
        ratio_r = jnp.full((8, 128), ratio_ref[rejected], F32)
        up_c, up_r = jnp.exp(ratio_c), jnp.exp(ratio_r)
        margin = CHI_BETA * (up_c + ratio_c - up_r - ratio_r)
        pull = CHI_BETA / (1.0 + jnp.exp(margin))
        weight = weight + jnp.where(chosen == own, -pull * (up_c + 1.0), 0.0)
        weight = weight + jnp.where(rejected == own, pull * (up_r + 1.0), 0.0)
    position = start + lax.broadcasted_iota(jnp.int32, (tokens, 1), 0)
    live = (position < lengths_ref[own]).astype(F32)
    factor = weight[0:1, 0:1] * live
    scaled_ref[...] = (cot_ref[...].astype(F32) * factor).astype(BF16)


def scale_local(sc, lengths, pairing, ratio, cot, steps=2):
    scalars = pl.BlockSpec(memory_space=pltpu.SMEM)
    rows = block((T // steps,) + cot.shape[1:], lambda i, sc: (i, 0))
    return pl.pallas_call(
        scale_kernel,
        grid_spec=pltpu.PrefetchScalarGridSpec(
            num_scalar_prefetch=1,
            grid=(steps,),
            in_specs=[scalars] * 3 + [rows],
            out_specs=rows,
        ),
        out_shape=shape(cot.shape),
        compiler_params=PARAMS,
        cost_estimate=cost(0.01),
        name="scale_local",
    )(sc, lengths, pairing, ratio, cot)


def turn(sc_ref):
    core, me = sc_ref[0], sc_ref[1]
    return (2 * (me % 2) + core) ^ me


def back_kernel(sc_ref, *refs):
    bo_ref, bx_ref = refs[16:]
    scaled = jnp.concatenate(
        [jnp.concatenate([refs[n][...], refs[4 + n][...]], axis=0) for n in range(4)], axis=1)
    first = pl.program_id(0) < 2
    weight = jnp.concatenate(
        [jnp.where(first, refs[8 + n][...], refs[12 + n][...]) for n in range(4)], axis=1)
    product = dot1(scaled, weight, NT).astype(BF16)
    bo_ref[...] = product[:T]
    bx_ref[...] = product[T:]


def back_local(sc, own, other, weights):
    features, columns = weights[0].shape
    width, part = features // 2, columns // 4
    tokens = [block((T, part), lambda i, sc, n=n: (0, n)) for n in range(4)]
    out = block((T, width), lambda i, sc: (0, 2 * ((i // 2) ^ (sc[1] % 2)) + i % 2))
    early = [block((width, part), lambda i, sc, n=n: (jnp.minimum(i, 1), n)) for n in range(4)]
    late = [block((width, part), lambda i, sc, n=n: (jnp.maximum(i - 2, 0), n)) for n in range(4)]
    return pl.pallas_call(
        back_kernel,
        grid_spec=pltpu.PrefetchScalarGridSpec(
            num_scalar_prefetch=1,
            grid=(4,),
            in_specs=tokens + tokens + early + late,
            out_specs=[out, out],
        ),
        out_shape=[shape((T, 2 * features))] * 2,
        compiler_params=PARAMS,
        cost_estimate=cost(0.01),
        name="back_local",
    )(sc, *[own] * 4, *[other] * 4, *[weights[0]] * 4, *[weights[1]] * 4)


def mixed_kernel(sc_ref, no_ref, nx_ref, *refs):
    own_ref, other_ref = refs[8:]
    features = 4 * refs[0].shape[0]
    odd = sc_ref[1] % 2
    first = pl.ds(pl.multiple_of(odd * features, features), features)
    second = pl.ds(pl.multiple_of((1 - odd) * features, features), features)
    weights = [jnp.concatenate([ref[...] for ref in refs[4 * n:4 * n + 4]], axis=0)
               for n in range(2)]
    product = (dot1(jnp.concatenate([no_ref[:, first], nx_ref[:, first]], axis=0), weights[0])
               + dot1(jnp.concatenate([no_ref[:, second], nx_ref[:, second]], axis=0), weights[1]))
    own_ref[...] = product[:T]
    other_ref[...] = product[T:].astype(BF16)


def mixed_local(sc, own, other, weights, width=512):
    features, columns = weights[0].shape
    tokens = block((T, 2 * features), lambda i, sc: (0, 0))
    rows = [block((features // 4, width), lambda i, sc, n=n: (n, i)) for n in range(4)]
    out = block((T, width), lambda i, sc: (0, i))
    return pl.pallas_call(
        mixed_kernel,
        grid_spec=pltpu.PrefetchScalarGridSpec(
            num_scalar_prefetch=1,
            grid=(columns // width,),
            in_specs=[tokens, tokens] + rows + rows,
            out_specs=[out, out],
        ),
        out_shape=[shape((T, columns), F32), shape((T, columns))],
        compiler_params=PARAMS,
        cost_estimate=cost(0.01),
        name="mixed_local",
    )(sc, own, other, *[weights[0]] * 4, *[weights[1]] * 4)


def weight_kernel(sc_ref, *refs):
    keep_ref, send_ref, rows_ref, part_ref, sems = refs[20:]
    for n in range(4):
        rows_ref[n ^ turn(sc_ref)] = refs[n][...]
    rows = rows_ref[...].reshape(4 * T, rows_ref.shape[2])
    chips, cores, height, columns = part_ref.shape
    width, some = columns // 4, chips // 2
    core = lax.axis_index("ctx") % 2
    copies = []
    for n in range(4):
        lanes = slice(n * width, (n + 1) * width)
        scaled = jnp.concatenate([ref[...] for ref in refs[4 + n:20:4]], axis=0)
        part_ref[:, :, :, lanes] = dot1(rows, scaled, TN).astype(BF16).reshape(
            chips, cores, height, width)
        for m in range(2):
            group, lane = pl.ds(m * some, some), pl.ds(n * width, width)
            for to_ref, row in ((keep_ref, core), (send_ref, 1 - core)):
                copies.append(pltpu.make_async_copy(
                    part_ref.at[group, row, :, lane], to_ref.at[group, :, lane],
                    sems.at[len(copies)]))
                copies[-1].start()
    for copy in copies:
        copy.wait()


def weight_local(sc, rows, scaled):
    features, columns = rows[0].shape[1], scaled[0].shape[1]
    same = lambda part: block(part.shape, lambda i, sc: (0, 0))
    return pl.pallas_call(
        weight_kernel,
        grid_spec=pltpu.PrefetchScalarGridSpec(
            num_scalar_prefetch=1,
            grid=(1,),
            in_specs=[same(part) for part in rows]
            + [block((T, columns // 4), lambda i, sc, n=n: (0, n)) for n in range(4)] * 4,
            out_specs=[pl.BlockSpec(memory_space=pl.ANY)] * 2,
            scratch_shapes=[pltpu.VMEM((4, T, features), BF16),
                            pltpu.VMEM((features // 32, 2, 16, columns), BF16),
                            pltpu.SemaphoreType.DMA((16,))],
        ),
        out_shape=[shape((features // 32, 16, columns))] * 2,
        compiler_params=PARAMS,
        cost_estimate=cost(4),
        name="weight_local",
    )(sc, *rows, *[part for part in scaled for _ in range(4)])


def join_kernel(*refs):
    for n in range(2):
        refs[4][4 * n:4 * n + 4] = (
            refs[n][...].astype(F32) + refs[2 + n][...].astype(F32)).astype(BF16)


def join(a, b):
    streams = [block((4,) + a.shape[1:], lambda i, n=n: (2 * i + n, 0, 0)) for n in range(2)]
    return pl.pallas_call(
        join_kernel,
        grid=(a.shape[0] // 8,),
        in_specs=streams * 2,
        out_specs=block((8,) + a.shape[1:], lambda i: (i, 0, 0)),
        out_shape=shape(a.shape),
        compiler_params=PARAMS,
        cost_estimate=cost(0.01),
        name="join",
    )(a, a, b, b)


def total_kernel(*refs):
    refs[-1][...] = functools.reduce(
        lambda a, b: a + b, [jnp.sum(ref[...].astype(F32), axis=0) for ref in refs[:-1]])


def total(parts, streams=8):
    count, rows, columns = parts.shape
    return pl.pallas_call(
        total_kernel,
        grid=(1,),
        in_specs=[block((count // streams, rows, columns), lambda i, n=n: (n, 0, 0))
                  for n in range(streams)],
        out_specs=block((rows, columns), lambda i: (0, 0)),
        out_shape=shape((rows, columns), F32),
        compiler_params=PARAMS,
        cost_estimate=cost(0.01),
        name="total",
    )(*[parts] * streams)


def fill_kernel(sc_ref, *refs):
    count = len(refs) // 3
    for part_ref, out_ref in zip(refs[count:2 * count], refs[2 * count:]):
        out_ref[...] = part_ref[...]


def fill(sc, wholes, parts, gflops):
    count = len(wholes)
    return pl.pallas_call(
        fill_kernel,
        grid_spec=pltpu.PrefetchScalarGridSpec(
            num_scalar_prefetch=1,
            grid=(1,),
            in_specs=[pl.BlockSpec(memory_space=pl.ANY)] * count
            + [block(part.shape, lambda i, sc: (0, 0)) for part in parts],
            out_specs=[block(part.shape, lambda i, sc: (0, 1 - sc[0])) for part in parts],
        ),
        out_shape=[shape(whole.shape) for whole in wholes],
        input_output_aliases={1 + n: n for n in range(count)},
        compiler_params=PARAMS,
        cost_estimate=cost(gflops),
        name="fill",
    )(sc, *wholes, *parts)


def finish_kernel(sc_ref, *refs):
    count = (len(refs) - 4) // 3
    owns, other_ref, mixed_ref = refs[:2], refs[2], refs[3 + 2 * count]
    for part_ref, out_ref in zip(refs[3 + count:3 + 2 * count], refs[4 + 2 * count:]):
        out_ref[...] = part_ref[...]
    width = owns[0].shape[1]
    for n in range(2):
        lanes = slice(n * width, (n + 1) * width)
        mixed_ref[:, lanes] = (owns[n][...] + other_ref[:, lanes].astype(F32)).astype(BF16)


def finish(sc, mixed, wholes, parts):
    count, steps = len(wholes), 2
    columns = mixed[1].shape[1]
    some = lambda part: block((T, part.shape[1] // steps), lambda i, sc: (0, i))
    return pl.pallas_call(
        finish_kernel,
        grid_spec=pltpu.PrefetchScalarGridSpec(
            num_scalar_prefetch=1,
            grid=(steps,),
            in_specs=[block((T, columns // 4), lambda i, sc, n=n: (0, 2 * i + n))
                      for n in range(2)]
            + [some(mixed[1])] + [pl.BlockSpec(memory_space=pl.ANY)] * count
            + [some(part) for part in parts],
            out_specs=[some(mixed[1])]
            + [block((T, part.shape[1] // steps), lambda i, sc: (0, steps * (1 - sc[0]) + i))
               for part in parts],
        ),
        out_shape=[shape(mixed[1].shape)] + [shape(whole.shape) for whole in wholes],
        input_output_aliases={4 + n: 1 + n for n in range(count)},
        compiler_params=PARAMS,
        cost_estimate=cost(0.01),
        name="finish",
    )(sc, mixed[0], *mixed, *wholes, *parts)


def exchange(x):
    count = lax.axis_size("ctx")
    groups = [list(range(core, count, 2)) for core in range(2)]
    return lax.all_to_all(x, "ctx", split_axis=0, concat_axis=0, tiled=True,
                          axis_index_groups=groups)


def cross(x, axis, distance):
    count = lax.axis_size(axis)
    return lax.ppermute(x, axis, [(i, i ^ distance) for i in range(count)])


def sibling(x):
    return cross(x, "ctx", 1)


def tie(*values):
    return lax.optimization_barrier(values)


def place_of(z, chip, core, chips):
    return (z * chips + chip) * 2 + core


def feature_round(x, n, seqs):
    chips = lax.axis_size("ctx") // 2
    pairs = [(place_of(z, chip, core, chips),
              place_of(2 * core + (z ^ n) // 2, chip, (z ^ n) % 2, chips))
             for z in range(seqs) for chip in range(chips) for core in range(2)]
    return lax.ppermute(x, ("fsdp", "ctx"), pairs)


def weight_round(x, n, seqs):
    chips = lax.axis_size("ctx") // 2
    pairs = [(place_of(2 * core + (z ^ n) % 2, chip, 1 - z // 2, chips),
              place_of(z, chip, core, chips))
             for z in range(seqs) for chip in range(chips) for core in range(2)]
    return lax.ppermute(x, ("fsdp", "ctx"), pairs)


def body(query_vectors, key_vectors, value_vectors, output_gate, log_decay, write_rate,
         out_weight, cotangent, lengths, pairing, log_ratio):
    q, k, v, gate = query_vectors[0], key_vectors[0], value_vectors[0], output_gate[0]
    spot = lax.axis_index("ctx")
    core, chips = spot % 2, lax.axis_size("ctx") // 2
    me = lax.axis_index("fsdp")
    seqs = lax.axis_size("fsdp")
    sc = jnp.stack([core, me, spot])

    with jax.named_scope("swap_heads"):
        ld, be = log_decay[0].T, write_rate[0].T
        k_x, v_x, ld_x, be_x = (sibling(part) for part in (k, v, ld, be))
    with jax.named_scope("out_weight"):
        heads_weight = [weight_round(out_weight, n, seqs) for n in range(2)]
    ab, t, u0, kg, a, b = write_local(sc, k, v, ld, be, k_x, v_x, ld_x, be_x)
    with jax.named_scope("every_scaled"):
        cotangent = tie(ab, cotangent)[1]
        scaled = scale_local(sc, lengths, pairing, log_ratio, cotangent[0])
    with jax.named_scope("swap_heads"):
        q_x, gate_x, scaled_x = sibling(q), sibling(gate), sibling(scaled)
    ab = exchange(ab)
    p, r, io = read_local(sc, q, k, ld, be, q_x, k_x, ld_x, be_x, u0, kg)
    ab, p, r, io, scaled = tie(ab, p, r, io, scaled)
    states = chain(chain_up_kernel, ab)
    entering = exchange(states).reshape(PAIR_SHAPE)
    with jax.named_scope("back_grad"):
        bg = back_local(sc, scaled, scaled_x, heads_weight)
    with jax.named_scope("every_scaled"):
        own_scaled = tie(heads_weight[0], heads_weight[1], scaled)[2]
        every_scaled = [scaled] + [cross(own_scaled, "fsdp", s) for s in range(1, seqs)]
    *rows, normed, normed_x, gate_grad, gate_grad_x, u, second, g, gs, dq, dq_x, dkn, du = gate_local(
        sc, entering, gate, ld, be, gate_x, ld_x, be_x, *bg, a, b, io, u0, kg, r, p, q, k, q_x, k_x)
    g = exchange(g.reshape(2 * HEADS, HALF, DK))
    with jax.named_scope("every_normed"):
        rows = [feature_round(rows[n], n, seqs) for n in range(seqs)]
    g, *every_scaled = tie(g, *every_scaled)
    states = chain(chain_down_kernel, ab, g)
    leaving = exchange(states).reshape(PAIR_SHAPE)
    with jax.named_scope("weight_grad"):
        rows = list(tie(states, *rows)[1:])
        keep, send = weight_local(sc, rows, every_scaled)
        send = sibling(send)
        gate_grad, dq = fill(sc, [gate_grad, dq], [sibling(gate_grad_x), sibling(dq_x)], 25)
        keep, gate_grad = tie(keep, gate_grad)
        terms = join(keep, send)
        weight_grad = total(exchange(terms))
        leaving, terms = tie(leaving, terms)
    dk, dv, dk_x, dv_x = late_local(sc, k, ld, be, k_x, ld_x, be_x, t, u, a, entering, second,
                                    leaving, gs, dkn, du)
    with jax.named_scope("mixed_out"):
        dk, normed, normed_x = tie(dk, normed, normed_x)
        mixed, mixed_x = mixed_local(sc, normed, normed_x, heads_weight)
    with jax.named_scope("swap_back"):
        mixed, dk, dv = finish(
            sc, [mixed, sibling(mixed_x)], [dk, dv], [sibling(dk_x), sibling(dv_x)])
    return mixed[None], dq[None], dk[None], dv[None], gate_grad[None], weight_grad


def solution(mesh):
    tokens = P("fsdp", "ctx", None)
    return jax.shard_map(
        body,
        mesh=mesh,
        in_specs=(tokens,) * 6 + (P("fsdp", None), tokens, P(), P(), P()),
        out_specs=(tokens,) * 5 + (P(("fsdp", "ctx"), None),),
        check_vma=False,
    )
```
